32 devices in a mesh: dp: 2 (over x), ctx: 4 (over z), tp: 4 (over y, core).
Axes of the slice: x: 2, y: 2, z: 4, core: 2. Of those that a mesh axis runs over, the one named last changes fastest.
Arguments:
- tokens: bfloat16 [4096, 2048], P(('dp', 'ctx')), may hold values from -6 to 6
- cotangent: bfloat16 [4096, 2048], P(('dp', 'ctx')), may hold values from -6 to 6
- lengths: int32 [2, 3], P('dp'), may hold values from 1 to 2046, as said below
- routes: int32 [4096, 8], P(('dp', 'ctx')), may hold values from 0 to 15, all different within a row; in each aligned block of 512 rows (0 to 511, 512 to 1023, ...) at most 320 rows name the same one
- attn_gain: bfloat16 [2048], P('dp'), may hold values from 0.099609375 to 1.8984375
- w_query: bfloat16 [2048, 2048], P('dp', 'tp'), may hold values from -0.125 to 0.125
- w_key: bfloat16 [2048, 2048], P('dp', 'tp'), may hold values from -0.125 to 0.125
- w_value: bfloat16 [2048, 2048], P('dp', 'tp'), may hold values from -0.125 to 0.125
- q_gain: bfloat16 [2048], P('dp'), may hold values from 1 to 1.59375
- k_gain: bfloat16 [2048], P('dp'), may hold values from 1 to 1.59375
- w_out: bfloat16 [2048, 2048], P('tp', 'dp'), may hold values from -2 to 2
- mlp_gain: bfloat16 [2048], P('dp'), may hold values from 0.099609375 to 1.8984375
- w_router: bfloat16 [2048, 16], P('dp'), may hold values from -0.06591797 to 0.06591797
- w_gate: bfloat16 [16, 2048, 1024], P(None, 'dp', 'tp'), may hold values from -0.125 to 0.125
- w_up: bfloat16 [16, 2048, 1024], P(None, 'dp', 'tp'), may hold values from -0.125 to 0.125
- w_down: bfloat16 [16, 1024, 2048], P(None, 'tp', 'dp'), may hold values from -1.5 to 1.5
Outputs:
- output: float32 [4096, 2048], P(('dp', 'ctx'))
- d_tokens: float32 [4096, 2048], P(('dp', 'ctx'))
- d_attn_gain: float32 [2048], P('dp')
- d_w_query: float32 [2048, 2048], P('dp', 'tp')
- d_w_key: float32 [2048, 2048], P('dp', 'tp')
- d_w_value: float32 [2048, 2048], P('dp', 'tp')
- d_q_gain: float32 [2048], P('dp')
- d_k_gain: float32 [2048], P('dp')
- d_w_out: float32 [2048, 2048], P('tp', 'dp')
- d_mlp_gain: float32 [2048], P('dp')
- d_w_router: float32 [2048, 16], P('dp')
- d_w_gate: float32 [16, 2048, 1024], P(None, 'dp', 'tp')
- d_w_up: float32 [16, 2048, 1024], P(None, 'dp', 'tp')
- d_w_down: float32 [16, 1024, 2048], P(None, 'tp', 'dp')
The draws below stay inside these ranges and needn't reach their ends.
Inputs may be any that keep to these rules, and one draw needn't show every extreme that they name: Each row's lengths sum to 2048; the first and the last are between 1 and 256, so the middle sequence covers positions of every index of ctx. In one pack the first and last are both 1. `routes`: in the 512 rows of one device no expert is named by more than 320 rows.
All inputs are finite; a program needn't handle non-finite values.
Results may differ from the reference program's by a relative error of at most 0.017.
The reference program's roundings to bfloat16 on the way count: a program that leaves them out, or rounds other values in their place, can miss the bound.
Values may be sent and summed in bfloat16 or wider, within the bound.
A program may use at most 320 MiB of HBM per device.

```python
import math
import jax
import jax.numpy as jnp
import numpy as np
from jax import lax

D = 2048
HEADS = 16
HEAD = 128
FF = 1024
TOP = 8
EXPERTS = 16
T_DEV = 512
CAP = 320
CTX_LEN = 2048
GROUPS = 2
TOKENS = 4096


def draw_lengths(key, part):
    key = jax.random.fold_in(key, 11)
    first_key, last_key, pick_key = jax.random.split(key, 3)
    first = jax.random.randint(first_key, (GROUPS,), 1, T_DEV // 2 + 1)
    last = jax.random.randint(last_key, (GROUPS,), 1, T_DEV // 2 + 1)
    chosen = jax.random.randint(pick_key, (), 0, GROUPS)
    hit = jnp.arange(GROUPS, dtype=jnp.int32) == chosen
    first = jnp.where(hit, 1, first)
    last = jnp.where(hit, 1, last)
    middle = CTX_LEN - first - last
    return jnp.stack([first, middle, last], axis=1).astype(jnp.int32)


def levels(key, extent, pieces, smallest, high):
    level, own = 1.0, jax.random.fold_in(key, 6)
    for axis_at, shards_of in pieces:
        heights = jnp.exp(jax.random.uniform(jax.random.fold_in(own, axis_at), (shards_of,), jnp.float32, smallest / len(pieces), high / len(pieces)))
        level = level * jnp.repeat(heights, extent[axis_at] // shards_of).reshape([-1 if axis == axis_at else 1 for axis in range(len(extent))])
    return level


def deal_out(key, own, number, rows, count, top, reach, slope):
    order = jax.random.permutation(key, count)
    packed, usual = load_shares(count, rows * top, reach, slope, True), load_shares(count, rows * top, reach, slope, False)
    places = jnp.arange(count)

    def named(sizes, turn):
        used = int((sizes > 0).sum())
        fixed = max(1, used // 4)
        moved = fixed + (places - fixed + turn * (used - fixed)) % max(1, count - fixed)
        return jnp.zeros((count,), jnp.int32).at[order[jnp.where(places < fixed, places, moved)]].set(jnp.asarray(sizes, jnp.int32))

    sizes = jnp.where(number % 4 == 0, named(packed, number // 4), named(usual, number - number // 4 - 1))
    mixed = jax.random.permutation(jax.random.fold_in(own, 3), count)
    donor, taker = mixed[0:count // 2 * 2:2], mixed[1:count // 2 * 2:2]
    room = jnp.minimum(sizes[donor] - 1, reach - sizes[taker]) // 2
    room = jnp.where((donor == order[0]) | (taker == order[0]) | (sizes[taker] == 0), 0, jnp.maximum(room, 0))
    moved = jax.random.randint(jax.random.fold_in(own, 4), (count // 2,), 0, 1 << 20) % (room + 1)
    sizes = sizes.at[donor].add(-moved).at[taker].add(moved)
    members = jnp.searchsorted(jnp.cumsum(sizes), jnp.arange(rows * top), side="right").astype(jnp.int32)
    table = members.reshape(top, rows).T
    table = table[jax.random.permutation(jax.random.fold_in(own, 1), rows)]
    turn = jax.random.randint(jax.random.fold_in(own, 2), (rows, 1), 0, top)
    return jnp.take_along_axis(table, (jnp.arange(top)[None, :] + turn) % top, axis=1)


def load_shares(number_of, total, limit, slope, full):
    loads = [(1 << 20) // math.isqrt(rank ** slope) + 1 for rank in range(1, number_of + 1)]
    largest = limit if full else min(limit, max(-(-total // number_of), total * loads[0] // sum(loads)))
    least = 1 if total - largest >= number_of - 1 else 0
    holding, rest = [largest] + [least] * (number_of - 1), total - largest - least * (number_of - 1)
    while rest > 0:
        candidates = [i for i in range(1, number_of) if holding[i] < largest] or [i for i in range(1, number_of) if holding[i] < limit]
        pool, budget = sum([loads[i] for i in candidates]), rest
        for i in candidates:
            addition = min(limit - holding[i], max(1, budget * loads[i] // pool), rest)
            holding[i] = holding[i] + addition
            rest = rest - addition
    return np.array(holding)


def centred(rng, extent, deviation, limit, shards=(), kind=jnp.bfloat16):
    level = levels(rng, extent, shards, -0.22, 0.18) if shards else 1.0
    values = jax.random.normal(rng, extent, jnp.float32) * deviation * level
    return jnp.minimum(jnp.maximum(values, -limit), limit).astype(kind)


def setup_inputs(seed: int = 0) -> dict:
    splits = jax.random.split(jax.random.key(seed), 17)
    tokens = centred(splits[0], (TOKENS, D), 1.0, 6.0, ((0, 8),))
    cotangent = centred(splits[1], (TOKENS, D), 1.0, 6.0, ((0, 8),))
    lengths = draw_lengths(jax.random.fold_in(splits[16], 71), 0)
    routes_keys = jax.random.split(jax.random.fold_in(splits[3], 1), TOKENS // T_DEV)
    routes_turns = jax.random.permutation(jax.random.fold_in(splits[3], 3), TOKENS // T_DEV)
    routes = jax.vmap(lambda own, number: deal_out(jax.random.fold_in(splits[3], 2), own, number, T_DEV, EXPERTS, TOP, CAP, 1))(routes_keys, routes_turns).reshape((TOKENS, TOP))
    attn_gain = jnp.clip(1.0 + 0.18 * jax.random.normal(splits[4], (D,), jnp.float32), 0.099609375, 1.8984375).astype(jnp.bfloat16)
    w_query = centred(splits[5], (D, D), D ** -0.5, 0.125, ((0, 2), (1, 4)))
    w_key = centred(splits[6], (D, D), D ** -0.5, 0.125, ((0, 2), (1, 4)))
    w_value = centred(splits[7], (D, D), D ** -0.5, 0.125, ((0, 2), (1, 4)))
    q_gain = jnp.clip(1.0 + 0.59375 * jax.random.uniform(splits[8], (D,), jnp.float32) ** levels(splits[8], (D,), ((0, 2),), -0.2, 0.2), 1.0, 1.59375).astype(jnp.bfloat16)
    k_gain = jnp.clip(1.0 + 0.59375 * jax.random.uniform(splits[9], (D,), jnp.float32) ** levels(splits[9], (D,), ((0, 2),), -0.2, 0.2), 1.0, 1.59375).astype(jnp.bfloat16)
    w_out = centred(splits[10], (D, D), (max(D // 256, 1)) ** -0.5, 2.0, ((0, 4), (1, 2)))
    mlp_gain = jnp.clip(1.0 + 0.18 * jax.random.normal(splits[11], (D,), jnp.float32), 0.099609375, 1.8984375).astype(jnp.bfloat16)
    w_router = centred(splits[12], (D, EXPERTS), (0.5 * D ** -0.5), 0.06591797, ((0, 2),))
    w_gate = centred(splits[13], (EXPERTS, D, FF), D ** -0.5, 0.125, ((1, 2), (2, 4)))
    w_up = centred(splits[14], (EXPERTS, D, FF), D ** -0.5, 0.125, ((1, 2), (2, 4)))
    w_down = centred(splits[15], (EXPERTS, FF, D), (max(FF // 64, 1)) ** -0.5, 1.5, ((1, 4), (2, 2)))
    return {"tokens": tokens, "cotangent": cotangent, "lengths": lengths, "routes": routes, "attn_gain": attn_gain, "w_query": w_query, "w_key": w_key, "w_value": w_value, "q_gain": q_gain, "k_gain": k_gain, "w_out": w_out, "mlp_gain": mlp_gain, "w_router": w_router, "w_gate": w_gate, "w_up": w_up, "w_down": w_down}


EPS = 1e-05
THETA = 10000.0

@jax.custom_vjp
def low(v):
    return lax.optimization_barrier(v.astype(jnp.bfloat16)).astype(jnp.float32)

@jax.custom_vjp
def low_back(v):
    return v

def low_keep(v):
    return (low(v), None)

def low_pass(kept, grad):
    return (grad,)

def back_keep(v):
    return (v, None)

def back_low(kept, grad):
    return (low(grad),)
low.defvjp(low_keep, low_pass)
low_back.defvjp(back_keep, back_low)

def matmul(left, right):
    return jnp.dot(left, right, precision=lax.Precision.HIGHEST)

def norm_rows(v, gain):
    return v * lax.rsqrt(lax.optimization_barrier(jnp.mean(v * v, axis=-1, keepdims=True)) + EPS) * gain

def layout(row, total):
    ends = jnp.cumsum(row).astype(jnp.int32)
    starts = (ends - row).astype(jnp.int32)
    index = jnp.arange(total, dtype=jnp.int32)
    segment = lax.optimization_barrier(jnp.sum((index[:, None] >= ends[None, :]).astype(jnp.int32), axis=1)).astype(jnp.int32)
    picked = segment[:, None] == jnp.arange(row.shape[0], dtype=jnp.int32)[None, :]
    first = lax.optimization_barrier(jnp.sum(jnp.where(picked, starts[None, :], 0), axis=1)).astype(jnp.int32)
    return (segment, (index - first).astype(jnp.int32))

def rotation(position):
    inverse = THETA ** (-jnp.arange(0, HEAD, 2).astype(jnp.float32) / HEAD)
    angle = position.astype(jnp.float32)[:, None] * inverse[None, :]
    return (jnp.cos(angle), jnp.sin(angle))

def rotate(v, cosine, sine):
    count = v.shape[0]
    parts = v.reshape(count, -1, 2, HEAD // 2)
    first = parts[:, :, 0]
    second = parts[:, :, 1]
    cos_b = cosine[:, None, :]
    sin_b = sine[:, None, :]
    turned = jnp.stack([first * cos_b - second * sin_b, second * cos_b + first * sin_b], axis=2)
    return turned.reshape(count, -1)

def pack_forward(x, weights, segment, position, chosen):
    attn_gain, w_query, w_key, w_value, q_gain, k_gain, w_out, mlp_gain, w_router, w_gate, w_up, w_down = weights
    length = x.shape[0]
    hidden_one = low(norm_rows(x, attn_gain))
    q_raw = low_back(matmul(hidden_one, w_query))
    k_raw = low_back(matmul(hidden_one, w_key))
    values = low_back(low(matmul(hidden_one, w_value)))
    cosine, sine = rotation(position)
    queries = low(rotate(norm_rows(q_raw, q_gain), cosine, sine))
    keys = low(rotate(norm_rows(k_raw, k_gain), cosine, sine))
    index = jnp.arange(length, dtype=jnp.int32)
    allowed = (segment[:, None] == segment[None, :]) & (index[None, :] <= index[:, None])

    def one_head(parts):
        query_h, key_h, value_h = parts
        scores = low_back(matmul(query_h, key_h.T)) * HEAD ** (-0.5)
        probs = jax.nn.softmax(jnp.where(allowed, scores, -1e+30), axis=-1)
        return matmul(low(probs), value_h)

    def split(v):
        return v.reshape(length, HEADS, HEAD).transpose(1, 0, 2)
    heads = lax.map(jax.checkpoint(one_head), (split(queries), split(keys), split(values)))
    attended = low_back(low(heads.transpose(1, 0, 2).reshape(length, D)))
    mixed = x + low_back(matmul(attended, w_out))
    hidden_two = low(norm_rows(mixed, mlp_gain))
    route_probs = jax.nn.softmax(low_back(matmul(hidden_two, w_router)), axis=-1)
    gates = route_probs * chosen

    def one_expert(total, parts):
        gate_w, up_w, down_w, column = parts
        gate = low_back(matmul(hidden_two, gate_w))
        up = low_back(matmul(hidden_two, up_w))
        inner = low(jax.nn.silu(gate) * up)
        return (total + column[:, None] * low_back(matmul(inner, down_w)), None)
    mixture, _ = lax.scan(jax.checkpoint(one_expert), jnp.zeros_like(x), (w_gate, w_up, w_down, gates.T))
    return mixed + low_back(mixture)

def reference(tokens, cotangent, lengths, routes, attn_gain, w_query, w_key, w_value, q_gain, k_gain, w_out, mlp_gain, w_router, w_gate, w_up, w_down):
    weights = (attn_gain.astype(jnp.float32), w_query.astype(jnp.float32), w_key.astype(jnp.float32), w_value.astype(jnp.float32), q_gain.astype(jnp.float32), k_gain.astype(jnp.float32), w_out.astype(jnp.float32), mlp_gain.astype(jnp.float32), w_router.astype(jnp.float32), w_gate.astype(jnp.float32), w_up.astype(jnp.float32), w_down.astype(jnp.float32))
    inputs = tokens.astype(jnp.float32).reshape(GROUPS, CTX_LEN, D)
    upstream = cotangent.astype(jnp.float32).reshape(GROUPS, CTX_LEN, D)
    picks = routes.reshape(GROUPS, CTX_LEN, TOP)

    def one_pack(totals, parts):
        x, grad_out, row, chosen_ids = parts
        segment, position = layout(row, CTX_LEN)
        chosen = lax.optimization_barrier(jnp.sum((chosen_ids[:, :, None] == jnp.arange(EXPERTS, dtype=jnp.int32)[None, None, :]).astype(jnp.float32), axis=1))
        result, pull = jax.vjp(lambda xv, wv: pack_forward(xv, wv, segment, position, chosen), x, weights)
        grad_x, grad_w = pull(grad_out)
        return (jax.tree.map(jnp.add, totals, grad_w), (result, grad_x))
    zeros = jax.tree.map(jnp.zeros_like, weights)
    grads, (results, grad_inputs) = lax.scan(one_pack, zeros, (inputs, upstream, lengths, picks))
    return (results.reshape(TOKENS, D), grad_inputs.reshape(TOKENS, D), grads[0], grads[1], grads[2], grads[3], grads[4], grads[5], grads[6], grads[7], grads[8], grads[9], grads[10], grads[11])
```

```python
import functools

import jax
import jax.numpy as jnp
from jax import lax
from jax.experimental import pallas as pl
from jax.experimental.pallas import tpu as pltpu
from jax.sharding import PartitionSpec as P

HEAD = 128
EPS = 1e-05
THETA = 10000.0
BLOCK = 256
BF16 = jnp.bfloat16
F32 = jnp.float32
MESH = pl.DeviceIdType.MESH
MICRO = 1 << 30


def dot(a, b):
    return jnp.dot(a, b, preferred_element_type=F32)


def dot_t(a, b):
    return lax.dot_general(a, b, (((1,), (1,)), ((), ())), preferred_element_type=F32)


def t_dot(a, b):
    return lax.dot_general(a, b, (((0,), (0,)), ((), ())), preferred_element_type=F32)


def rotation(row, first, rows):
    ends = jnp.cumsum(row)
    index = first + jnp.arange(rows, dtype=jnp.int32)
    before = jnp.where(index[:, None] >= ends[None, :], ends[None, :], 0)
    position = index - jnp.max(before, axis=1)
    inverse = THETA ** (-jnp.arange(0, HEAD, 2).astype(F32) / HEAD)
    angle = position.astype(F32)[:, None] * inverse[None, :]
    cosine, sine = jnp.cos(angle), jnp.sin(angle)
    return (
        jnp.concatenate([cosine, cosine], axis=1)[:, None, :],
        jnp.concatenate([-sine, sine], axis=1)[:, None, :],
    )


def rotate(v, cosine, sine):
    return v * cosine + jnp.roll(v, HEAD // 2, axis=2) * sine


def allowed_block(lengths_ref, base, rows, columns):
    index = base + lax.broadcasted_iota(jnp.int32, (rows, 1), 0)
    start = jnp.zeros((rows, 1), jnp.int32)
    end = 0
    for at in range(lengths_ref.shape[1]):
        end = end + lengths_ref[0, at]
        start = jnp.where(index >= end, end, start)
    key = lax.broadcasted_iota(jnp.int32, (rows, columns), 1)
    return (key >= start) & (key <= index)


def attend_kernel(lengths_ref, q_ref, k_ref, v_ref, out_ref, log_ref):
    scale = HEAD ** (-0.5)
    rows = q_ref.shape[0]
    for base in range(0, rows, BLOCK):
        upto = base + BLOCK
        own = pl.ds(base, BLOCK)
        keys, values = k_ref[pl.ds(0, upto), :], v_ref[pl.ds(0, upto), :]
        scores = dot_t(q_ref[own, :], keys) * scale
        scores = jnp.where(allowed_block(lengths_ref, base, BLOCK, upto), scores, -1e30)
        top = jnp.max(scores, axis=1, keepdims=True)
        weights = jnp.exp(scores - top)
        total = jnp.sum(weights, axis=1, keepdims=True)
        probs = (weights * (1.0 / total)).astype(BF16)
        out_ref[own, :] = dot(probs, values).astype(BF16)
        log_ref[own, :] = top + jnp.log(total)


def attend(lengths, q, k, v):
    heads, rows, _ = q.shape
    spec = pl.BlockSpec((None, rows, HEAD), lambda h: (h, 0, 0))
    column = pl.BlockSpec((None, rows, 1), lambda h: (h, 0, 0))
    return pl.pallas_call(
        attend_kernel,
        cost_estimate=pl.CostEstimate(flops=7 * MICRO, bytes_accessed=0, transcendentals=0),
        grid=(heads,),
        out_shape=(
            jax.ShapeDtypeStruct((heads, rows, HEAD), BF16),
            jax.ShapeDtypeStruct((heads, rows, 1), F32),
        ),
        in_specs=[pl.BlockSpec(memory_space=pltpu.SMEM), spec, spec, spec],
        out_specs=(spec, column),
        compiler_params=pltpu.CompilerParams(vmem_limit_bytes=48 << 20),
    )(lengths, q, k, v)


def attend_back_kernel(
    lengths_ref, q_ref, k_ref, v_ref, d_ref, log_ref, dq_ref, dk_ref, dv_ref, dk_sum, dv_sum
):
    scale = HEAD ** (-0.5)
    rows = q_ref.shape[0]
    dk_sum[...] = jnp.zeros_like(dk_sum)
    dv_sum[...] = jnp.zeros_like(dv_sum)
    for base in range(0, rows, BLOCK):
        upto = base + BLOCK
        own, seen = pl.ds(base, BLOCK), pl.ds(0, upto)
        q, d = q_ref[own, :], d_ref[own, :]
        keys, values = k_ref[seen, :], v_ref[seen, :]
        scores = dot_t(q, keys) * scale - log_ref[own, :]
        probs = jnp.where(
            allowed_block(lengths_ref, base, BLOCK, upto), jnp.exp(scores), 0.0
        )
        d_probs = dot_t(d, values)
        delta = jnp.sum(probs * d_probs, axis=1, keepdims=True)
        d_raw = (probs * (d_probs - delta) * scale).astype(BF16)
        dq_ref[own, :] = dot(d_raw, keys).astype(dq_ref.dtype)
        dk_sum[seen, :] += t_dot(d_raw, q)
        dv_sum[seen, :] += t_dot(probs.astype(BF16), d)
    dk_ref[...] = dk_sum[...].astype(dk_ref.dtype)
    dv_ref[...] = dv_sum[...].astype(dv_ref.dtype)


def attend_back(lengths, q, k, v, d, log):
    heads, rows, _ = q.shape
    spec = pl.BlockSpec((None, rows, HEAD), lambda h: (h, 0, 0))
    column = pl.BlockSpec((None, rows, 1), lambda h: (h, 0, 0))
    return pl.pallas_call(
        attend_back_kernel,
        cost_estimate=pl.CostEstimate(flops=10 * MICRO, bytes_accessed=0, transcendentals=0),
        grid=(heads,),
        out_shape=(jax.ShapeDtypeStruct((heads, rows, HEAD), BF16),) * 3,
        in_specs=[pl.BlockSpec(memory_space=pltpu.SMEM), spec, spec, spec, spec, column],
        out_specs=(spec,) * 3,
        scratch_shapes=[pltpu.VMEM((rows, HEAD), F32)] * 2,
        compiler_params=pltpu.CompilerParams(vmem_limit_bytes=48 << 20),
    )(lengths, q, k, v, d, log)


def to_heads(parts, heads):
    count = lax.axis_size("ctx")
    rows = parts[0].shape[0]
    stacked = jnp.stack([p.reshape(rows, count, heads // count, HEAD) for p in parts])
    sent = stacked.transpose(2, 0, 3, 1, 4)
    got = lax.all_to_all(sent, "ctx", 0, 0, tiled=True)
    return got.transpose(1, 2, 0, 3, 4).reshape(len(parts), heads // count, count * rows, HEAD)


def to_rows(parts):
    count = lax.axis_size("ctx")
    mine, pack, _ = parts[0].shape
    stacked = jnp.stack([p.reshape(mine, count, pack // count, HEAD) for p in parts])
    sent = stacked.transpose(2, 0, 1, 3, 4)
    got = lax.all_to_all(sent, "ctx", 0, 0, tiled=True)
    turned = got.transpose(1, 3, 0, 2, 4)
    return turned.reshape(len(parts), pack // count, count * mine, HEAD)


def expert_kernel(blocks, at_ref, hidden_ref, up_ref, chosen_ref, router_ref, *refs):
    gate_w, up_w, down_w = (refs[i * blocks : (i + 1) * blocks] for i in range(3))
    inner_ref, dgate_ref, dup_ref, dots_ref, grads_ref = refs[3 * blocks : 3 * blocks + 5]
    gate_sum, up_sum, down_sum = refs[3 * blocks + 5 :]
    turn, last = pl.program_id(0), pl.num_programs(0) - 1
    wide = gate_w[0].shape[0]
    hidden, upstream = hidden_ref[...], up_ref[...]

    def over(v, ws, f):
        return sum(f(v[:, s * wide : (s + 1) * wide], w[...]) for s, w in enumerate(ws))

    gate, up = over(hidden, gate_w, dot), over(hidden, up_w, dot)
    pulled = over(upstream, down_w, dot_t)
    logits = dot_t(hidden, router_ref[...])
    odds = jnp.exp(logits - jnp.max(logits, axis=1, keepdims=True))
    probs = odds / jnp.sum(odds, axis=1, keepdims=True) * chosen_ref[...]
    named = lax.broadcasted_iota(jnp.int32, probs.shape, 1) == at_ref[0]
    weight = jnp.sum(jnp.where(named, probs, 0.0), axis=1, keepdims=True)
    sigma = jax.nn.sigmoid(gate)
    active = gate * sigma
    inner = (active * up).astype(BF16).astype(F32)
    dots = jnp.sum(inner * pulled, axis=1, keepdims=True)
    dots_ref[...] = jnp.where(weight > 0.0, dots, 0.0)
    inner = (weight * inner).astype(BF16)
    pulled = weight * pulled
    d_gate = (pulled * up * sigma * (1.0 + gate * (1.0 - sigma))).astype(BF16)
    d_up = (pulled * active).astype(BF16)
    inner_ref[...], dgate_ref[...], dup_ref[...] = inner, d_gate, d_up

    @pl.when(turn == 0)
    def _():
        for total in (gate_sum, up_sum, down_sum):
            total[...] = jnp.zeros_like(total)

    gate_sum[...] += t_dot(d_gate, hidden)
    up_sum[...] += t_dot(d_up, hidden)
    down_sum[...] += t_dot(inner, upstream)

    @pl.when(turn == last)
    def _():
        fine = down_sum.shape[0]
        for s in range(blocks):
            own = pl.ds(s * wide, wide)
            grads_ref[s, 0] = gate_sum[:, own].T.astype(BF16)
            grads_ref[s, 1] = up_sum[:, own].T.astype(BF16)
            for j in range(wide // fine):
                grads_ref[s, 2, pl.ds(j * fine, fine), :] = down_sum[
                    :, pl.ds(s * wide + j * fine, fine)
                ].astype(BF16)


def expert(at, hidden, upstream, chosen, router, gate_w, up_w, down_w, tile=512):
    blocks = len(gate_w)
    pack, width = hidden.shape
    _, wide, fine = gate_w[0].shape

    def weight_spec(which, shape):
        return pl.BlockSpec((None,) + shape, lambda i, at_ref: (at_ref[which], 0, 0))

    ups = [weight_spec(0 if s == 0 else 1, (wide, fine)) for s in range(blocks)]
    downs = [weight_spec(0 if s == 0 else 1, (fine, wide)) for s in range(blocks)]
    def token(n):
        return pl.BlockSpec((tile, n), lambda i, at_ref: (i, 0))

    whole = pl.BlockSpec((blocks, 3, wide, fine), lambda i, at_ref: (0, 0, 0, 0))
    return pl.pallas_call(
        functools.partial(expert_kernel, blocks),
        cost_estimate=pl.CostEstimate(flops=27 * MICRO, bytes_accessed=0, transcendentals=0),
        grid_spec=pltpu.PrefetchScalarGridSpec(
            num_scalar_prefetch=1,
            grid=(pack // tile,),
            in_specs=[token(width), token(width), token(chosen.shape[1])]
            + [pl.BlockSpec(router.shape, lambda i, at_ref: (0, 0))]
            + ups
            + ups
            + downs,
            out_specs=[token(fine)] * 3 + [token(1), whole],
            scratch_shapes=[pltpu.VMEM((fine, width), F32)] * 3,
        ),
        out_shape=[jax.ShapeDtypeStruct((pack, fine), BF16)] * 3
        + [
            jax.ShapeDtypeStruct((pack, 1), F32),
            jax.ShapeDtypeStruct((blocks, 3, wide, fine), BF16),
        ],
        compiler_params=pltpu.CompilerParams(vmem_limit_bytes=56 << 20),
    )(at, hidden, upstream, chosen, router, *gate_w, *up_w, *down_w)

def signal_all(partners):
    barrier = pltpu.get_barrier_semaphore()
    count = 0
    for device, there in partners:

        @pl.when(there)
        def _():
            pl.semaphore_signal(barrier, inc=1, device_id=device, device_id_type=MESH)

        count = count + jnp.where(there, 1, 0)
    pl.semaphore_wait(barrier, count)


def place():
    c, t = lax.axis_index("ctx"), lax.axis_index("tp")
    core, side = lax.rem(t, 2), t // 2
    over_core = {"tp": t + 1 - 2 * core}
    over_side = {"tp": t + 2 - 4 * side}
    return c, lax.axis_size("ctx"), core, side, over_core, over_side


def remote(source, target, sems, at, device):
    send, recv = sems
    return pltpu.make_async_remote_copy(
        src_ref=source,
        dst_ref=target,
        send_sem=send.at[at],
        recv_sem=recv.at[at],
        device_id=device,
        device_id_type=MESH,
    )


def spread_kernel(x_ref, out_ref, local, zs, zr, ys, yr, cs, cr):
    c, n, core, side, over_core, over_side = place()
    rows, part = x_ref.shape
    left, right = {"ctx": c - 1}, {"ctx": c + 1}
    signal_all([(left, c > 0), (right, c < n - 1), (over_core, c >= 0), (over_side, c >= 0)])
    mine = core * 2 + side
    other = core * 2 + 1 - side

    def tile(owner, column):
        return out_ref.at[
            pl.ds(pl.multiple_of(owner * rows, rows), rows),
            pl.ds(pl.multiple_of(column * part, part), part),
        ]

    def along(owner, source, target, at):
        return remote(source, tile(owner, mine), (zs, zr), at, target)

    keep = pltpu.make_async_copy(x_ref, tile(c, mine), local)
    keep.start()

    @pl.when(c > 0)
    def _():
        along(c, x_ref, left, n + c).start()

    @pl.when(c < n - 1)
    def _():
        along(c, x_ref, right, c).start()

    def to_side(owner, source):
        return remote(source, tile(owner, mine), (ys, yr), owner, over_side)

    def to_core(owner, column, source, which):
        return remote(source, tile(owner, column), (cs, cr), which * n + owner, over_core)

    to_side(c, x_ref).start()
    to_core(c, mine, x_ref, 0).start()

    def from_side(owner):
        here = tile(owner, other)
        remote(here, here, (ys, yr), owner, over_side).wait_recv()
        to_core(owner, other, here, 1).start()

    from_side(c)
    for far in range(1, n):
        for sign, there, onward, more in (
            (-1, c - far >= 0, right, c < n - 1),
            (1, c + far < n, left, c > 0),
        ):
            owner = c + sign * far
            slot = owner if sign < 0 else n + owner

            @pl.when(there)
            def _():
                here = tile(owner, mine)
                along(owner, here, onward, slot).wait_recv()

                @pl.when(more)
                def _():
                    along(owner, here, onward, slot).start()

                to_side(owner, here).start()
                to_core(owner, mine, here, 0).start()

        for sign, there in ((-1, c - far >= 0), (1, c + far < n)):

            @pl.when(there)
            def _():
                from_side(c + sign * far)

    keep.wait()

    @pl.when(c > 0)
    def _():
        along(c, x_ref, left, n + c).wait_send()

    @pl.when(c < n - 1)
    def _():
        along(c, x_ref, right, c).wait_send()

    for far in range(1, n):
        for sign, there, onward, more in (
            (-1, c - far >= 0, right, c < n - 1),
            (1, c + far < n, left, c > 0),
        ):
            owner = c + sign * far

            @pl.when(there & more)
            def _():
                here = tile(owner, mine)
                along(owner, here, onward, owner if sign < 0 else n + owner).wait_send()

    for owner in range(n):
        to_side(owner, tile(owner, mine)).wait_send()
        to_core(owner, mine, tile(owner, mine), 0).wait_send()
        to_core(owner, other, tile(owner, other), 1).wait_send()
        for which, column in ((0, (1 - core) * 2 + side), (1, (1 - core) * 2 + 1 - side)):
            here = tile(owner, column)
            remote(here, here, (cs, cr), which * n + owner, over_core).wait_recv()


def spread(v, ident):
    n, tp = lax.axis_size("ctx"), lax.axis_size("tp")
    rows, part = v.shape
    dma = pltpu.SemaphoreType.DMA
    return pl.pallas_call(
        spread_kernel,
        cost_estimate=pl.CostEstimate(flops=60 * MICRO, bytes_accessed=0, transcendentals=0),
        out_shape=jax.ShapeDtypeStruct((n * rows, tp * part), v.dtype),
        in_specs=[pl.BlockSpec(memory_space=pl.ANY)],
        out_specs=pl.BlockSpec(memory_space=pl.ANY),
        scratch_shapes=[dma] + [dma((2 * n,))] * 2 + [dma((n,))] * 2 + [dma((2 * n,))] * 2,
        compiler_params=pltpu.CompilerParams(collective_id=ident, has_side_effects=True),
    )(v)


def join_kernel(x_ref, out_ref, local, ss, sr):
    c, n, core, side, over_core, over_side = place()
    rows, part = x_ref.shape
    signal_all([(over_core, c >= 0), (over_side, c >= 0)])
    mine, other = core * 2 + side, core * 2 + 1 - side

    def tile(column):
        return out_ref.at[:, pl.ds(pl.multiple_of(column * part, part), part)]

    keep = pltpu.make_async_copy(x_ref, tile(mine), local)
    keep.start()
    first = remote(x_ref, tile(mine), (ss, sr), 0, over_side)
    first.start()
    second = remote(x_ref, tile(mine), (ss, sr), 1, over_core)
    second.start()
    first.wait_recv()
    third = remote(tile(other), tile(other), (ss, sr), 2, over_core)
    third.start()
    keep.wait()
    first.wait_send()
    second.wait()
    third.wait()


def join(v, ident):
    tp = lax.axis_size("tp")
    rows, part = v.shape
    dma = pltpu.SemaphoreType.DMA
    return pl.pallas_call(
        join_kernel,
        cost_estimate=pl.CostEstimate(flops=25 * MICRO, bytes_accessed=0, transcendentals=0),
        out_shape=jax.ShapeDtypeStruct((rows, tp * part), v.dtype),
        in_specs=[pl.BlockSpec(memory_space=pl.ANY)],
        out_specs=pl.BlockSpec(memory_space=pl.ANY),
        scratch_shapes=[dma] + [dma((3,))] * 2,
        compiler_params=pltpu.CompilerParams(collective_id=ident, has_side_effects=True),
    )(v)


def collect_kernel(
    owners, x_ref, out_ref, core_in, side_out, side_in, z_out, z_in, cs, cr, ys, yr, zs, zr
):
    c, n, core, side, over_core, over_side = place()
    rows, part = out_ref.shape
    left, right = {"ctx": c - 1}, {"ctx": c + 1}
    partners = [(over_core, c >= 0), (over_side, c >= 0)]
    if owners > 1:
        partners += [(left, c > 0), (right, c < n - 1)]
    signal_all(partners)

    def owner_of(i):
        if owners == 1:
            return 0
        owner = 0
        for at in range(n):
            for turn, far in enumerate(sorted(range(n), key=lambda o: -abs(o - at))):
                owner = jnp.where((c == at) & (i == turn), far, owner)
        return owner

    def own_rows(owner):
        return pl.ds(pl.multiple_of(owner * rows, rows), rows)

    def half(which):
        return pl.ds(pl.multiple_of(which * 2 * part, 2 * part), 2 * part)

    def quarter(which):
        return pl.ds(pl.multiple_of((core * 2 + which) * part, part), part)

    def to_core(i):
        source = x_ref.at[own_rows(owner_of(i)), half(1 - core)]
        return remote(source, core_in.at[i], (cs, cr), i, over_core)

    def to_side(i):
        return remote(side_out.at[i], side_in.at[i], (ys, yr), i, over_side)

    def to_left(owner):
        return remote(z_out.at[owner], z_in.at[1, owner], (zs, zr), n + owner, left)

    def to_right(owner):
        return remote(z_out.at[owner], z_in.at[0, owner], (zs, zr), owner, right)

    def from_core(i, which):
        local = x_ref[own_rows(owner_of(i)), quarter(which)].astype(F32)
        near = core_in[i, :, pl.ds(pl.multiple_of(which * part, part), part)]
        return local + near.astype(F32)

    for i in range(owners):
        to_core(i).start()

    def finish(i):
        to_side(i).wait_recv()
        owner = owner_of(i)
        total = from_core(i, side) + side_in[i].astype(F32)
        if owners == 1:
            out_ref[...] = total
            return

        @pl.when(owner > c)
        def _():
            @pl.when(c > 0)
            def _():
                to_right(owner).wait_recv()
                z_out[owner] = (total + z_in[0, owner].astype(F32)).astype(z_out.dtype)

            @pl.when(c == 0)
            def _():
                z_out[owner] = total.astype(z_out.dtype)

            to_right(owner).start()

        @pl.when(owner < c)
        def _():
            @pl.when(c < n - 1)
            def _():
                to_left(owner).wait_recv()
                z_out[owner] = (total + z_in[1, owner].astype(F32)).astype(z_out.dtype)

            @pl.when(c == n - 1)
            def _():
                z_out[owner] = total.astype(z_out.dtype)

            to_left(owner).start()

        @pl.when(owner == c)
        def _():
            out_ref[...] = total

    def step(i, carry):
        @pl.when(i < owners)
        def _():
            to_core(i).wait_recv()
            side_out[i] = from_core(i, 1 - side).astype(side_out.dtype)
            to_side(i).start()

        @pl.when(i > 0)
        def _():
            finish(i - 1)

        return carry

    lax.fori_loop(0, owners + 1, step, 0)

    if owners > 1:

        @pl.when(c > 0)
        def _():
            to_right(c).wait_recv()
            out_ref[...] += z_in[0, c].astype(F32)

        @pl.when(c < n - 1)
        def _():
            to_left(c).wait_recv()
            out_ref[...] += z_in[1, c].astype(F32)

    def close(i, carry):
        to_core(i).wait_send()
        to_side(i).wait_send()
        if owners > 1:
            owner = owner_of(i)

            @pl.when(owner > c)
            def _():
                to_right(owner).wait_send()

            @pl.when(owner < c)
            def _():
                to_left(owner).wait_send()

        return carry

    lax.fori_loop(0, owners, close, 0)


def collect(v, owners, ident):
    n, tp = lax.axis_size("ctx"), lax.axis_size("tp")
    rows, part = v.shape[0] // owners, v.shape[1] // tp
    dma = pltpu.SemaphoreType.DMA
    z = n if owners > 1 else 1
    return pl.pallas_call(
        functools.partial(collect_kernel, owners),
        cost_estimate=pl.CostEstimate(flops=17 * MICRO, bytes_accessed=0, transcendentals=0),
        out_shape=jax.ShapeDtypeStruct((rows, part), F32),
        in_specs=[pl.BlockSpec(memory_space=pltpu.VMEM)],
        out_specs=pl.BlockSpec(memory_space=pltpu.VMEM),
        scratch_shapes=[
            pltpu.VMEM((owners, rows, 2 * part), BF16),
            pltpu.VMEM((owners, rows, part), BF16),
            pltpu.VMEM((owners, rows, part), BF16),
            pltpu.VMEM((z, rows, part), BF16),
            pltpu.VMEM((2, z, rows, part), BF16),
        ]
        + [dma((owners,))] * 4
        + [dma((2 * z,))] * 2,
        compiler_params=pltpu.CompilerParams(
            collective_id=ident, has_side_effects=True, vmem_limit_bytes=48 << 20
        ),
    )(v)


def returns_kernel(kinds, mine, blocks, flipped, with_dots, *refs):
    refs = list(refs)
    take = lambda count: [refs.pop(0) for _ in range(count)]
    lhs_refs, own_refs, other_refs = take(kinds * mine), take(kinds), take(kinds * (blocks - 1))
    dots_ref = take(1)[0] if with_dots else None
    out_ref = take(1)[0]
    dots_out = take(1)[0] if with_dots else None
    lhs, weights, core_out, core_in, keep, near, side_out, side_in, z_out, z_in = take(10)
    ls, ws, cs, cr, ys, yr, zs, zr = take(8)
    dots_in, ds, dr = take(3) if with_dots else (None, None, None)
    c, n, core, side, over_core, over_side = place()
    t, tp = lax.axis_index("tp"), lax.axis_size("tp")
    rows, part = out_ref.shape
    fine = lhs_refs[0].shape[1]
    wide = out_ref.shape[1] * tp // blocks
    half_blocks = blocks // 2
    left, right = {"ctx": c - 1}, {"ctx": c + 1}

    loads = []
    for k in range(kinds):
        for e in range(mine):
            at = k * mine + e
            columns = pl.ds(at * fine, fine)
            loads.append(pltpu.make_async_copy(lhs_refs[at], lhs.at[:, columns], ls.at[at]))
            for s in range(blocks):
                source = own_refs[k].at[c * mine + e] if s == 0 else other_refs[k * (blocks - 1) + s - 1].at[e]
                target = weights.at[s, columns, :] if flipped else weights.at[s, :, columns]
                loads.append(pltpu.make_async_copy(source, target, ws.at[at * blocks + s]))
    for load in loads:
        load.start()
    if with_dots:
        others = []
        for far_c in range(n):
            for far_t in range(tp):
                others.append(({"ctx": far_c, "tp": far_t}, (c != far_c) | (t != far_t)))
        signal_all(others)
    else:
        signal_all(
            [(over_core, c >= 0), (over_side, c >= 0), (left, c > 0), (right, c < n - 1)]
        )

    def own_rows(owner):
        return pl.ds(pl.multiple_of(owner * rows, rows), rows)

    def dots_copy(owner, far_t):
        source = dots_ref.at[:, own_rows(owner)]
        return pltpu.make_async_remote_copy(
            src_ref=source,
            dst_ref=dots_in.at[c * tp + t],
            send_sem=ds.at[owner * tp + far_t],
            recv_sem=dr.at[c * tp + t],
            device_id={"ctx": owner, "tp": far_t},
            device_id_type=MESH,
        )

    def dots_from(at):
        here = dots_in.at[at]
        return pltpu.make_async_remote_copy(
            src_ref=here,
            dst_ref=here,
            send_sem=ds.at[at],
            recv_sem=dr.at[at],
            device_id=over_core,
            device_id_type=MESH,
        )

    if with_dots:
        for owner in range(n):
            for far_t in range(tp):

                @pl.when((c != owner) | (t != far_t))
                def _():
                    dots_copy(owner, far_t).start()

        dots_in[c * tp + t] = dots_ref[:, own_rows(c)]

    for load in loads:
        load.wait()

    def owner_of(i):
        owner = 0
        for at in range(n):
            for turn, far in enumerate(sorted(range(n), key=lambda o: -abs(o - at))):
                owner = jnp.where((c == at) & (i == turn), far, owner)
        return owner

    def to_core(i):
        return remote(core_out.at[i], core_in.at[i], (cs, cr), i, over_core)

    def to_side(i):
        return remote(side_out.at[i], side_in.at[i], (ys, yr), i, over_side)

    def to_left(owner):
        return remote(z_out.at[owner], z_in.at[1, owner], (zs, zr), n + owner, left)

    def to_right(owner):
        return remote(z_out.at[owner], z_in.at[0, owner], (zs, zr), owner, right)

    def product(i, which, into):
        taken = lhs[own_rows(owner_of(i)), :]
        for j in range(half_blocks):
            w = weights[which * half_blocks + j]
            into(j, dot(taken, w) if flipped else dot_t(taken, w))

    def columns_of(j):
        return pl.ds(j * wide, wide)

    def quarter(which):
        return pl.ds(pl.multiple_of(which * part, part), part)

    def begin(i):
        def send_part(j, v):
            core_out[i, :, columns_of(j)] = v.astype(core_out.dtype)

        def keep_part(j, v):
            keep[lax.rem(i, 2), :, columns_of(j)] = v

        product(i, 1 - core, send_part)
        to_core(i).start()
        product(i, core, keep_part)

    def cross(i):
        to_core(i).wait_recv()
        slot = lax.rem(i, 2)

        def summed(which):
            return keep[slot, :, quarter(which)] + core_in[i, :, quarter(which)].astype(F32)

        side_out[i] = summed(1 - side).astype(side_out.dtype)
        to_side(i).start()
        near[slot] = summed(side)

    def finish(i):
        to_side(i).wait_recv()
        owner = owner_of(i)
        total = near[lax.rem(i, 2)] + side_in[i].astype(F32)

        @pl.when(owner > c)
        def _():
            @pl.when(c > 0)
            def _():
                to_right(owner).wait_recv()
                z_out[owner] = (total + z_in[0, owner].astype(F32)).astype(z_out.dtype)

            @pl.when(c == 0)
            def _():
                z_out[owner] = total.astype(z_out.dtype)

            to_right(owner).start()

        @pl.when(owner < c)
        def _():
            @pl.when(c < n - 1)
            def _():
                to_left(owner).wait_recv()
                z_out[owner] = (total + z_in[1, owner].astype(F32)).astype(z_out.dtype)

            @pl.when(c == n - 1)
            def _():
                z_out[owner] = total.astype(z_out.dtype)

            to_left(owner).start()

        @pl.when(owner == c)
        def _():
            out_ref[...] = total

    def step(i, carry):
        @pl.when(i < n)
        def _():
            begin(i)

        @pl.when(i > 1)
        def _():
            finish(i - 2)

        @pl.when((i > 0) & (i <= n))
        def _():
            cross(i - 1)

        return carry

    lax.fori_loop(0, n + 2, step, 0)

    @pl.when(c > 0)
    def _():
        to_right(c).wait_recv()
        out_ref[...] += z_in[0, c].astype(F32)

    @pl.when(c < n - 1)
    def _():
        to_left(c).wait_recv()
        out_ref[...] += z_in[1, c].astype(F32)

    if with_dots:
        for at in range(n * tp):

            @pl.when(c * tp + t != at)
            def _():
                dots_from(at).wait_recv()

        for at in range(n):
            dots_out[at] = sum(dots_in[at * tp + far_t] for far_t in range(tp))
        for owner in range(n):
            for far_t in range(tp):

                @pl.when((c != owner) | (t != far_t))
                def _():
                    dots_copy(owner, far_t).wait_send()

    def close(i, carry):
        to_core(i).wait_send()
        to_side(i).wait_send()
        owner = owner_of(i)

        @pl.when(owner > c)
        def _():
            to_right(owner).wait_send()

        @pl.when(owner < c)
        def _():
            to_left(owner).wait_send()

        return carry

    lax.fori_loop(0, n, close, 0)


def returns(lhs, own, others, dots, flipped, ident):
    n, tp = lax.axis_size("ctx"), lax.axis_size("tp")
    kinds, mine = len(lhs), len(lhs[0])
    blocks = len(others[0]) + 1
    pack, fine = lhs[0][0].shape
    wide = own[0].shape[2 if flipped else 1]
    rows, part = pack // n, wide * blocks // tp
    deep = kinds * mine * fine
    dma, vmem = pltpu.SemaphoreType.DMA, pltpu.VMEM
    hbm = pl.BlockSpec(memory_space=pl.ANY)
    near = pl.BlockSpec(memory_space=pltpu.VMEM)
    operands = [v for kind in lhs for v in kind] + list(own) + [v for kind in others for v in kind]
    in_specs = [hbm] * len(operands)
    out_shape = [jax.ShapeDtypeStruct((rows, part), F32)]
    extra = []
    if dots is not None:
        operands.append(dots)
        in_specs.append(near)
        out_shape.append(jax.ShapeDtypeStruct((n, mine, rows), F32))
        extra = [vmem((n * tp, mine, rows), F32), dma((n * tp,)), dma((n * tp,))]
    return pl.pallas_call(
        functools.partial(returns_kernel, kinds, mine, blocks, flipped, dots is not None),
        cost_estimate=pl.CostEstimate(flops=65 * MICRO, bytes_accessed=0, transcendentals=0),
        out_shape=out_shape,
        in_specs=in_specs,
        out_specs=[near] * len(out_shape),
        scratch_shapes=[
            vmem((pack, deep), BF16),
            vmem((blocks, deep, wide) if flipped else (blocks, wide, deep), BF16),
            vmem((n, rows, 2 * part), BF16),
            vmem((n, rows, 2 * part), BF16),
            vmem((2, rows, 2 * part), F32),
            vmem((2, rows, part), F32),
            vmem((n, rows, part), BF16),
            vmem((n, rows, part), BF16),
            vmem((n, rows, part), BF16),
            vmem((2, n, rows, part), BF16),
            dma((kinds * mine,)),
            dma((kinds * mine * blocks,)),
        ]
        + [dma((n,))] * 4
        + [dma((2 * n,))] * 2
        + extra,
        compiler_params=pltpu.CompilerParams(
            collective_id=ident, has_side_effects=True, vmem_limit_bytes=56 << 20
        ),
    )(*operands)


def body(
    tokens,
    cotangent,
    lengths,
    routes,
    attn_gain,
    w_query,
    w_key,
    w_value,
    q_gain,
    k_gain,
    w_out,
    mlp_gain,
    w_router,
    w_gate,
    w_up,
    w_down,
):
    dp_at, ctx_at, tp_at = (lax.axis_index(a) for a in ("dp", "ctx", "tp"))
    dp_count, ctx_count, tp_count = (lax.axis_size(a) for a in ("dp", "ctx", "tp"))
    rows, width = tokens.shape
    wide = w_query.shape[0]
    local = w_query.shape[1]
    heads = local // HEAD
    experts = w_router.shape[1]
    mine = experts // ctx_count
    part = width // tp_count
    column_at = lax.rem(tp_at, 2) * 2 + tp_at // 2

    def fetch(v):
        others = [
            lax.ppermute(v, "dp", [((i + s) % dp_count, i) for i in range(dp_count)])
            for s in range(1, dp_count)
        ]
        return [v] + others

    def hand_over(blocks):
        total = blocks[0].astype(F32)
        for s in range(1, dp_count):
            pairs = [(i, (i + s) % dp_count) for i in range(dp_count)]
            total = total + lax.ppermute(blocks[s].astype(BF16), "dp", pairs).astype(F32)
        return total

    def columns(v):
        return lax.dynamic_slice_in_dim(v, column_at * part, part, v.ndim - 1)

    def block(v, s):
        return v[:, s * wide : (s + 1) * wide]

    def own_experts(w):
        return lax.dynamic_slice_in_dim(w, ctx_at * mine, mine, 0)

    small = jnp.concatenate(
        [attn_gain[None], q_gain[None], k_gain[None], mlp_gain[None], w_router.T], axis=0
    )
    small = jnp.concatenate(fetch(small), axis=1)
    gains = small[:4].astype(F32)
    router_w = small[4:]
    gain_one, gain_two = gains[0], columns(gains[3])

    def heads_gain(v):
        back = jnp.roll(v, dp_at * wide)
        return lax.dynamic_slice_in_dim(back, tp_at * local, local)

    gain_q, gain_k = heads_gain(gains[1]), heads_gain(gains[2])
    query_w, key_w, value_w = fetch(w_query), fetch(w_key), fetch(w_value)
    out_w = fetch(w_out)
    gate_others = fetch(own_experts(w_gate))[1:]
    up_others = fetch(own_experts(w_up))[1:]
    down_others = fetch(own_experts(w_down))[1:]
    tokens = jnp.roll(tokens, -dp_at * wide, axis=1)
    cotangent = jnp.roll(cotangent, -dp_at * wide, axis=1)
    chosen = jnp.any(
        routes[:, :, None] == jnp.arange(experts, dtype=jnp.int32)[None, None, :], axis=1
    )
    upstream_all = jnp.concatenate(
        [
            lax.dynamic_slice_in_dim(cotangent, tp_at * part, part, 1),
            jnp.pad(chosen.astype(BF16), ((0, 0), (0, HEAD - experts))),
        ],
        axis=1,
    )
    upstream_all = lax.all_gather(upstream_all, "ctx", axis=0, tiled=True)
    chosen_all = upstream_all[:, part : part + experts].astype(F32)
    upstream_all = lax.all_gather(upstream_all[:, :part], "tp", axis=1, tiled=True)

    inputs = tokens.astype(F32)
    scale_one = lax.rsqrt(jnp.mean(inputs * inputs, axis=1, keepdims=True) + EPS)
    hidden_one = (inputs * scale_one * gain_one).astype(BF16)

    def project(blocks):
        return sum(dot(block(hidden_one, s), w) for s, w in enumerate(blocks))

    q_raw, k_raw = project(query_w), project(key_w)
    values = project(value_w).astype(BF16)
    squares = lax.psum(
        jnp.stack([jnp.sum(q_raw * q_raw, axis=1), jnp.sum(k_raw * k_raw, axis=1)]), "tp"
    )
    q_scale, k_scale = lax.rsqrt(squares / width + EPS)[:, :, None]
    q_hat, k_hat = q_raw * q_scale, k_raw * k_scale
    cosine, sine = rotation(lengths[0], ctx_at * rows, rows)

    def turn(v):
        return rotate(v.reshape(rows, heads, HEAD), cosine, sine).astype(BF16)

    q_all, k_all, v_all = to_heads(
        (turn(q_hat * gain_q), turn(k_hat * gain_k), values), heads
    )
    q_all, out_w, gate_others = lax.optimization_barrier((q_all, out_w, gate_others))
    attended_all, log = attend(lengths, q_all, k_all, v_all)
    attended = to_rows((attended_all,))[0].reshape(rows, local)
    branch = jnp.concatenate([dot(attended, w).astype(BF16) for w in out_w], axis=1)
    branch, up_others = lax.optimization_barrier((branch, up_others))
    branch = collect(branch, 1, 2)
    inputs_c = columns(inputs)
    mixed = inputs_c + branch
    square = lax.psum(jnp.sum(mixed * mixed, axis=1), "tp")
    scale_two = lax.rsqrt(square / width + EPS)[:, None]
    normed_two = mixed * scale_two
    hidden_mine = (normed_two * gain_two).astype(BF16)
    hidden_two = spread(hidden_mine, 3)
    hidden_two, down_others = lax.optimization_barrier((hidden_two, down_others))

    parts, sums = [], []
    for e in range(mine):
        at = ctx_at * mine + e
        if e > 1:
            hidden_two, sums[e - 2] = lax.optimization_barrier((hidden_two, sums[e - 2]))
        parts.append(
            expert(
                jnp.stack([at, jnp.int32(e)]).astype(jnp.int32),
                hidden_two,
                upstream_all,
                chosen_all,
                router_w,
                [w_gate] + gate_others,
                [w_up] + up_others,
                [w_down] + down_others,
            )
        )
        sums.append(hand_over(list(parts[-1][-1])).astype(BF16))

    gathered = [lax.all_gather(v, "ctx", axis=0, tiled=False) for v in sums]

    dots = jnp.concatenate([p[3] for p in parts], axis=1).T
    expert_in, dots = returns(
        [[p[1] for p in parts], [p[2] for p in parts]],
        [w_gate, w_up],
        [gate_others, up_others],
        dots,
        False,
        4,
    )

    dots = dots.reshape(experts, rows).T
    hidden_rows = lax.dynamic_slice_in_dim(hidden_two, ctx_at * rows, rows, 0)
    route_mine = jax.nn.softmax(dot_t(hidden_rows, router_w), axis=1)
    d_logits = (
        route_mine * (dots - jnp.sum(route_mine * dots, axis=1, keepdims=True))
    ).astype(BF16)
    router_grad = t_dot(d_logits, hidden_mine)
    d_hidden_two = expert_in + dot(d_logits, columns(router_w))
    gain_two_grad = jnp.sum(d_hidden_two * normed_two, axis=0)
    pull_two = d_hidden_two * gain_two
    mean_two = lax.psum(jnp.sum(pull_two * mixed, axis=1), "tp")[:, None] / width
    d_mixed = (
        columns(cotangent).astype(F32) + scale_two * pull_two - mixed * scale_two**3 * mean_two
    )

    d_branch = join(d_mixed.astype(BF16), 7)
    d_attended = sum(dot_t(block(d_branch, s), w) for s, w in enumerate(out_w)).astype(BF16)
    d_all = to_heads((d_attended,), heads)[0]
    d_all, gathered[0] = lax.optimization_barrier((d_all, gathered[0]))
    dq_all, dk_all, dv_all = attend_back(lengths, q_all, k_all, v_all, d_all, log)
    d_query, d_key, d_value = to_rows((dq_all, dk_all, dv_all))
    d_values_raw = d_value.reshape(rows, local)
    d_q_normed = rotate(d_query.astype(F32), cosine, -sine).reshape(rows, local)
    d_k_normed = rotate(d_key.astype(F32), cosine, -sine).reshape(rows, local)
    q_pull, k_pull = d_q_normed * gain_q, d_k_normed * gain_k
    totals = lax.psum(
        jnp.stack([jnp.sum(q_pull * q_raw, axis=1), jnp.sum(k_pull * k_raw, axis=1)]), "tp"
    )
    q_mean, k_mean = totals[:, :, None] / width
    d_q_raw = (q_scale * q_pull - q_raw * q_scale**3 * q_mean).astype(BF16)
    d_k_raw = (k_scale * k_pull - k_raw * k_scale**3 * k_mean).astype(BF16)
    d_hidden = jnp.concatenate(
        [
            (
                dot_t(d_q_raw, query_w[s])
                + dot_t(d_k_raw, key_w[s])
                + dot_t(d_values_raw, value_w[s])
            ).astype(BF16)
            for s in range(dp_count)
        ],
        axis=1,
    )
    d_hidden, gathered[1] = lax.optimization_barrier((d_hidden, gathered[1]))
    d_hidden = collect(d_hidden, 1, 8)
    gain_one_grad = jnp.sum(d_hidden * inputs_c * scale_one, axis=0)
    pull_one = d_hidden * columns(gain_one)
    mean_one = lax.psum(jnp.sum(pull_one * inputs_c, axis=1), "tp")[:, None] / width
    d_inputs = d_mixed + scale_one * pull_one - inputs_c * scale_one**3 * mean_one
    d_inputs = jnp.roll(join(d_inputs, 9), dp_at * wide, axis=1)

    def in_order(v):
        return jnp.roll(v, dp_at * wide, axis=-1)

    small_grads = jnp.concatenate(
        [
            gain_one_grad[None],
            gain_two_grad[None],
            router_grad,
            jnp.sum(d_q_normed * q_hat, axis=0)[None],
            jnp.sum(d_k_normed * k_hat, axis=0)[None],
        ]
    )
    small_grads = lax.all_gather(small_grads, "tp", axis=0, tiled=False)
    turned = [small_grads[(p % 2) * 2 + p // 2, : 2 + experts] for p in range(tp_count)]
    heads_grads = small_grads[:, 2 + experts :].transpose(1, 0, 2).reshape(2, width)
    heads_grads = jnp.roll(heads_grads, -dp_at * wide, axis=1)
    small_grads = jnp.concatenate([jnp.concatenate(turned, axis=1), heads_grads])
    small_rows = small_grads.shape[0] * wide // local
    filler = -small_rows % (16 * ctx_count)

    def grad_blocks(s):
        hidden, grads = block(hidden_one, s), (d_q_raw, d_k_raw, d_values_raw)
        small = block(small_grads, s).reshape(small_rows, local)
        return jnp.concatenate(
            [t_dot(hidden, d) for d in grads]
            + [t_dot(block(d_branch, s), attended), jnp.pad(small, ((0, filler), (0, 0)))]
        )

    grads = hand_over([grad_blocks(s) for s in range(dp_count)]).astype(BF16)
    grads = lax.psum_scatter(grads, "ctx", scatter_dimension=0, tiled=True)
    grads = lax.all_gather(grads, "ctx", axis=0, tiled=True).astype(F32)
    grad_query, grad_key, grad_value, grad_out = (
        grads[i * wide : (i + 1) * wide] for i in range(4)
    )
    small_grads = grads[4 * wide : 4 * wide + small_rows].reshape(-1, wide)

    inners = [p[0] for p in parts]
    inners, d_inputs = lax.optimization_barrier((inners, d_inputs))
    (mixture,) = returns([inners], [w_down], [down_others], None, True, 5)
    mixture, gathered[2] = lax.optimization_barrier((mixture, gathered[2]))
    output = jnp.roll(join(mixed + mixture, 6), dp_at * wide, axis=1)

    fine = w_gate.shape[2]

    def assemble(which):
        each = [v[:, which].astype(F32) for v in gathered]
        if which == 2:
            each = [
                v.reshape(ctx_count, wide // fine, fine, fine)
                .transpose(0, 2, 1, 3)
                .reshape(ctx_count, fine, wide)
                for v in each
            ]
        stacked = jnp.stack(each, axis=1)
        return stacked.reshape((experts,) + stacked.shape[2:])

    return (
        output,
        d_inputs,
        small_grads[0],
        grad_query,
        grad_key,
        grad_value,
        small_grads[2 + experts],
        small_grads[3 + experts],
        grad_out.T,
        small_grads[1],
        small_grads[2 : 2 + experts].T,
        assemble(0),
        assemble(1),
        assemble(2),
    )


def solution(mesh):
    in_specs = (
        P(("dp", "ctx"), None),
        P(("dp", "ctx"), None),
        P("dp", None),
        P(("dp", "ctx"), None),
        P("dp"),
        P("dp", "tp"),
        P("dp", "tp"),
        P("dp", "tp"),
        P("dp"),
        P("dp"),
        P("tp", "dp"),
        P("dp"),
        P("dp", None),
        P(None, "dp", "tp"),
        P(None, "dp", "tp"),
        P(None, "tp", "dp"),
    )
    out_specs = (
        P(("dp", "ctx"), None),
        P(("dp", "ctx"), None),
        P("dp"),
        P("dp", "tp"),
        P("dp", "tp"),
        P("dp", "tp"),
        P("dp"),
        P("dp"),
        P("tp", "dp"),
        P("dp"),
        P("dp", None),
        P(None, "dp", "tp"),
        P(None, "dp", "tp"),
        P(None, "tp", "dp"),
    )
    return jax.shard_map(body, mesh=mesh, in_specs=in_specs, out_specs=out_specs, check_vma=False)
```

```python
import functools

import jax
import jax.numpy as jnp
from jax import lax
from jax.experimental import pallas as pl
from jax.experimental.pallas import tpu as pltpu
from jax.sharding import PartitionSpec as P

HEAD = 128
EPS = 1e-05
THETA = 10000.0
BLOCK = 256
BF16 = jnp.bfloat16
F32 = jnp.float32
MESH = pl.DeviceIdType.MESH
MICRO = 1 << 26


def dot(a, b):
    return jnp.dot(a, b, preferred_element_type=F32)


def dot_t(a, b):
    return lax.dot_general(a, b, (((1,), (1,)), ((), ())), preferred_element_type=F32)


def t_dot(a, b):
    return lax.dot_general(a, b, (((0,), (0,)), ((), ())), preferred_element_type=F32)


def rotation(row, first, rows):
    ends = jnp.cumsum(row)
    index = first + jnp.arange(rows, dtype=jnp.int32)
    before = jnp.where(index[:, None] >= ends[None, :], ends[None, :], 0)
    position = index - jnp.max(before, axis=1)
    inverse = THETA ** (-jnp.arange(0, HEAD, 2).astype(F32) / HEAD)
    angle = position.astype(F32)[:, None] * inverse[None, :]
    cosine, sine = jnp.cos(angle), jnp.sin(angle)
    return (
        jnp.concatenate([cosine, cosine], axis=1)[:, None, :],
        jnp.concatenate([-sine, sine], axis=1)[:, None, :],
    )


def rotate(v, cosine, sine):
    return v * cosine + jnp.roll(v, HEAD // 2, axis=2) * sine


def allowed_block(lengths_ref, base, rows, columns):
    index = base + lax.broadcasted_iota(jnp.int32, (rows, 1), 0)
    start = jnp.zeros((rows, 1), jnp.int32)
    end = 0
    for at in range(lengths_ref.shape[1]):
        end = end + lengths_ref[0, at]
        start = jnp.where(index >= end, end, start)
    key = lax.broadcasted_iota(jnp.int32, (rows, columns), 1)
    return (key >= start) & (key <= index)


def attend_kernel(lengths_ref, q_ref, k_ref, v_ref, out_ref, log_ref):
    scale = HEAD ** (-0.5)
    rows = q_ref.shape[0]
    for base in range(0, rows, BLOCK):
        upto = base + BLOCK
        own = pl.ds(base, BLOCK)
        keys, values = k_ref[pl.ds(0, upto), :], v_ref[pl.ds(0, upto), :]
        scores = dot_t(q_ref[own, :], keys) * scale
        scores = jnp.where(allowed_block(lengths_ref, base, BLOCK, upto), scores, -1e30)
        top = jnp.max(scores, axis=1, keepdims=True)
        weights = jnp.exp(scores - top)
        total = jnp.sum(weights, axis=1, keepdims=True)
        probs = (weights * (1.0 / total)).astype(BF16)
        out_ref[own, :] = dot(probs, values).astype(BF16)
        log_ref[own, :] = top + jnp.log(total)


def attend(lengths, q, k, v):
    heads, rows, _ = q.shape
    spec = pl.BlockSpec((None, rows, HEAD), lambda h: (h, 0, 0))
    column = pl.BlockSpec((None, rows, 1), lambda h: (h, 0, 0))
    return pl.pallas_call(
        attend_kernel,
        cost_estimate=pl.CostEstimate(flops=7 * MICRO, bytes_accessed=0, transcendentals=0),
        grid=(heads,),
        out_shape=(
            jax.ShapeDtypeStruct((heads, rows, HEAD), BF16),
            jax.ShapeDtypeStruct((heads, rows, 1), F32),
        ),
        in_specs=[pl.BlockSpec(memory_space=pltpu.SMEM), spec, spec, spec],
        out_specs=(spec, column),
        compiler_params=pltpu.CompilerParams(vmem_limit_bytes=48 << 20),
    )(lengths, q, k, v)


def attend_back_kernel(
    lengths_ref, q_ref, k_ref, v_ref, d_ref, log_ref, dq_ref, dk_ref, dv_ref, dk_sum, dv_sum
):
    scale = HEAD ** (-0.5)
    rows = q_ref.shape[0]
    dk_sum[...] = jnp.zeros_like(dk_sum)
    dv_sum[...] = jnp.zeros_like(dv_sum)
    for base in range(0, rows, BLOCK):
        upto = base + BLOCK
        own, seen = pl.ds(base, BLOCK), pl.ds(0, upto)
        q, d = q_ref[own, :], d_ref[own, :]
        keys, values = k_ref[seen, :], v_ref[seen, :]
        scores = dot_t(q, keys) * scale - log_ref[own, :]
        probs = jnp.where(
            allowed_block(lengths_ref, base, BLOCK, upto), jnp.exp(scores), 0.0
        )
        d_probs = dot_t(d, values)
        delta = jnp.sum(probs * d_probs, axis=1, keepdims=True)
        d_raw = (probs * (d_probs - delta) * scale).astype(BF16)
        dq_ref[own, :] = dot(d_raw, keys).astype(dq_ref.dtype)
        dk_sum[seen, :] += t_dot(d_raw, q)
        dv_sum[seen, :] += t_dot(probs.astype(BF16), d)
    dk_ref[...] = dk_sum[...].astype(dk_ref.dtype)
    dv_ref[...] = dv_sum[...].astype(dv_ref.dtype)


def attend_back(lengths, q, k, v, d, log):
    heads, rows, _ = q.shape
    spec = pl.BlockSpec((None, rows, HEAD), lambda h: (h, 0, 0))
    column = pl.BlockSpec((None, rows, 1), lambda h: (h, 0, 0))
    return pl.pallas_call(
        attend_back_kernel,
        cost_estimate=pl.CostEstimate(flops=10 * MICRO, bytes_accessed=0, transcendentals=0),
        grid=(heads,),
        out_shape=(jax.ShapeDtypeStruct((heads, rows, HEAD), F32),) * 2
        + (jax.ShapeDtypeStruct((heads, rows, HEAD), BF16),),
        in_specs=[pl.BlockSpec(memory_space=pltpu.SMEM), spec, spec, spec, spec, column],
        out_specs=(spec,) * 3,
        scratch_shapes=[pltpu.VMEM((rows, HEAD), F32)] * 2,
        compiler_params=pltpu.CompilerParams(vmem_limit_bytes=48 << 20),
    )(lengths, q, k, v, d, log)


def to_heads(parts, heads):
    count = lax.axis_size("ctx")
    rows = parts[0].shape[0]
    stacked = jnp.stack([p.reshape(rows, count, heads // count, HEAD) for p in parts])
    sent = stacked.transpose(2, 0, 3, 1, 4)
    got = lax.all_to_all(sent, "ctx", 0, 0, tiled=True)
    return got.transpose(1, 2, 0, 3, 4).reshape(len(parts), heads // count, count * rows, HEAD)


def to_rows(parts):
    count = lax.axis_size("ctx")
    mine, pack, _ = parts[0].shape
    stacked = jnp.stack([p.reshape(mine, count, pack // count, HEAD) for p in parts])
    sent = stacked.transpose(2, 0, 1, 3, 4)
    got = lax.all_to_all(sent, "ctx", 0, 0, tiled=True)
    turned = got.transpose(1, 3, 0, 2, 4)
    return turned.reshape(len(parts), pack // count, count * mine, HEAD)


def carried(pairs, sems):
    d, count = lax.axis_index("dp"), lax.axis_size("dp")
    copies, partners = [], []
    for axis, source, target in pairs:
        send, recv = sems[axis]
        if axis == "z":
            partner = {"ctx": jnp.bitwise_xor(lax.axis_index("ctx"), 1)}
            copies.append(remote(source, target, (send, recv), 0, partner))
            partners.append((partner, d >= 0))
            continue
        for s in range(1, count):
            partner = {"dp": lax.rem(d + s, count)}
            copies.append(remote(source.at[s - 1], target.at[s - 1], (send, recv), s - 1, partner))
            partners.append((partner, d >= 0))
    return copies, partners


def carry_operands(carry):
    dma = pltpu.SemaphoreType.DMA
    shapes, sems = [], []
    for axis, v in carry:
        shapes.append(jax.ShapeDtypeStruct(v.shape, v.dtype))
        sems += [dma((v.shape[0] if axis == "x" else 1,))] * 2
    return [v for _, v in carry], shapes, sems


def expert_kernel(blocks, number, far, mine, full, axes, *refs):
    refs = list(refs)

    def take(count):
        return [refs.pop(0) for _ in range(count)]

    hidden_ref, up_ref, chosen_ref, router_ref = take(4)
    gate_w, up_w, down_w = take(blocks), take(blocks), take(blocks)
    sources = take(len(axes))
    if full:
        inner_ref, dgate_ref, dup_ref, dots_ref = take(4)
    near_ref, others_ref = take(2)
    targets = take(len(axes))
    gate_sum, up_sum, down_sum = take(3)
    sems = {axis: take(2) for axis in axes}
    turn, last = pl.program_id(0), pl.num_programs(0) - 1
    wide = gate_w[0].shape[0]

    def transfers():
        return carried(list(zip(axes, sources, targets)), sems)

    if axes:

        @pl.when(turn == 0)
        def _():
            copies, partners = transfers()
            signal_all(partners)
            for copy in copies:
                copy.start()

    hidden, upstream = hidden_ref[...], up_ref[...]

    def over(v, ws, f):
        return sum(f(v[:, s * wide : (s + 1) * wide], w[...]) for s, w in enumerate(ws))

    gate, up = over(hidden, gate_w, dot), over(hidden, up_w, dot)
    pulled = over(upstream, down_w, dot_t)
    logits = dot_t(hidden, router_ref[...])
    odds = jnp.exp(logits - jnp.max(logits, axis=1, keepdims=True))
    probs = odds / jnp.sum(odds, axis=1, keepdims=True) * chosen_ref[...]
    plane = lax.axis_index("ctx")
    if far:
        plane = jnp.bitwise_xor(plane, 2)
    named = lax.broadcasted_iota(jnp.int32, probs.shape, 1) == plane * mine + number
    weight = jnp.sum(jnp.where(named, probs, 0.0), axis=1, keepdims=True)
    sigma = jax.nn.sigmoid(gate)
    active = gate * sigma
    inner = (active * up).astype(BF16).astype(F32)
    if full:
        dots = jnp.sum(inner * pulled, axis=1, keepdims=True)
        dots_ref[...] = jnp.where(weight > 0.0, dots, 0.0)
    inner = (weight * inner).astype(BF16)
    pulled = weight * pulled
    d_gate = (pulled * up * sigma * (1.0 + gate * (1.0 - sigma))).astype(BF16)
    d_up = (pulled * active).astype(BF16)
    if full:
        inner_ref[...], dgate_ref[...], dup_ref[...] = inner, d_gate, d_up

    @pl.when(turn == 0)
    def _():
        gate_sum[...] = t_dot(d_gate, hidden)
        up_sum[...] = t_dot(d_up, hidden)
        down_sum[...] = t_dot(inner, upstream)

    @pl.when(turn > 0)
    def _():
        gate_sum[...] += t_dot(d_gate, hidden)
        up_sum[...] += t_dot(d_up, hidden)
        down_sum[...] += t_dot(inner, upstream)

    @pl.when(turn == last)
    def _():
        fine = down_sum.shape[0]
        for s in range(blocks):
            target = near_ref if s == 0 else others_ref.at[s - 1]
            own = pl.ds(s * wide, wide)
            target[0] = gate_sum[:, own].T.astype(BF16)
            target[1] = up_sum[:, own].T.astype(BF16)
            for j in range(wide // fine):
                target[2, pl.ds(j * fine, fine), :] = down_sum[
                    :, pl.ds(s * wide + j * fine, fine)
                ].astype(BF16)
        if axes:
            for copy in transfers()[0]:
                copy.wait()


def expert(e, hidden, upstream, chosen, router, weights, far, full, carry, ident, tile=512):
    both_w, down_w = weights
    blocks = len(both_w)
    pack, width = hidden.shape
    mine, fine, wide = down_w[0].shape
    operands, shapes, sems = carry_operands(carry)
    hbm = pl.BlockSpec(memory_space=pl.ANY)

    def token(n):
        return pl.BlockSpec((tile, n), lambda i: (i, 0))

    def weight(first, *shape):
        return pl.BlockSpec((None,) + shape, lambda i: (first + e, 0, 0))

    near = pl.BlockSpec((3, wide, fine), lambda i: (0, 0, 0))
    others = pl.BlockSpec((blocks - 1, 3, wide, fine), lambda i: (0, 0, 0, 0))
    out_specs, out_shape = [near, others], [
        jax.ShapeDtypeStruct((3, wide, fine), BF16),
        jax.ShapeDtypeStruct((blocks - 1, 3, wide, fine), BF16),
    ]
    if full:
        out_specs = [token(fine)] * 3 + [token(1)] + out_specs
        out_shape = (
            [jax.ShapeDtypeStruct((pack, fine), BF16)] * 3
            + [jax.ShapeDtypeStruct((pack, 1), F32)]
            + out_shape
        )
    remote_params = dict(collective_id=ident, has_side_effects=True) if carry else {}
    return pl.pallas_call(
        functools.partial(expert_kernel, blocks, e, far, mine, full, [axis for axis, _ in carry]),
        cost_estimate=pl.CostEstimate(flops=27 * MICRO, bytes_accessed=0, transcendentals=0),
        grid=(pack // tile,),
        in_specs=[token(width), token(width), token(chosen.shape[1])]
        + [pl.BlockSpec(router.shape, lambda i: (0, 0))]
        + [weight(0, wide, fine)] * blocks
        + [weight(mine, wide, fine)] * blocks
        + [weight(0, fine, wide)] * blocks
        + [hbm] * len(operands),
        out_specs=out_specs + [hbm] * len(shapes),
        out_shape=out_shape + shapes,
        scratch_shapes=[pltpu.VMEM((fine, width), F32)] * 3 + sems,
        compiler_params=pltpu.CompilerParams(vmem_limit_bytes=56 << 20, **remote_params),
    )(hidden, upstream, chosen, router, *both_w, *both_w, *down_w, *operands)


def signal_all(partners):
    barrier = pltpu.get_barrier_semaphore()
    count = 0
    for device, there in partners:

        @pl.when(there)
        def _():
            pl.semaphore_signal(barrier, inc=1, device_id=device, device_id_type=MESH)

        count = count + jnp.where(there, 1, 0)
    pl.semaphore_wait(barrier, count)


def place():
    c, t = lax.axis_index("ctx"), lax.axis_index("tp")
    core, side = lax.rem(t, 2), t // 2
    over_core = {"tp": t + 1 - 2 * core}
    over_side = {"tp": t + 2 - 4 * side}
    return c, lax.axis_size("ctx"), core, side, over_core, over_side


def remote(source, target, sems, at, device):
    send, recv = sems
    return pltpu.make_async_remote_copy(
        src_ref=source,
        dst_ref=target,
        send_sem=send.at[at],
        recv_sem=recv.at[at],
        device_id=device,
        device_id_type=MESH,
    )


def spread_kernel(x_ref, out_ref, local, zs, zr, ys, yr, cs, cr):
    c, n, core, side, over_core, over_side = place()
    rows, part = x_ref.shape
    left, right = {"ctx": c - 1}, {"ctx": c + 1}
    signal_all([(left, c > 0), (right, c < n - 1), (over_core, c >= 0), (over_side, c >= 0)])
    mine = core * 2 + side
    other = core * 2 + 1 - side

    def tile(owner, column):
        return out_ref.at[
            pl.ds(pl.multiple_of(owner * rows, rows), rows),
            pl.ds(pl.multiple_of(column * part, part), part),
        ]

    def along(owner, source, target, at):
        return remote(source, tile(owner, mine), (zs, zr), at, target)

    keep = pltpu.make_async_copy(x_ref, tile(c, mine), local)
    keep.start()

    @pl.when(c > 0)
    def _():
        along(c, x_ref, left, n + c).start()

    @pl.when(c < n - 1)
    def _():
        along(c, x_ref, right, c).start()

    def to_side(owner, source):
        return remote(source, tile(owner, mine), (ys, yr), owner, over_side)

    def to_core(owner, column, source, which):
        return remote(source, tile(owner, column), (cs, cr), which * n + owner, over_core)

    to_side(c, x_ref).start()
    to_core(c, mine, x_ref, 0).start()

    def from_side(owner):
        here = tile(owner, other)
        remote(here, here, (ys, yr), owner, over_side).wait_recv()
        to_core(owner, other, here, 1).start()

    from_side(c)
    for far in range(1, n):
        for sign, there, onward, more in (
            (-1, c - far >= 0, right, c < n - 1),
            (1, c + far < n, left, c > 0),
        ):
            owner = c + sign * far
            slot = owner if sign < 0 else n + owner

            @pl.when(there)
            def _():
                here = tile(owner, mine)
                along(owner, here, onward, slot).wait_recv()

                @pl.when(more)
                def _():
                    along(owner, here, onward, slot).start()

                to_side(owner, here).start()
                to_core(owner, mine, here, 0).start()

        for sign, there in ((-1, c - far >= 0), (1, c + far < n)):

            @pl.when(there)
            def _():
                from_side(c + sign * far)

    keep.wait()

    @pl.when(c > 0)
    def _():
        along(c, x_ref, left, n + c).wait_send()

    @pl.when(c < n - 1)
    def _():
        along(c, x_ref, right, c).wait_send()

    for far in range(1, n):
        for sign, there, onward, more in (
            (-1, c - far >= 0, right, c < n - 1),
            (1, c + far < n, left, c > 0),
        ):
            owner = c + sign * far

            @pl.when(there & more)
            def _():
                here = tile(owner, mine)
                along(owner, here, onward, owner if sign < 0 else n + owner).wait_send()

    for owner in range(n):
        to_side(owner, tile(owner, mine)).wait_send()
        to_core(owner, mine, tile(owner, mine), 0).wait_send()
        to_core(owner, other, tile(owner, other), 1).wait_send()
        for which, column in ((0, (1 - core) * 2 + side), (1, (1 - core) * 2 + 1 - side)):
            here = tile(owner, column)
            remote(here, here, (cs, cr), which * n + owner, over_core).wait_recv()


def spread(v, ident):
    n, tp = lax.axis_size("ctx"), lax.axis_size("tp")
    rows, part = v.shape
    dma = pltpu.SemaphoreType.DMA
    return pl.pallas_call(
        spread_kernel,
        cost_estimate=pl.CostEstimate(flops=60 * MICRO, bytes_accessed=0, transcendentals=0),
        out_shape=jax.ShapeDtypeStruct((n * rows, tp * part), v.dtype),
        in_specs=[pl.BlockSpec(memory_space=pl.ANY)],
        out_specs=pl.BlockSpec(memory_space=pl.ANY),
        scratch_shapes=[dma] + [dma((2 * n,))] * 2 + [dma((n,))] * 2 + [dma((2 * n,))] * 2,
        compiler_params=pltpu.CompilerParams(collective_id=ident, has_side_effects=True),
    )(v)


def join_kernel(x_ref, out_ref, local, ss, sr):
    c, n, core, side, over_core, over_side = place()
    rows, part = x_ref.shape
    signal_all([(over_core, c >= 0), (over_side, c >= 0)])
    mine, other = core * 2 + side, core * 2 + 1 - side

    def tile(column):
        return out_ref.at[:, pl.ds(pl.multiple_of(column * part, part), part)]

    keep = pltpu.make_async_copy(x_ref, tile(mine), local)
    keep.start()
    first = remote(x_ref, tile(mine), (ss, sr), 0, over_side)
    first.start()
    second = remote(x_ref, tile(mine), (ss, sr), 1, over_core)
    second.start()
    first.wait_recv()
    third = remote(tile(other), tile(other), (ss, sr), 2, over_core)
    third.start()
    keep.wait()
    first.wait_send()
    second.wait()
    third.wait()


def join(v, ident):
    tp = lax.axis_size("tp")
    rows, part = v.shape
    dma = pltpu.SemaphoreType.DMA
    return pl.pallas_call(
        join_kernel,
        cost_estimate=pl.CostEstimate(flops=25 * MICRO, bytes_accessed=0, transcendentals=0),
        out_shape=jax.ShapeDtypeStruct((rows, tp * part), v.dtype),
        in_specs=[pl.BlockSpec(memory_space=pl.ANY)],
        out_specs=pl.BlockSpec(memory_space=pl.ANY),
        scratch_shapes=[dma] + [dma((3,))] * 2,
        compiler_params=pltpu.CompilerParams(collective_id=ident, has_side_effects=True),
    )(v)


def collect_kernel(
    owners, x_ref, out_ref, core_in, side_out, side_in, z_out, z_in, cs, cr, ys, yr, zs, zr
):
    c, n, core, side, over_core, over_side = place()
    rows, part = out_ref.shape
    left, right = {"ctx": c - 1}, {"ctx": c + 1}
    partners = [(over_core, c >= 0), (over_side, c >= 0)]
    if owners > 1:
        partners += [(left, c > 0), (right, c < n - 1)]
    signal_all(partners)

    def owner_of(i):
        if owners == 1:
            return 0
        owner = 0
        for at in range(n):
            for turn, far in enumerate(sorted(range(n), key=lambda o: -abs(o - at))):
                owner = jnp.where((c == at) & (i == turn), far, owner)
        return owner

    def own_rows(owner):
        return pl.ds(pl.multiple_of(owner * rows, rows), rows)

    def half(which):
        return pl.ds(pl.multiple_of(which * 2 * part, 2 * part), 2 * part)

    def quarter(which):
        return pl.ds(pl.multiple_of((core * 2 + which) * part, part), part)

    def to_core(i):
        source = x_ref.at[own_rows(owner_of(i)), half(1 - core)]
        return remote(source, core_in.at[i], (cs, cr), i, over_core)

    def to_side(i):
        return remote(side_out.at[i], side_in.at[i], (ys, yr), i, over_side)

    def to_left(owner):
        return remote(z_out.at[owner], z_in.at[1, owner], (zs, zr), n + owner, left)

    def to_right(owner):
        return remote(z_out.at[owner], z_in.at[0, owner], (zs, zr), owner, right)

    def from_core(i, which):
        local = x_ref[own_rows(owner_of(i)), quarter(which)].astype(F32)
        near = core_in[i, :, pl.ds(pl.multiple_of(which * part, part), part)]
        return local + near.astype(F32)

    for i in range(owners):
        to_core(i).start()

    def finish(i):
        to_side(i).wait_recv()
        owner = owner_of(i)
        total = from_core(i, side) + side_in[i].astype(F32)
        if owners == 1:
            out_ref[...] = total
            return

        @pl.when(owner > c)
        def _():
            @pl.when(c > 0)
            def _():
                to_right(owner).wait_recv()
                z_out[owner] = (total + z_in[0, owner].astype(F32)).astype(z_out.dtype)

            @pl.when(c == 0)
            def _():
                z_out[owner] = total.astype(z_out.dtype)

            to_right(owner).start()

        @pl.when(owner < c)
        def _():
            @pl.when(c < n - 1)
            def _():
                to_left(owner).wait_recv()
                z_out[owner] = (total + z_in[1, owner].astype(F32)).astype(z_out.dtype)

            @pl.when(c == n - 1)
            def _():
                z_out[owner] = total.astype(z_out.dtype)

            to_left(owner).start()

        @pl.when(owner == c)
        def _():
            out_ref[...] = total

    def step(i, carry):
        @pl.when(i < owners)
        def _():
            to_core(i).wait_recv()
            side_out[i] = from_core(i, 1 - side).astype(side_out.dtype)
            to_side(i).start()

        @pl.when(i > 0)
        def _():
            finish(i - 1)

        return carry

    lax.fori_loop(0, owners + 1, step, 0)

    if owners > 1:

        @pl.when(c > 0)
        def _():
            to_right(c).wait_recv()
            out_ref[...] += z_in[0, c].astype(F32)

        @pl.when(c < n - 1)
        def _():
            to_left(c).wait_recv()
            out_ref[...] += z_in[1, c].astype(F32)

    def close(i, carry):
        to_core(i).wait_send()
        to_side(i).wait_send()
        if owners > 1:
            owner = owner_of(i)

            @pl.when(owner > c)
            def _():
                to_right(owner).wait_send()

            @pl.when(owner < c)
            def _():
                to_left(owner).wait_send()

        return carry

    lax.fori_loop(0, owners, close, 0)


def collect(v, owners, ident):
    n, tp = lax.axis_size("ctx"), lax.axis_size("tp")
    rows, part = v.shape[0] // owners, v.shape[1] // tp
    dma = pltpu.SemaphoreType.DMA
    z = n if owners > 1 else 1
    return pl.pallas_call(
        functools.partial(collect_kernel, owners),
        cost_estimate=pl.CostEstimate(flops=17 * MICRO, bytes_accessed=0, transcendentals=0),
        out_shape=jax.ShapeDtypeStruct((rows, part), F32),
        in_specs=[pl.BlockSpec(memory_space=pltpu.VMEM)],
        out_specs=pl.BlockSpec(memory_space=pltpu.VMEM),
        scratch_shapes=[
            pltpu.VMEM((owners, rows, 2 * part), BF16),
            pltpu.VMEM((owners, rows, part), BF16),
            pltpu.VMEM((owners, rows, part), BF16),
            pltpu.VMEM((z, rows, part), BF16),
            pltpu.VMEM((2, z, rows, part), BF16),
        ]
        + [dma((owners,))] * 4
        + [dma((2 * z,))] * 2,
        compiler_params=pltpu.CompilerParams(
            collective_id=ident, has_side_effects=True, vmem_limit_bytes=48 << 20
        ),
    )(v)


def returns_kernel(kinds, mine, blocks, flipped, with_dots, axes, *refs):
    refs = list(refs)

    def take(count):
        return [refs.pop(0) for _ in range(count)]

    lhs_refs, own_refs, other_refs = take(kinds * mine), take(1), take(blocks - 1)
    dots_ref = take(1)[0] if with_dots else None
    sources = take(len(axes))
    out_ref = take(1)[0]
    dots_out = take(1)[0] if with_dots else None
    targets = take(len(axes))
    lhs, weights, core_out, core_in, keep, near, side_out, side_in, z_out, z_in = take(10)
    ls, ws, cs, cr, ys, yr, zs, zr = take(8)
    dots_in, ds, dr = take(3) if with_dots else (None, None, None)
    moving, more = carried(
        list(zip(axes, sources, targets)), {axis: take(2) for axis in axes}
    )
    c, n, core, side, over_core, over_side = place()
    t, tp = lax.axis_index("tp"), lax.axis_size("tp")
    rows, part = out_ref.shape
    fine = lhs_refs[0].shape[1]
    wide = out_ref.shape[1] * tp // blocks
    half_blocks = blocks // 2
    left, right = {"ctx": c - 1}, {"ctx": c + 1}

    loads = []
    for k in range(kinds):
        for e in range(mine):
            at = k * mine + e
            columns = pl.ds(at * fine, fine)
            loads.append(pltpu.make_async_copy(lhs_refs[at], lhs.at[:, columns], ls.at[at]))
            for s in range(blocks):
                source = own_refs[0] if s == 0 else other_refs[s - 1]
                source = source.at[at]
                target = weights.at[s, columns, :] if flipped else weights.at[s, :, columns]
                loads.append(pltpu.make_async_copy(source, target, ws.at[at * blocks + s]))
    for load in loads:
        load.start()
    if with_dots:
        others = []
        for far_c in range(n):
            for far_t in range(tp):
                others.append(({"ctx": far_c, "tp": far_t}, (c != far_c) | (t != far_t)))
    else:
        others = [(over_core, c >= 0), (over_side, c >= 0), (left, c > 0), (right, c < n - 1)]
    at = 0
    for axis in axes:
        count = 1 if axis == "z" else blocks - 1
        others += [] if axis == "z" else more[at : at + count]
        at += count
    signal_all(others)
    for copy in moving:
        copy.start()

    def own_rows(owner):
        return pl.ds(pl.multiple_of(owner * rows, rows), rows)

    def dots_copy(owner, far_t):
        source = dots_ref.at[:, own_rows(owner)]
        return pltpu.make_async_remote_copy(
            src_ref=source,
            dst_ref=dots_in.at[c * tp + t],
            send_sem=ds.at[owner * tp + far_t],
            recv_sem=dr.at[c * tp + t],
            device_id={"ctx": owner, "tp": far_t},
            device_id_type=MESH,
        )

    def dots_from(at):
        here = dots_in.at[at]
        return pltpu.make_async_remote_copy(
            src_ref=here,
            dst_ref=here,
            send_sem=ds.at[at],
            recv_sem=dr.at[at],
            device_id=over_core,
            device_id_type=MESH,
        )

    if with_dots:
        for owner in range(n):
            for far_t in range(tp):

                @pl.when((c != owner) | (t != far_t))
                def _():
                    dots_copy(owner, far_t).start()

        dots_in[c * tp + t] = dots_ref[:, own_rows(c)]

    for load in loads:
        load.wait()

    def owner_of(i):
        owner = 0
        for at in range(n):
            for turn, far in enumerate(sorted(range(n), key=lambda o: -abs(o - at))):
                owner = jnp.where((c == at) & (i == turn), far, owner)
        return owner

    def to_core(i):
        return remote(core_out.at[i], core_in.at[i], (cs, cr), i, over_core)

    def to_side(i):
        return remote(side_out.at[i], side_in.at[i], (ys, yr), i, over_side)

    def to_left(owner):
        return remote(z_out.at[owner], z_in.at[1, owner], (zs, zr), n + owner, left)

    def to_right(owner):
        return remote(z_out.at[owner], z_in.at[0, owner], (zs, zr), owner, right)

    def product(i, which, into):
        taken = lhs[own_rows(owner_of(i)), :]
        for j in range(half_blocks):
            w = weights[which * half_blocks + j]
            into(j, dot(taken, w) if flipped else dot_t(taken, w))

    def columns_of(j):
        return pl.ds(j * wide, wide)

    def quarter(which):
        return pl.ds(pl.multiple_of(which * part, part), part)

    def begin(i):
        def send_part(j, v):
            core_out[i, :, columns_of(j)] = v.astype(core_out.dtype)

        def keep_part(j, v):
            keep[lax.rem(i, 2), :, columns_of(j)] = v

        product(i, 1 - core, send_part)
        to_core(i).start()
        product(i, core, keep_part)

    def cross(i):
        to_core(i).wait_recv()
        slot = lax.rem(i, 2)

        def summed(which):
            return keep[slot, :, quarter(which)] + core_in[i, :, quarter(which)].astype(F32)

        side_out[i] = summed(1 - side).astype(side_out.dtype)
        to_side(i).start()
        near[slot] = summed(side)

    def finish(i):
        to_side(i).wait_recv()
        owner = owner_of(i)
        total = near[lax.rem(i, 2)] + side_in[i].astype(F32)

        @pl.when(owner > c)
        def _():
            @pl.when(c > 0)
            def _():
                to_right(owner).wait_recv()
                z_out[owner] = (total + z_in[0, owner].astype(F32)).astype(z_out.dtype)

            @pl.when(c == 0)
            def _():
                z_out[owner] = total.astype(z_out.dtype)

            to_right(owner).start()

        @pl.when(owner < c)
        def _():
            @pl.when(c < n - 1)
            def _():
                to_left(owner).wait_recv()
                z_out[owner] = (total + z_in[1, owner].astype(F32)).astype(z_out.dtype)

            @pl.when(c == n - 1)
            def _():
                z_out[owner] = total.astype(z_out.dtype)

            to_left(owner).start()

        @pl.when(owner == c)
        def _():
            out_ref[...] = total

    def step(i, carry):
        @pl.when(i < n)
        def _():
            begin(i)

        @pl.when(i > 1)
        def _():
            finish(i - 2)

        @pl.when((i > 0) & (i <= n))
        def _():
            cross(i - 1)

        return carry

    lax.fori_loop(0, n + 2, step, 0)

    @pl.when(c > 0)
    def _():
        to_right(c).wait_recv()
        out_ref[...] += z_in[0, c].astype(F32)

    @pl.when(c < n - 1)
    def _():
        to_left(c).wait_recv()
        out_ref[...] += z_in[1, c].astype(F32)

    if with_dots:
        for at in range(n * tp):

            @pl.when(c * tp + t != at)
            def _():
                dots_from(at).wait_recv()

        for at in range(n):
            dots_out[at] = sum(dots_in[at * tp + far_t] for far_t in range(tp))
        for owner in range(n):
            for far_t in range(tp):

                @pl.when((c != owner) | (t != far_t))
                def _():
                    dots_copy(owner, far_t).wait_send()

    def close(i, carry):
        to_core(i).wait_send()
        to_side(i).wait_send()
        owner = owner_of(i)

        @pl.when(owner > c)
        def _():
            to_right(owner).wait_send()

        @pl.when(owner < c)
        def _():
            to_left(owner).wait_send()

        return carry

    lax.fori_loop(0, n, close, 0)
    for copy in moving:
        copy.wait()


def returns(lhs, own, others, dots, flipped, ident, carry=()):
    n, tp = lax.axis_size("ctx"), lax.axis_size("tp")
    kinds, mine = len(lhs), len(lhs[0])
    blocks = len(others) + 1
    pack, fine = lhs[0][0].shape
    wide = own.shape[2 if flipped else 1]
    rows, part = pack // n, wide * blocks // tp
    deep = kinds * mine * fine
    dma, vmem = pltpu.SemaphoreType.DMA, pltpu.VMEM
    hbm = pl.BlockSpec(memory_space=pl.ANY)
    near = pl.BlockSpec(memory_space=pltpu.VMEM)
    operands = [v for kind in lhs for v in kind] + [own] + list(others)
    in_specs = [hbm] * len(operands)
    out_shape = [jax.ShapeDtypeStruct((rows, part), F32)]
    extra = []
    if dots is not None:
        operands.append(dots)
        in_specs.append(near)
        out_shape.append(jax.ShapeDtypeStruct((n, mine, rows), F32))
        extra = [vmem((n * tp, mine, rows), F32), dma((n * tp,)), dma((n * tp,))]
    carried_in, shapes, sems = carry_operands(carry)
    axes = [axis for axis, _ in carry]
    return pl.pallas_call(
        functools.partial(
            returns_kernel, kinds, mine, blocks, flipped, dots is not None, axes
        ),
        cost_estimate=pl.CostEstimate(flops=65 * MICRO, bytes_accessed=0, transcendentals=0),
        out_shape=out_shape + shapes,
        in_specs=in_specs + [hbm] * len(shapes),
        out_specs=[near] * len(out_shape) + [hbm] * len(shapes),
        scratch_shapes=[
            vmem((pack, deep), BF16),
            vmem((blocks, deep, wide) if flipped else (blocks, wide, deep), BF16),
            vmem((n, rows, 2 * part), BF16),
            vmem((n, rows, 2 * part), BF16),
            vmem((2, rows, 2 * part), F32),
            vmem((2, rows, part), F32),
            vmem((n, rows, part), BF16),
            vmem((n, rows, part), BF16),
            vmem((n, rows, part), BF16),
            vmem((2, n, rows, part), BF16),
            dma((kinds * mine,)),
            dma((kinds * mine * blocks,)),
        ]
        + [dma((n,))] * 4
        + [dma((2 * n,))] * 2
        + extra
        + sems,
        compiler_params=pltpu.CompilerParams(
            collective_id=ident, has_side_effects=True, vmem_limit_bytes=56 << 20
        ),
    )(*operands, *carried_in)


def mixture_kernel(blocks, tp, *refs):
    inner_refs, out_ref = refs[: -1 - blocks], refs[-1]
    weights = refs[-1 - blocks : -1]
    wide, part = weights[0].shape[2], out_ref.shape[2]
    step = min(wide, part)
    inners = [r[...] for r in inner_refs]
    for start in range(0, wide * blocks, step):
        s, here = start // wide, pl.ds(start % wide, step)
        total = sum(dot(v, weights[s][e, :, here]) for e, v in enumerate(inners))
        column = start // part
        out_ref[(column % 2) * 2 + column // 2, :, pl.ds(start % part, step)] = total.astype(BF16)


def mixture_parts(inners, weights, tp, tile=512):
    pack, fine = inners[0].shape
    mine, blocks = len(inners), len(weights)
    wide = weights[0].shape[2]
    part = wide * blocks // tp
    return pl.pallas_call(
        functools.partial(mixture_kernel, blocks, tp),
        cost_estimate=pl.CostEstimate(flops=15 * MICRO, bytes_accessed=0, transcendentals=0),
        grid=(pack // tile,),
        in_specs=[pl.BlockSpec((tile, fine), lambda i: (i, 0))] * mine
        + [pl.BlockSpec((mine, fine, wide), lambda i: (0, 0, 0))] * blocks,
        out_specs=pl.BlockSpec((tp, tile, part), lambda i: (0, i, 0)),
        out_shape=jax.ShapeDtypeStruct((tp, pack, part), BF16),
        compiler_params=pltpu.CompilerParams(vmem_limit_bytes=48 << 20),
    )(*inners, *weights)


def place_kernel(at_ref, near_ref, far_ref, *refs):
    gate_ref, up_ref, down_ref = refs[-3:]
    fine, wide = down_ref.shape

    def write(source):
        gate_ref[...] = source[0].astype(F32)
        up_ref[...] = source[1].astype(F32)
        for j in range(wide // fine):
            down_ref[:, pl.ds(j * fine, fine)] = source[2, pl.ds(j * fine, fine), :].astype(F32)

    pl.when(pl.program_id(0) == 0)(lambda: write(near_ref))
    pl.when(pl.program_id(0) == 1)(lambda: write(far_ref))


def place_grads(at, near, far, experts, held):
    _, wide, fine = near.shape
    source = pl.BlockSpec(near.shape, lambda i, at_ref: (0, 0, 0))
    gate = pl.BlockSpec((None, wide, fine), lambda i, at_ref: (at_ref[i], 0, 0))
    down = pl.BlockSpec((None, fine, wide), lambda i, at_ref: (at_ref[i], 0, 0))
    return pl.pallas_call(
        place_kernel,
        cost_estimate=pl.CostEstimate(flops=4 * MICRO, bytes_accessed=0, transcendentals=0),
        grid_spec=pltpu.PrefetchScalarGridSpec(
            num_scalar_prefetch=1,
            grid=(2,),
            in_specs=[source, source] + [pl.BlockSpec(memory_space=pl.ANY)] * len(held),
            out_specs=[gate, gate, down],
        ),
        out_shape=[jax.ShapeDtypeStruct((experts, wide, fine), F32)] * 2
        + [jax.ShapeDtypeStruct((experts, fine, wide), F32)],
        input_output_aliases={3 + i: i for i in range(len(held))},
        compiler_params=pltpu.CompilerParams(vmem_limit_bytes=32 << 20),
    )(at, near, far, *held)


def share_kernel(over_tp, x_ref, out_ref, slots, ss, sr):
    c, t = lax.axis_index("ctx"), lax.axis_index("tp")
    n, tp = lax.axis_size("ctx"), lax.axis_size("tp")
    me = c * tp + t
    everyone = [(far_c, far_t) for far_c in range(n) for far_t in range(tp)]
    signal_all(
        [({"ctx": far_c, "tp": far_t}, (c != far_c) | (t != far_t)) for far_c, far_t in everyone]
    )

    def copy(far_c, far_t):
        return pltpu.make_async_remote_copy(
            src_ref=x_ref,
            dst_ref=slots.at[me],
            send_sem=ss.at[far_c * tp + far_t],
            recv_sem=sr.at[me],
            device_id={"ctx": far_c, "tp": far_t},
            device_id_type=MESH,
        )

    for far_c, far_t in everyone:

        @pl.when((c != far_c) | (t != far_t))
        def _():
            copy(far_c, far_t).start()

    slots[me] = x_ref[...]
    for at in range(n * tp):

        @pl.when(me != at)
        def _():
            pltpu.make_async_remote_copy(
                src_ref=slots.at[at],
                dst_ref=slots.at[at],
                send_sem=ss.at[at],
                recv_sem=sr.at[at],
                device_id={"tp": lax.rem(t + 1, tp)},
                device_id_type=MESH,
            ).wait_recv()

    sums = [sum(slots[far_c * tp + far_t] for far_c in range(n)) for far_t in range(tp)]
    if over_tp:
        out_ref[...] = sum(sums)
    else:
        for far_t in range(tp):
            out_ref[far_t] = sums[far_t]
    for far_c, far_t in everyone:

        @pl.when((c != far_c) | (t != far_t))
        def _():
            copy(far_c, far_t).wait_send()


def share(v, over_tp, ident):
    n, tp = lax.axis_size("ctx"), lax.axis_size("tp")
    dma = pltpu.SemaphoreType.DMA
    near = pl.BlockSpec(memory_space=pltpu.VMEM)
    return pl.pallas_call(
        functools.partial(share_kernel, over_tp),
        cost_estimate=pl.CostEstimate(flops=8 * MICRO, bytes_accessed=0, transcendentals=0),
        out_shape=jax.ShapeDtypeStruct(v.shape if over_tp else (tp,) + v.shape, v.dtype),
        in_specs=[near],
        out_specs=near,
        scratch_shapes=[pltpu.VMEM((n * tp,) + v.shape, v.dtype)] + [dma((n * tp,))] * 2,
        compiler_params=pltpu.CompilerParams(
            collective_id=ident, has_side_effects=True, vmem_limit_bytes=32 << 20
        ),
    )(v)


def body(
    tokens,
    cotangent,
    lengths,
    routes,
    attn_gain,
    w_query,
    w_key,
    w_value,
    q_gain,
    k_gain,
    w_out,
    mlp_gain,
    w_router,
    w_gate,
    w_up,
    w_down,
):
    dp_at, ctx_at, tp_at = (lax.axis_index(a) for a in ("dp", "ctx", "tp"))
    dp_count, ctx_count, tp_count = (lax.axis_size(a) for a in ("dp", "ctx", "tp"))
    rows, width = tokens.shape
    wide = w_query.shape[0]
    local = w_query.shape[1]
    heads = local // HEAD
    experts = w_router.shape[1]
    mine = experts // ctx_count
    part = width // tp_count
    column_at = lax.rem(tp_at, 2) * 2 + tp_at // 2

    def fetch(v):
        others = [
            lax.ppermute(v, "dp", [((i + s) % dp_count, i) for i in range(dp_count)])
            for s in range(1, dp_count)
        ]
        return [v] + others

    def hand_over(blocks):
        total = blocks[0].astype(F32)
        for s in range(1, dp_count):
            pairs = [(i, (i + s) % dp_count) for i in range(dp_count)]
            total = total + lax.ppermute(blocks[s].astype(BF16), "dp", pairs).astype(F32)
        return total

    def swap(blocks):
        return [
            lax.ppermute(blocks[s], "dp", [(i, (i + s) % dp_count) for i in range(dp_count)])
            for s in range(1, dp_count)
        ]

    def add(blocks, arrived):
        return sum(v.astype(F32) for v in [blocks[0]] + arrived).astype(BF16)

    def columns(v):
        return lax.dynamic_slice_in_dim(v, column_at * part, part, v.ndim - 1)

    def block(v, s):
        return v[:, s * wide : (s + 1) * wide]

    def own_experts(w):
        return lax.dynamic_slice_in_dim(w, ctx_at * mine, mine, 0)

    small = jnp.concatenate(
        [attn_gain[None], q_gain[None], k_gain[None], mlp_gain[None], w_router.T], axis=0
    )
    small = jnp.concatenate(fetch(small), axis=1)
    gains = small[:4].astype(F32)
    router_w = small[4:]
    gain_one, gain_two = gains[0], columns(gains[3])

    def heads_gain(v):
        back = jnp.roll(v, dp_at * wide)
        return lax.dynamic_slice_in_dim(back, tp_at * local, local)

    gain_q, gain_k = heads_gain(gains[1]), heads_gain(gains[2])
    own_cols = local // ctx_count
    head_at = tp_at * local + ctx_at * own_cols

    def own_heads(w):
        return lax.dynamic_slice_in_dim(w, ctx_at * own_cols, own_cols, 1)

    def natural(v):
        return jnp.roll(v, dp_at * wide, axis=-1)

    gain_q, gain_k = lax.dynamic_slice_in_dim(natural(gains[1:3]), head_at, own_cols, 1)
    heads_w = fetch(jnp.concatenate([own_heads(w) for w in (w_query, w_key, w_value)], axis=1))
    out_w = fetch(w_out)
    weights = (w_gate, w_up, w_down)
    beside = jnp.bitwise_xor(ctx_at, 2)

    def experts_of(w, plane):
        return lax.dynamic_slice_in_dim(w, plane * mine, mine, 0)


    def both(ws, plane):
        gate, up, down = (experts_of(w, plane) for w in ws)
        return [jnp.concatenate([gate, up]), down]

    own_slices = both(weights, ctx_at)
    tokens = jnp.roll(tokens, -dp_at * wide, axis=1)

    inputs = tokens.astype(F32)
    scale_one = lax.rsqrt(jnp.mean(inputs * inputs, axis=1, keepdims=True) + EPS)
    hidden_one = columns((inputs * scale_one * gain_one).astype(BF16))
    hidden_one, own_slices = lax.optimization_barrier((hidden_one, own_slices))
    own_others = [fetch(w)[1:] for w in own_slices]
    hidden_one = spread(hidden_one, 1)
    cotangent = jnp.roll(cotangent, -dp_at * wide, axis=1)
    chosen = jnp.any(
        routes[:, :, None] == jnp.arange(experts, dtype=jnp.int32)[None, None, :], axis=1
    )
    upstream_all = jnp.concatenate(
        [
            lax.dynamic_slice_in_dim(cotangent, tp_at * part, part, 1),
            jnp.pad(chosen.astype(BF16), ((0, 0), (0, HEAD - experts))),
        ],
        axis=1,
    )
    upstream_all = lax.all_gather(upstream_all, "ctx", axis=0, tiled=True)
    raw = sum(dot(block(hidden_one, s), w) for s, w in enumerate(heads_w))
    q_raw, k_raw = raw[:, :own_cols], raw[:, own_cols : 2 * own_cols]
    values = raw[:, 2 * own_cols :].astype(BF16)
    pack = raw.shape[0]
    squares = share(
        jnp.stack([jnp.sum(q_raw * q_raw, axis=1), jnp.sum(k_raw * k_raw, axis=1)]), True, 5
    )
    squares, out_w = lax.optimization_barrier((squares, out_w))
    q_scale, k_scale = lax.rsqrt(squares / width + EPS)[:, :, None]
    q_hat, k_hat = q_raw * q_scale, k_raw * k_scale
    cosine, sine = rotation(lengths[0], 0, pack)
    mine_heads = own_cols // HEAD

    def turn(v, sine):
        return rotate(v.reshape(pack, mine_heads, HEAD), cosine, sine)

    def by_head(v):
        return v.astype(BF16).reshape(pack, mine_heads, HEAD).transpose(1, 0, 2)

    q_all, k_all = by_head(turn(q_hat * gain_q, sine)), by_head(turn(k_hat * gain_k, sine))
    v_all = by_head(values)
    attended_all, log = attend(lengths, q_all, k_all, v_all)
    attended_all, own_others[0] = lax.optimization_barrier((attended_all, own_others[0]))
    attended = to_rows((attended_all,))[0].reshape(rows, local)
    branch = jnp.concatenate([dot(attended, w).astype(BF16) for w in out_w], axis=1)
    branch, upstream_all = lax.optimization_barrier((branch, upstream_all))
    chosen_all = upstream_all[:, part : part + experts].astype(F32)
    upstream_all = lax.all_gather(upstream_all[:, :part], "tp", axis=1, tiled=True)
    branch = collect(branch, 1, 2)
    branch, late = lax.optimization_barrier((branch, weights))
    far_slices = both(late, beside)
    far_others = [fetch(w)[1:] for w in far_slices]
    inputs_c = columns(inputs)
    mixed = inputs_c + branch
    square = lax.psum(jnp.sum(mixed * mixed, axis=1), "tp")
    scale_two = lax.rsqrt(square / width + EPS)[:, None]
    normed_two = mixed * scale_two
    hidden_mine = (normed_two * gain_two).astype(BF16)
    hidden_mine, own_others[1] = lax.optimization_barrier((hidden_mine, own_others[1]))
    hidden_two = spread(hidden_mine, 3)

    tie = lax.optimization_barrier
    grads, sums, there = {}, {}, {}

    def run(e):
        far = e >= mine
        w = far_w if far else own_w
        number = e % mine
        out = expert(
            number, hidden_two, upstream_all, chosen_all, router_w, w, far, not far, [], 20 + e
        )
        grads[e] = [out[-2], out[-1]]
        return list(out[:-2])

    def start_x(e):
        grads[e][1] = swap([None] + [grads[e][1][s] for s in range(dp_count - 1)])

    def end_x(e, after):
        grads[e][1], after = tie((grads[e][1], after))
        sums[e] = add([grads[e][0]], grads[e][1])
        return after

    def start_z(e):
        there[e] = lax.ppermute(sums[e], "ctx", [(i, i ^ 1) for i in range(ctx_count)])

    def end_z(e, after):
        there[e], after = tie((there[e], after))
        return after

    own_w = [[w] + o for w, o in zip(own_slices, own_others)]
    far_w = [[w] + o for w, o in zip(far_slices, far_others)]
    parts = []
    for e in range(mine):
        parts.append(run(e))
        if e > 0:
            hidden_two = end_x(e - 1, (hidden_two, grads[e][1]))[0]
            start_z(e - 1)
        if e > 2:
            hidden_two = end_z(e - 3, hidden_two)
        start_x(e)
    mixture = mixture_parts([p[0] for p in parts], own_w[1], tp_count)
    mixture, hidden_two = tie((mixture, hidden_two))
    mixture = lax.psum_scatter(mixture, "tp", scatter_dimension=0, tiled=False)
    dots = jnp.concatenate([p[3] for p in parts], axis=1).T
    dots, hidden_two = tie((dots, hidden_two))
    expert_in, dots = returns(
        [[p[1] for p in parts], [p[2] for p in parts]],
        own_w[0][0],
        own_w[0][1:],
        dots,
        False,
        4,
    )
    for e in range(1, mine - 1):
        expert_in = end_z(e, expert_in)
    expert_in = end_x(mine - 1, expert_in)
    start_z(mine - 1)

    dots = dots.reshape(experts, rows).T
    hidden_rows = lax.dynamic_slice_in_dim(hidden_two, ctx_at * rows, rows, 0)
    route_mine = jax.nn.softmax(dot_t(hidden_rows, router_w), axis=1)
    d_logits = (
        route_mine * (dots - jnp.sum(route_mine * dots, axis=1, keepdims=True))
    ).astype(BF16)
    router_grad = t_dot(d_logits, hidden_mine)
    d_hidden_two = expert_in + dot(d_logits, columns(router_w))
    gain_two_grad = jnp.sum(d_hidden_two * normed_two, axis=0)
    pull_two = d_hidden_two * gain_two
    mean_two = lax.psum(jnp.sum(pull_two * mixed, axis=1), "tp")[:, None] / width
    d_mixed = (
        columns(cotangent).astype(F32) + scale_two * pull_two - mixed * scale_two**3 * mean_two
    )

    d_branch = join(d_mixed.astype(BF16), 7)
    d_branch = end_z(mine - 1, d_branch)
    hidden_two, d_branch = tie((hidden_two, d_branch))
    d_attended = sum(dot_t(block(d_branch, s), w) for s, w in enumerate(out_w)).astype(BF16)
    out_grad = swap([t_dot(block(d_branch, s), attended).astype(BF16) for s in range(dp_count)])
    out_mine = t_dot(block(d_branch, 0), attended)
    d_all = to_heads((d_attended,), heads)[0]
    run(mine)
    start_x(mine)
    mixture, grads[mine][0] = tie((mixture, grads[mine][0]))
    mixture = lax.psum_scatter(mixture, "ctx", scatter_dimension=0, tiled=True)
    d_all, grads[mine][0] = tie((d_all, grads[mine][0]))
    dq_all, dk_all, dv_all = attend_back(lengths, q_all, k_all, v_all, d_all, log)
    def by_token(v):
        return v.transpose(1, 0, 2).reshape(pack, own_cols)

    d_q_normed = turn(by_token(dq_all), -sine).reshape(pack, own_cols)
    d_k_normed = turn(by_token(dk_all), -sine).reshape(pack, own_cols)
    q_pull, k_pull = d_q_normed * gain_q, d_k_normed * gain_k
    totals = share(
        jnp.stack([jnp.sum(q_pull * q_raw, axis=1), jnp.sum(k_pull * k_raw, axis=1)]), True, 6
    )
    q_mean, k_mean = totals[:, :, None] / width
    d_q_raw = (q_scale * q_pull - q_raw * q_scale**3 * q_mean).astype(BF16)
    d_k_raw = (k_scale * k_pull - k_raw * k_scale**3 * k_mean).astype(BF16)
    d_raw = jnp.concatenate([d_q_raw, d_k_raw, by_token(dv_all)], axis=1)
    heads_mine = t_dot(block(hidden_one, 0), d_raw)
    heads_grads = swap([t_dot(block(hidden_one, s), d_raw).astype(BF16) for s in range(dp_count)])
    d_raw, hidden_two = tie((d_raw, hidden_two))
    for e in range(mine + 1, 2 * mine):
        run(e)
        hidden_two, d_raw = end_x(e - 1, (hidden_two, d_raw, grads[e][1]))[:2]
        start_z(e - 1)
        if e > mine + 1:
            hidden_two, d_raw = end_z(e - 2, (hidden_two, d_raw))
        start_x(e)
        if e == mine + 1:
            mixture, d_raw = tie((mixture, d_raw))
            output = lax.all_gather(mixed + mixture.astype(F32), "tp", axis=0, tiled=False)
        if e == mine + 2:
            heads_grads, output, d_raw = tie((heads_grads, output, d_raw))
            heads_grads = add([heads_mine], heads_grads)
            heads_grads = lax.all_gather(heads_grads, "ctx", axis=0, tiled=False)
        if e == mine + 3:
            out_grad, heads_grads, d_raw = tie((out_grad, heads_grads, d_raw))
            out_grad = add([out_mine], out_grad)
            out_grad = lax.psum_scatter(out_grad, "ctx", scatter_dimension=0, tiled=True)
            out_grad = lax.all_gather(out_grad, "ctx", axis=0, tiled=True)
    d_raw, far = tie((d_raw, grads[2 * mine - 1][0]))
    (d_hidden,) = returns(
        [[d_raw]],
        heads_w[0][None],
        [w[None] for w in heads_w[1:]],
        None,
        False,
        8,
    )
    d_hidden = end_z(2 * mine - 2, end_x(2 * mine - 1, d_hidden))
    start_z(2 * mine - 1)
    gain_one_grad = jnp.sum(d_hidden * inputs_c * scale_one, axis=0)
    pull_one = d_hidden * columns(gain_one)
    mean_one = lax.psum(jnp.sum(pull_one * inputs_c, axis=1), "tp")[:, None] / width
    d_inputs = d_mixed + scale_one * pull_one - inputs_c * scale_one**3 * mean_one

    def whole(every):
        every = [every[(p % 2) * 2 + p // 2] for p in range(tp_count)]
        return natural(jnp.concatenate(every, axis=1))

    output = whole(output)
    d_inputs = join(d_inputs, 10)
    gain_one_grad, d_inputs = tie((gain_one_grad, d_inputs))
    d_inputs = natural(d_inputs)
    heads_gains = lax.dynamic_update_slice_in_dim(
        jnp.zeros((2, local), F32),
        jnp.stack([jnp.sum(d_q_normed * q_hat, axis=0), jnp.sum(d_k_normed * k_hat, axis=0)]),
        ctx_at * own_cols,
        1,
    )
    small_grads = jnp.concatenate(
        [gain_one_grad[None], gain_two_grad[None], router_grad, heads_gains]
    )
    small_grads = jnp.pad(small_grads, ((0, -small_grads.shape[0] % 8), (0, 0)))
    small_grads = share(small_grads, False, 9)

    turned = [small_grads[(p % 2) * 2 + p // 2, : 2 + experts] for p in range(tp_count)]
    heads_gains = small_grads[:, 2 + experts : 4 + experts].transpose(1, 0, 2).reshape(2, width)
    small_grads = jnp.concatenate([natural(jnp.concatenate(turned, axis=1)), heads_gains])
    small_grads = hand_over(
        [small_grads if s == 0 else small_grads for s in range(dp_count)]
    )
    small_grads = lax.dynamic_slice_in_dim(small_grads, dp_at * wide, wide, 1)

    def heads_grad(i):
        v = heads_grads[:, :, i * own_cols : (i + 1) * own_cols].astype(F32)
        return v.transpose(1, 0, 2).reshape(wide, local)

    held = []
    for e in range(2 * mine - 1):
        there[e], d_hidden = tie((there[e], d_hidden))
    for e in range(2 * mine):
        plane = ctx_at if e < mine else beside
        at = plane * mine + e % mine
        other = jnp.bitwise_xor(plane, 1) * mine + e % mine
        held = place_grads(
            jnp.stack([at, other]).astype(jnp.int32), sums[e], there[e], experts, held
        )
    return (
        output,
        d_inputs,
        small_grads[0],
        heads_grad(0),
        heads_grad(1),
        heads_grad(2),
        small_grads[2 + experts],
        small_grads[3 + experts],
        out_grad.astype(F32).T,
        small_grads[1],
        small_grads[2 : 2 + experts].T,
        held[0],
        held[1],
        held[2],
    )


def solution(mesh):
    in_specs = (
        P(("dp", "ctx"), None),
        P(("dp", "ctx"), None),
        P("dp", None),
        P(("dp", "ctx"), None),
        P("dp"),
        P("dp", "tp"),
        P("dp", "tp"),
        P("dp", "tp"),
        P("dp"),
        P("dp"),
        P("tp", "dp"),
        P("dp"),
        P("dp", None),
        P(None, "dp", "tp"),
        P(None, "dp", "tp"),
        P(None, "tp", "dp"),
    )
    out_specs = (
        P(("dp", "ctx"), None),
        P(("dp", "ctx"), None),
        P("dp"),
        P("dp", "tp"),
        P("dp", "tp"),
        P("dp", "tp"),
        P("dp"),
        P("dp"),
        P("tp", "dp"),
        P("dp"),
        P("dp", None),
        P(None, "dp", "tp"),
        P(None, "dp", "tp"),
        P(None, "tp", "dp"),
    )
    return jax.shard_map(body, mesh=mesh, in_specs=in_specs, out_specs=out_specs, check_vma=False)
```

```python
import functools

import jax
import jax.numpy as jnp
from jax import lax
from jax.experimental import pallas as pl
from jax.experimental.pallas import tpu as pltpu
from jax.sharding import PartitionSpec as P

HEAD = 128
EPS = 1e-05
THETA = 10000.0
BLOCK = 256
BF16 = jnp.bfloat16
F32 = jnp.float32
MESH = pl.DeviceIdType.MESH
MICRO = 1 << 26


def dot(a, b):
    return jnp.dot(a, b, preferred_element_type=F32)


def dot_t(a, b):
    return lax.dot_general(a, b, (((1,), (1,)), ((), ())), preferred_element_type=F32)


def t_dot(a, b):
    return lax.dot_general(a, b, (((0,), (0,)), ((), ())), preferred_element_type=F32)


def rotation(row, first, rows):
    ends = jnp.cumsum(row)
    index = first + jnp.arange(rows, dtype=jnp.int32)
    before = jnp.where(index[:, None] >= ends[None, :], ends[None, :], 0)
    position = index - jnp.max(before, axis=1)
    inverse = THETA ** (-jnp.arange(0, HEAD, 2).astype(F32) / HEAD)
    angle = position.astype(F32)[:, None] * inverse[None, :]
    cosine, sine = jnp.cos(angle), jnp.sin(angle)
    return (
        jnp.concatenate([cosine, cosine], axis=1)[:, None, :],
        jnp.concatenate([-sine, sine], axis=1)[:, None, :],
    )


def rotate(v, cosine, sine):
    return v * cosine + jnp.roll(v, HEAD // 2, axis=2) * sine


def allowed_block(lengths_ref, base, rows, columns):
    index = base + lax.broadcasted_iota(jnp.int32, (rows, 1), 0)
    start = jnp.zeros((rows, 1), jnp.int32)
    end = 0
    for at in range(lengths_ref.shape[1]):
        end = end + lengths_ref[0, at]
        start = jnp.where(index >= end, end, start)
    key = lax.broadcasted_iota(jnp.int32, (rows, columns), 1)
    return (key >= start) & (key <= index)


def attend_kernel(lengths_ref, q_ref, k_ref, v_ref, out_ref, log_ref):
    scale = HEAD ** (-0.5)
    rows = q_ref.shape[0]
    for base in range(0, rows, BLOCK):
        upto = base + BLOCK
        own = pl.ds(base, BLOCK)
        keys, values = k_ref[pl.ds(0, upto), :], v_ref[pl.ds(0, upto), :]
        scores = dot_t(q_ref[own, :], keys) * scale
        scores = jnp.where(allowed_block(lengths_ref, base, BLOCK, upto), scores, -1e30)
        top = jnp.max(scores, axis=1, keepdims=True)
        weights = jnp.exp(scores - top)
        total = jnp.sum(weights, axis=1, keepdims=True)
        probs = (weights * (1.0 / total)).astype(BF16)
        out_ref[own, :] = dot(probs, values).astype(BF16)
        log_ref[own, :] = top + jnp.log(total)


def attend(lengths, q, k, v):
    heads, rows, _ = q.shape
    spec = pl.BlockSpec((None, rows, HEAD), lambda h: (h, 0, 0))
    column = pl.BlockSpec((None, rows, 1), lambda h: (h, 0, 0))
    return pl.pallas_call(
        attend_kernel,
        cost_estimate=pl.CostEstimate(flops=7 * MICRO, bytes_accessed=0, transcendentals=0),
        grid=(heads,),
        out_shape=(
            jax.ShapeDtypeStruct((heads, rows, HEAD), BF16),
            jax.ShapeDtypeStruct((heads, rows, 1), F32),
        ),
        in_specs=[pl.BlockSpec(memory_space=pltpu.SMEM), spec, spec, spec],
        out_specs=(spec, column),
        compiler_params=pltpu.CompilerParams(vmem_limit_bytes=48 << 20),
    )(lengths, q, k, v)


def attend_back_kernel(
    lengths_ref, q_ref, k_ref, v_ref, d_ref, log_ref, dq_ref, dk_ref, dv_ref, dk_sum, dv_sum
):
    scale = HEAD ** (-0.5)
    rows = q_ref.shape[0]
    dk_sum[...] = jnp.zeros_like(dk_sum)
    dv_sum[...] = jnp.zeros_like(dv_sum)
    for base in range(0, rows, BLOCK):
        upto = base + BLOCK
        own, seen = pl.ds(base, BLOCK), pl.ds(0, upto)
        q, d = q_ref[own, :], d_ref[own, :]
        keys, values = k_ref[seen, :], v_ref[seen, :]
        scores = dot_t(q, keys) * scale - log_ref[own, :]
        probs = jnp.where(
            allowed_block(lengths_ref, base, BLOCK, upto), jnp.exp(scores), 0.0
        )
        d_probs = dot_t(d, values)
        delta = jnp.sum(probs * d_probs, axis=1, keepdims=True)
        d_raw = (probs * (d_probs - delta) * scale).astype(BF16)
        dq_ref[own, :] = dot(d_raw, keys).astype(dq_ref.dtype)
        dk_sum[seen, :] += t_dot(d_raw, q)
        dv_sum[seen, :] += t_dot(probs.astype(BF16), d)
    dk_ref[...] = dk_sum[...].astype(dk_ref.dtype)
    dv_ref[...] = dv_sum[...].astype(dv_ref.dtype)


def attend_back(lengths, q, k, v, d, log):
    heads, rows, _ = q.shape
    spec = pl.BlockSpec((None, rows, HEAD), lambda h: (h, 0, 0))
    column = pl.BlockSpec((None, rows, 1), lambda h: (h, 0, 0))
    return pl.pallas_call(
        attend_back_kernel,
        cost_estimate=pl.CostEstimate(flops=10 * MICRO, bytes_accessed=0, transcendentals=0),
        grid=(heads,),
        out_shape=(jax.ShapeDtypeStruct((heads, rows, HEAD), F32),) * 2
        + (jax.ShapeDtypeStruct((heads, rows, HEAD), BF16),),
        in_specs=[pl.BlockSpec(memory_space=pltpu.SMEM), spec, spec, spec, spec, column],
        out_specs=(spec,) * 3,
        scratch_shapes=[pltpu.VMEM((rows, HEAD), F32)] * 2,
        compiler_params=pltpu.CompilerParams(vmem_limit_bytes=48 << 20),
    )(lengths, q, k, v, d, log)


def to_heads(parts, heads):
    count = lax.axis_size("ctx")
    rows = parts[0].shape[0]
    stacked = jnp.stack([p.reshape(rows, count, heads // count, HEAD) for p in parts])
    sent = stacked.transpose(2, 0, 3, 1, 4)
    got = lax.all_to_all(sent, "ctx", 0, 0, tiled=True)
    return got.transpose(1, 2, 0, 3, 4).reshape(len(parts), heads // count, count * rows, HEAD)


def to_rows(parts):
    count = lax.axis_size("ctx")
    mine, pack, _ = parts[0].shape
    stacked = jnp.stack([p.reshape(mine, count, pack // count, HEAD) for p in parts])
    sent = stacked.transpose(2, 0, 1, 3, 4)
    got = lax.all_to_all(sent, "ctx", 0, 0, tiled=True)
    turned = got.transpose(1, 3, 0, 2, 4)
    return turned.reshape(len(parts), pack // count, count * mine, HEAD)


def carried(axes, sources, targets, sems):
    d, count = lax.axis_index("dp"), lax.axis_size("dp")
    copies = []
    for i, axis in enumerate(axes):
        pair = (sems[2 * i], sems[2 * i + 1])
        if axis == "z":
            partner = {"ctx": jnp.bitwise_xor(lax.axis_index("ctx"), 1)}
            copies.append(remote(sources[i], targets[i], pair, 0, partner))
            continue
        for s in range(1, count):
            source = sources[i].at[s - 1] if axis == "x" else sources[i]
            partner = {"dp": lax.rem(d + (s if axis == "x" else count - s), count)}
            copies.append(remote(source, targets[i].at[s - 1], pair, s - 1, partner))
    partners = []
    if any(axis != "z" for axis in axes):
        partners = [({"dp": lax.rem(d + s, count)}, d >= 0) for s in range(1, count)]
    return copies, partners


def beside():
    return [({"ctx": jnp.bitwise_xor(lax.axis_index("ctx"), 1)}, lax.axis_index("ctx") >= 0)]


def carry_operands(carry):
    dma, count = pltpu.SemaphoreType.DMA, lax.axis_size("dp")
    shapes, sems = [], []
    for axis, v in carry:
        shape = (count - 1,) + v.shape if axis == "w" else v.shape
        shapes.append(jax.ShapeDtypeStruct(shape, v.dtype))
        sems += [dma((1 if axis == "z" else count - 1,))] * 2
    return [v for _, v in carry], shapes, sems


def expert_kernel(blocks, number, far, mine, full, axes, *refs):
    refs = list(refs)

    def take(count):
        return [refs.pop(0) for _ in range(count)]

    hidden_ref, up_ref, chosen_ref, router_ref = take(4)
    gate_w, up_w, down_w = take(blocks), take(blocks), take(blocks)
    sources = take(len(axes))
    if full:
        inner_ref, dgate_ref, dup_ref, dots_ref = take(4)
    near_ref, others_ref = take(2)
    targets = take(len(axes))
    gate_sum, up_sum, down_sum = take(3)
    sems = take(2 * len(axes))
    turn, last = pl.program_id(0), pl.num_programs(0) - 1
    wide = gate_w[0].shape[0]

    def transfers():
        return carried(axes, sources, targets, sems)

    if axes:

        @pl.when(turn == 0)
        def _():
            copies, partners = transfers()
            signal_all(partners + (beside() if "z" in axes else []))
            for copy in copies:
                copy.start()

    hidden, upstream = hidden_ref[...], up_ref[...]

    def over(v, ws, f):
        return sum(f(v[:, s * wide : (s + 1) * wide], w[...]) for s, w in enumerate(ws))

    gate, up = over(hidden, gate_w, dot), over(hidden, up_w, dot)
    pulled = over(upstream, down_w, dot_t)
    logits = dot_t(hidden, router_ref[...])
    odds = jnp.exp(logits - jnp.max(logits, axis=1, keepdims=True))
    probs = odds / jnp.sum(odds, axis=1, keepdims=True) * chosen_ref[...]
    plane = lax.axis_index("ctx")
    if far:
        plane = jnp.bitwise_xor(plane, 2)
    named = lax.broadcasted_iota(jnp.int32, probs.shape, 1) == plane * mine + number
    weight = jnp.sum(jnp.where(named, probs, 0.0), axis=1, keepdims=True)
    sigma = jax.nn.sigmoid(gate)
    active = gate * sigma
    inner = (active * up).astype(BF16).astype(F32)
    if full:
        dots = jnp.sum(inner * pulled, axis=1, keepdims=True)
        dots_ref[...] = jnp.where(weight > 0.0, dots, 0.0)
    inner = (weight * inner).astype(BF16)
    pulled = weight * pulled
    d_gate = (pulled * up * sigma * (1.0 + gate * (1.0 - sigma))).astype(BF16)
    d_up = (pulled * active).astype(BF16)
    if full:
        inner_ref[...], dgate_ref[...], dup_ref[...] = inner, d_gate, d_up

    @pl.when(turn == 0)
    def _():
        gate_sum[...] = t_dot(d_gate, hidden)
        up_sum[...] = t_dot(d_up, hidden)
        down_sum[...] = t_dot(inner, upstream)

    @pl.when(turn > 0)
    def _():
        gate_sum[...] += t_dot(d_gate, hidden)
        up_sum[...] += t_dot(d_up, hidden)
        down_sum[...] += t_dot(inner, upstream)

    @pl.when(turn == last)
    def _():
        fine = down_sum.shape[0]
        for s in range(blocks):
            target = near_ref if s == 0 else others_ref.at[s - 1]
            own = pl.ds(s * wide, wide)
            target[0] = gate_sum[:, own].T.astype(BF16)
            target[1] = up_sum[:, own].T.astype(BF16)
            for j in range(wide // fine):
                target[2, pl.ds(j * fine, fine), :] = down_sum[
                    :, pl.ds(s * wide + j * fine, fine)
                ].astype(BF16)
        if axes:
            for copy in transfers()[0]:
                copy.wait()


def expert(e, hidden, upstream, chosen, router, weights, far, full, carry, ident, tile=512):
    gate_w, up_w, down_w = weights
    blocks = len(gate_w)
    pack, width = hidden.shape
    mine, fine, wide = down_w[0].shape
    first = up_w[0].shape[0] - mine
    operands, shapes, sems = carry_operands(carry)
    hbm = pl.BlockSpec(memory_space=pl.ANY)

    def token(n):
        return pl.BlockSpec((tile, n), lambda i: (i, 0))

    def weight(first, *shape):
        return pl.BlockSpec((None,) + shape, lambda i: (first + e, 0, 0))

    near = pl.BlockSpec((3, wide, fine), lambda i: (0, 0, 0))
    others = pl.BlockSpec((blocks - 1, 3, wide, fine), lambda i: (0, 0, 0, 0))
    out_specs, out_shape = [near, others], [
        jax.ShapeDtypeStruct((3, wide, fine), BF16),
        jax.ShapeDtypeStruct((blocks - 1, 3, wide, fine), BF16),
    ]
    if full:
        out_specs = [token(fine)] * 3 + [token(1)] + out_specs
        out_shape = (
            [jax.ShapeDtypeStruct((pack, fine), BF16)] * 3
            + [jax.ShapeDtypeStruct((pack, 1), F32)]
            + out_shape
        )
    remote_params = dict(collective_id=ident, has_side_effects=True) if carry else {}
    return pl.pallas_call(
        functools.partial(expert_kernel, blocks, e, far, mine, full, [axis for axis, _ in carry]),
        cost_estimate=pl.CostEstimate(flops=27 * MICRO, bytes_accessed=0, transcendentals=0),
        grid=(pack // tile,),
        in_specs=[token(width), token(width), token(chosen.shape[1])]
        + [pl.BlockSpec(router.shape, lambda i: (0, 0))]
        + [weight(0, wide, fine)] * blocks
        + [weight(first, wide, fine)] * blocks
        + [weight(0, fine, wide)] * blocks
        + [hbm] * len(operands),
        out_specs=out_specs + [hbm] * len(shapes),
        out_shape=out_shape + shapes,
        scratch_shapes=[pltpu.VMEM((fine, width), F32)] * 3 + sems,
        compiler_params=pltpu.CompilerParams(vmem_limit_bytes=56 << 20, **remote_params),
    )(hidden, upstream, chosen, router, *gate_w, *up_w, *down_w, *operands)


def signal_all(partners):
    barrier = pltpu.get_barrier_semaphore()
    count = 0
    for device, there in partners:

        @pl.when(there)
        def _():
            pl.semaphore_signal(barrier, inc=1, device_id=device, device_id_type=MESH)

        count = count + jnp.where(there, 1, 0)
    pl.semaphore_wait(barrier, count)


def place():
    c, t = lax.axis_index("ctx"), lax.axis_index("tp")
    core, side = lax.rem(t, 2), t // 2
    over_core = {"tp": t + 1 - 2 * core}
    over_side = {"tp": t + 2 - 4 * side}
    return c, lax.axis_size("ctx"), core, side, over_core, over_side


def remote(source, target, sems, at, device):
    send, recv = sems
    return pltpu.make_async_remote_copy(
        src_ref=source,
        dst_ref=target,
        send_sem=send.at[at],
        recv_sem=recv.at[at],
        device_id=device,
        device_id_type=MESH,
    )


def spread_kernel(axes, x_ref, *refs):
    count = len(axes)
    sources, out_ref, targets = refs[:count], refs[count], refs[count + 1 : 2 * count + 1]
    local, zs, zr, ys, yr, cs, cr = refs[2 * count + 1 : 2 * count + 8]
    moving, more = carried(axes, sources, targets, refs[2 * count + 8 :])
    c, n, core, side, over_core, over_side = place()
    rows, part = x_ref.shape
    left, right = {"ctx": c - 1}, {"ctx": c + 1}
    signal_all(
        [(left, c > 0), (right, c < n - 1), (over_core, c >= 0), (over_side, c >= 0)] + more
    )
    for copy in moving:
        copy.start()
    mine = core * 2 + side
    other = core * 2 + 1 - side

    def tile(owner, column):
        return out_ref.at[
            pl.ds(pl.multiple_of(owner * rows, rows), rows),
            pl.ds(pl.multiple_of(column * part, part), part),
        ]

    def along(owner, source, target, at):
        return remote(source, tile(owner, mine), (zs, zr), at, target)

    keep = pltpu.make_async_copy(x_ref, tile(c, mine), local)
    keep.start()

    @pl.when(c > 0)
    def _():
        along(c, x_ref, left, n + c).start()

    @pl.when(c < n - 1)
    def _():
        along(c, x_ref, right, c).start()

    def to_side(owner, source):
        return remote(source, tile(owner, mine), (ys, yr), owner, over_side)

    def to_core(owner, column, source, which):
        return remote(source, tile(owner, column), (cs, cr), which * n + owner, over_core)

    to_side(c, x_ref).start()
    to_core(c, mine, x_ref, 0).start()

    def from_side(owner):
        here = tile(owner, other)
        remote(here, here, (ys, yr), owner, over_side).wait_recv()
        to_core(owner, other, here, 1).start()

    from_side(c)
    for far in range(1, n):
        for sign, there, onward, more in (
            (-1, c - far >= 0, right, c < n - 1),
            (1, c + far < n, left, c > 0),
        ):
            owner = c + sign * far
            slot = owner if sign < 0 else n + owner

            @pl.when(there)
            def _():
                here = tile(owner, mine)
                along(owner, here, onward, slot).wait_recv()

                @pl.when(more)
                def _():
                    along(owner, here, onward, slot).start()

                to_side(owner, here).start()
                to_core(owner, mine, here, 0).start()

        for sign, there in ((-1, c - far >= 0), (1, c + far < n)):

            @pl.when(there)
            def _():
                from_side(c + sign * far)

    keep.wait()

    @pl.when(c > 0)
    def _():
        along(c, x_ref, left, n + c).wait_send()

    @pl.when(c < n - 1)
    def _():
        along(c, x_ref, right, c).wait_send()

    for far in range(1, n):
        for sign, there, onward, more in (
            (-1, c - far >= 0, right, c < n - 1),
            (1, c + far < n, left, c > 0),
        ):
            owner = c + sign * far

            @pl.when(there & more)
            def _():
                here = tile(owner, mine)
                along(owner, here, onward, owner if sign < 0 else n + owner).wait_send()

    for owner in range(n):
        to_side(owner, tile(owner, mine)).wait_send()
        to_core(owner, mine, tile(owner, mine), 0).wait_send()
        to_core(owner, other, tile(owner, other), 1).wait_send()
        for which, column in ((0, (1 - core) * 2 + side), (1, (1 - core) * 2 + 1 - side)):
            here = tile(owner, column)
            remote(here, here, (cs, cr), which * n + owner, over_core).wait_recv()
    for copy in moving:
        copy.wait()


def spread(v, ident, carry=()):
    operands, shapes, sems = carry_operands(carry)
    hbm = pl.BlockSpec(memory_space=pl.ANY)
    n, tp = lax.axis_size("ctx"), lax.axis_size("tp")
    rows, part = v.shape
    dma = pltpu.SemaphoreType.DMA
    return pl.pallas_call(
        functools.partial(spread_kernel, [axis for axis, _ in carry]),
        cost_estimate=pl.CostEstimate(flops=60 * MICRO, bytes_accessed=0, transcendentals=0),
        out_shape=[jax.ShapeDtypeStruct((n * rows, tp * part), v.dtype)] + shapes,
        in_specs=[hbm] * (1 + len(shapes)),
        out_specs=[hbm] * (1 + len(shapes)),
        scratch_shapes=[dma]
        + [dma((2 * n,))] * 2
        + [dma((n,))] * 2
        + [dma((2 * n,))] * 2
        + sems,
        compiler_params=pltpu.CompilerParams(collective_id=ident, has_side_effects=True),
    )(v, *operands)


def join_kernel(x_ref, out_ref, local, ss, sr):
    c, n, core, side, over_core, over_side = place()
    rows, part = x_ref.shape
    signal_all([(over_core, c >= 0), (over_side, c >= 0)])
    mine, other = core * 2 + side, core * 2 + 1 - side

    def tile(column):
        return out_ref.at[:, pl.ds(pl.multiple_of(column * part, part), part)]

    keep = pltpu.make_async_copy(x_ref, tile(mine), local)
    keep.start()
    first = remote(x_ref, tile(mine), (ss, sr), 0, over_side)
    first.start()
    second = remote(x_ref, tile(mine), (ss, sr), 1, over_core)
    second.start()
    first.wait_recv()
    third = remote(tile(other), tile(other), (ss, sr), 2, over_core)
    third.start()
    keep.wait()
    first.wait_send()
    second.wait()
    third.wait()


def join(v, ident):
    tp = lax.axis_size("tp")
    rows, part = v.shape
    dma = pltpu.SemaphoreType.DMA
    return pl.pallas_call(
        join_kernel,
        cost_estimate=pl.CostEstimate(flops=25 * MICRO, bytes_accessed=0, transcendentals=0),
        out_shape=jax.ShapeDtypeStruct((rows, tp * part), v.dtype),
        in_specs=[pl.BlockSpec(memory_space=pl.ANY)],
        out_specs=pl.BlockSpec(memory_space=pl.ANY),
        scratch_shapes=[dma] + [dma((3,))] * 2,
        compiler_params=pltpu.CompilerParams(collective_id=ident, has_side_effects=True),
    )(v)


def collect_kernel(
    owners, x_ref, out_ref, core_in, side_out, side_in, z_out, z_in, cs, cr, ys, yr, zs, zr
):
    c, n, core, side, over_core, over_side = place()
    rows, part = out_ref.shape
    left, right = {"ctx": c - 1}, {"ctx": c + 1}
    partners = [(over_core, c >= 0), (over_side, c >= 0)]
    if owners > 1:
        partners += [(left, c > 0), (right, c < n - 1)]
    signal_all(partners)

    def owner_of(i):
        if owners == 1:
            return 0
        owner = 0
        for at in range(n):
            for turn, far in enumerate(sorted(range(n), key=lambda o: -abs(o - at))):
                owner = jnp.where((c == at) & (i == turn), far, owner)
        return owner

    def own_rows(owner):
        return pl.ds(pl.multiple_of(owner * rows, rows), rows)

    def half(which):
        return pl.ds(pl.multiple_of(which * 2 * part, 2 * part), 2 * part)

    def quarter(which):
        return pl.ds(pl.multiple_of((core * 2 + which) * part, part), part)

    def to_core(i):
        source = x_ref.at[own_rows(owner_of(i)), half(1 - core)]
        return remote(source, core_in.at[i], (cs, cr), i, over_core)

    def to_side(i):
        return remote(side_out.at[i], side_in.at[i], (ys, yr), i, over_side)

    def to_left(owner):
        return remote(z_out.at[owner], z_in.at[1, owner], (zs, zr), n + owner, left)

    def to_right(owner):
        return remote(z_out.at[owner], z_in.at[0, owner], (zs, zr), owner, right)

    def from_core(i, which):
        local = x_ref[own_rows(owner_of(i)), quarter(which)].astype(F32)
        near = core_in[i, :, pl.ds(pl.multiple_of(which * part, part), part)]
        return local + near.astype(F32)

    for i in range(owners):
        to_core(i).start()

    def finish(i):
        to_side(i).wait_recv()
        owner = owner_of(i)
        total = from_core(i, side) + side_in[i].astype(F32)
        if owners == 1:
            out_ref[...] = total
            return

        @pl.when(owner > c)
        def _():
            @pl.when(c > 0)
            def _():
                to_right(owner).wait_recv()
                z_out[owner] = (total + z_in[0, owner].astype(F32)).astype(z_out.dtype)

            @pl.when(c == 0)
            def _():
                z_out[owner] = total.astype(z_out.dtype)

            to_right(owner).start()

        @pl.when(owner < c)
        def _():
            @pl.when(c < n - 1)
            def _():
                to_left(owner).wait_recv()
                z_out[owner] = (total + z_in[1, owner].astype(F32)).astype(z_out.dtype)

            @pl.when(c == n - 1)
            def _():
                z_out[owner] = total.astype(z_out.dtype)

            to_left(owner).start()

        @pl.when(owner == c)
        def _():
            out_ref[...] = total

    def step(i, carry):
        @pl.when(i < owners)
        def _():
            to_core(i).wait_recv()
            side_out[i] = from_core(i, 1 - side).astype(side_out.dtype)
            to_side(i).start()

        @pl.when(i > 0)
        def _():
            finish(i - 1)

        return carry

    lax.fori_loop(0, owners + 1, step, 0)

    if owners > 1:

        @pl.when(c > 0)
        def _():
            to_right(c).wait_recv()
            out_ref[...] += z_in[0, c].astype(F32)

        @pl.when(c < n - 1)
        def _():
            to_left(c).wait_recv()
            out_ref[...] += z_in[1, c].astype(F32)

    def close(i, carry):
        to_core(i).wait_send()
        to_side(i).wait_send()
        if owners > 1:
            owner = owner_of(i)

            @pl.when(owner > c)
            def _():
                to_right(owner).wait_send()

            @pl.when(owner < c)
            def _():
                to_left(owner).wait_send()

        return carry

    lax.fori_loop(0, owners, close, 0)


def collect(v, owners, ident):
    n, tp = lax.axis_size("ctx"), lax.axis_size("tp")
    rows, part = v.shape[0] // owners, v.shape[1] // tp
    dma = pltpu.SemaphoreType.DMA
    z = n if owners > 1 else 1
    return pl.pallas_call(
        functools.partial(collect_kernel, owners),
        cost_estimate=pl.CostEstimate(flops=17 * MICRO, bytes_accessed=0, transcendentals=0),
        out_shape=jax.ShapeDtypeStruct((rows, part), F32),
        in_specs=[pl.BlockSpec(memory_space=pltpu.VMEM)],
        out_specs=pl.BlockSpec(memory_space=pltpu.VMEM),
        scratch_shapes=[
            pltpu.VMEM((owners, rows, 2 * part), BF16),
            pltpu.VMEM((owners, rows, part), BF16),
            pltpu.VMEM((owners, rows, part), BF16),
            pltpu.VMEM((z, rows, part), BF16),
            pltpu.VMEM((2, z, rows, part), BF16),
        ]
        + [dma((owners,))] * 4
        + [dma((2 * z,))] * 2,
        compiler_params=pltpu.CompilerParams(
            collective_id=ident, has_side_effects=True, vmem_limit_bytes=48 << 20
        ),
    )(v)


def returns_kernel(kinds, mine, blocks, flipped, with_dots, axes, *refs):
    refs = list(refs)

    def take(count):
        return [refs.pop(0) for _ in range(count)]

    lhs_refs, weight_refs = take(kinds * mine), take(kinds * blocks)
    dots_ref = take(1)[0] if with_dots else None
    sources = take(len(axes))
    out_ref = take(1)[0]
    dots_out = take(1)[0] if with_dots else None
    targets = take(len(axes))
    lhs, weights, core_out, core_in, keep, near, side_out, side_in, z_out, z_in = take(10)
    ls, ws, cs, cr, ys, yr, zs, zr = take(8)
    dots_in, ds, dr = take(3) if with_dots else (None, None, None)
    moving, more = carried(axes, sources, targets, take(2 * len(axes)))
    c, n, core, side, over_core, over_side = place()
    t, tp = lax.axis_index("tp"), lax.axis_size("tp")
    rows, part = out_ref.shape
    fine = lhs_refs[0].shape[1]
    wide = out_ref.shape[1] * tp // blocks
    half_blocks = blocks // 2
    left, right = {"ctx": c - 1}, {"ctx": c + 1}

    loads = []
    for k in range(kinds):
        for e in range(mine):
            at = k * mine + e
            columns = pl.ds(at * fine, fine)
            loads.append(pltpu.make_async_copy(lhs_refs[at], lhs.at[:, columns], ls.at[at]))
            for s in range(blocks):
                source = weight_refs[k * blocks + s].at[e]
                target = weights.at[s, columns, :] if flipped else weights.at[s, :, columns]
                loads.append(pltpu.make_async_copy(source, target, ws.at[at * blocks + s]))
    for load in loads:
        load.start()
    if with_dots:
        others = []
        for far_c in range(n):
            for far_t in range(tp):
                others.append(({"ctx": far_c, "tp": far_t}, (c != far_c) | (t != far_t)))
    else:
        others = [(over_core, c >= 0), (over_side, c >= 0), (left, c > 0), (right, c < n - 1)]
    others += more
    signal_all(others)
    for copy in moving:
        copy.start()

    def own_rows(owner):
        return pl.ds(pl.multiple_of(owner * rows, rows), rows)

    def dots_copy(owner, far_t):
        source = dots_ref.at[:, own_rows(owner)]
        return pltpu.make_async_remote_copy(
            src_ref=source,
            dst_ref=dots_in.at[c * tp + t],
            send_sem=ds.at[owner * tp + far_t],
            recv_sem=dr.at[c * tp + t],
            device_id={"ctx": owner, "tp": far_t},
            device_id_type=MESH,
        )

    def dots_from(at):
        here = dots_in.at[at]
        return pltpu.make_async_remote_copy(
            src_ref=here,
            dst_ref=here,
            send_sem=ds.at[at],
            recv_sem=dr.at[at],
            device_id=over_core,
            device_id_type=MESH,
        )

    if with_dots:
        for owner in range(n):
            for far_t in range(tp):

                @pl.when((c != owner) | (t != far_t))
                def _():
                    dots_copy(owner, far_t).start()

        dots_in[c * tp + t] = dots_ref[:, own_rows(c)]

    for load in loads:
        load.wait()

    def owner_of(i):
        owner = 0
        for at in range(n):
            for turn, far in enumerate(sorted(range(n), key=lambda o: -abs(o - at))):
                owner = jnp.where((c == at) & (i == turn), far, owner)
        return owner

    def to_core(i):
        return remote(core_out.at[i], core_in.at[i], (cs, cr), i, over_core)

    def to_side(i):
        return remote(side_out.at[i], side_in.at[i], (ys, yr), i, over_side)

    def to_left(owner):
        return remote(z_out.at[owner], z_in.at[1, owner], (zs, zr), n + owner, left)

    def to_right(owner):
        return remote(z_out.at[owner], z_in.at[0, owner], (zs, zr), owner, right)

    def product(i, which, into):
        taken = lhs[own_rows(owner_of(i)), :]
        for j in range(half_blocks):
            w = weights[which * half_blocks + j]
            into(j, dot(taken, w) if flipped else dot_t(taken, w))

    def columns_of(j):
        return pl.ds(j * wide, wide)

    def quarter(which):
        return pl.ds(pl.multiple_of(which * part, part), part)

    def begin(i):
        def send_part(j, v):
            core_out[i, :, columns_of(j)] = v.astype(core_out.dtype)

        def keep_part(j, v):
            keep[lax.rem(i, 2), :, columns_of(j)] = v

        product(i, 1 - core, send_part)
        to_core(i).start()
        product(i, core, keep_part)

    def cross(i):
        to_core(i).wait_recv()
        slot = lax.rem(i, 2)

        def summed(which):
            return keep[slot, :, quarter(which)] + core_in[i, :, quarter(which)].astype(F32)

        side_out[i] = summed(1 - side).astype(side_out.dtype)
        to_side(i).start()
        near[slot] = summed(side)

    def finish(i):
        to_side(i).wait_recv()
        owner = owner_of(i)
        total = near[lax.rem(i, 2)] + side_in[i].astype(F32)

        @pl.when(owner > c)
        def _():
            @pl.when(c > 0)
            def _():
                to_right(owner).wait_recv()
                z_out[owner] = (total + z_in[0, owner].astype(F32)).astype(z_out.dtype)

            @pl.when(c == 0)
            def _():
                z_out[owner] = total.astype(z_out.dtype)

            to_right(owner).start()

        @pl.when(owner < c)
        def _():
            @pl.when(c < n - 1)
            def _():
                to_left(owner).wait_recv()
                z_out[owner] = (total + z_in[1, owner].astype(F32)).astype(z_out.dtype)

            @pl.when(c == n - 1)
            def _():
                z_out[owner] = total.astype(z_out.dtype)

            to_left(owner).start()

        @pl.when(owner == c)
        def _():
            out_ref[...] = total

    def step(i, carry):
        @pl.when(i < n)
        def _():
            begin(i)

        @pl.when(i > 1)
        def _():
            finish(i - 2)

        @pl.when((i > 0) & (i <= n))
        def _():
            cross(i - 1)

        return carry

    lax.fori_loop(0, n + 2, step, 0)

    @pl.when(c > 0)
    def _():
        to_right(c).wait_recv()
        out_ref[...] += z_in[0, c].astype(F32)

    @pl.when(c < n - 1)
    def _():
        to_left(c).wait_recv()
        out_ref[...] += z_in[1, c].astype(F32)

    if with_dots:
        for at in range(n * tp):

            @pl.when(c * tp + t != at)
            def _():
                dots_from(at).wait_recv()

        for at in range(n):
            dots_out[at] = sum(dots_in[at * tp + far_t] for far_t in range(tp))
        for owner in range(n):
            for far_t in range(tp):

                @pl.when((c != owner) | (t != far_t))
                def _():
                    dots_copy(owner, far_t).wait_send()

    def close(i, carry):
        to_core(i).wait_send()
        to_side(i).wait_send()
        owner = owner_of(i)

        @pl.when(owner > c)
        def _():
            to_right(owner).wait_send()

        @pl.when(owner < c)
        def _():
            to_left(owner).wait_send()

        return carry

    lax.fori_loop(0, n, close, 0)
    for copy in moving:
        copy.wait()


def returns(lhs, weights, dots, flipped, ident, carry=()):
    n, tp = lax.axis_size("ctx"), lax.axis_size("tp")
    kinds, mine = len(lhs), len(lhs[0])
    blocks = len(weights[0])
    pack, fine = lhs[0][0].shape
    wide = weights[0][0].shape[2 if flipped else 1]
    rows, part = pack // n, wide * blocks // tp
    deep = kinds * mine * fine
    dma, vmem = pltpu.SemaphoreType.DMA, pltpu.VMEM
    hbm = pl.BlockSpec(memory_space=pl.ANY)
    near = pl.BlockSpec(memory_space=pltpu.VMEM)
    operands = [v for kind in lhs for v in kind] + [w for kind in weights for w in kind]
    in_specs = [hbm] * len(operands)
    out_shape = [jax.ShapeDtypeStruct((rows, part), F32)]
    extra = []
    if dots is not None:
        operands.append(dots)
        in_specs.append(near)
        out_shape.append(jax.ShapeDtypeStruct((n, mine, rows), F32))
        extra = [vmem((n * tp, mine, rows), F32), dma((n * tp,)), dma((n * tp,))]
    carried_in, shapes, sems = carry_operands(carry)
    axes = [axis for axis, _ in carry]
    return pl.pallas_call(
        functools.partial(
            returns_kernel, kinds, mine, blocks, flipped, dots is not None, axes
        ),
        cost_estimate=pl.CostEstimate(flops=65 * MICRO, bytes_accessed=0, transcendentals=0),
        out_shape=out_shape + shapes,
        in_specs=in_specs + [hbm] * len(shapes),
        out_specs=[near] * len(out_shape) + [hbm] * len(shapes),
        scratch_shapes=[
            vmem((pack, deep), BF16),
            vmem((blocks, deep, wide) if flipped else (blocks, wide, deep), BF16),
            vmem((n, rows, 2 * part), BF16),
            vmem((n, rows, 2 * part), BF16),
            vmem((2, rows, 2 * part), F32),
            vmem((2, rows, part), F32),
            vmem((n, rows, part), BF16),
            vmem((n, rows, part), BF16),
            vmem((n, rows, part), BF16),
            vmem((2, n, rows, part), BF16),
            dma((kinds * mine,)),
            dma((kinds * mine * blocks,)),
        ]
        + [dma((n,))] * 4
        + [dma((2 * n,))] * 2
        + extra
        + sems,
        compiler_params=pltpu.CompilerParams(
            collective_id=ident, has_side_effects=True, vmem_limit_bytes=56 << 20
        ),
    )(*operands, *carried_in)


def mixture_kernel(blocks, tp, *refs):
    inner_refs, out_ref = refs[: -1 - blocks], refs[-1]
    weights = refs[-1 - blocks : -1]
    wide, part = weights[0].shape[2], out_ref.shape[2]
    step = min(wide, part)
    inners = [r[...] for r in inner_refs]
    for start in range(0, wide * blocks, step):
        s, here = start // wide, pl.ds(start % wide, step)
        total = sum(dot(v, weights[s][e, :, here]) for e, v in enumerate(inners))
        column = start // part
        out_ref[(column % 2) * 2 + column // 2, :, pl.ds(start % part, step)] = total.astype(BF16)


def mixture_parts(inners, weights, tp, tile=512):
    pack, fine = inners[0].shape
    mine, blocks = len(inners), len(weights)
    wide = weights[0].shape[2]
    part = wide * blocks // tp
    return pl.pallas_call(
        functools.partial(mixture_kernel, blocks, tp),
        cost_estimate=pl.CostEstimate(flops=15 * MICRO, bytes_accessed=0, transcendentals=0),
        grid=(pack // tile,),
        in_specs=[pl.BlockSpec((tile, fine), lambda i: (i, 0))] * mine
        + [pl.BlockSpec((mine, fine, wide), lambda i: (0, 0, 0))] * blocks,
        out_specs=pl.BlockSpec((tp, tile, part), lambda i: (0, i, 0)),
        out_shape=jax.ShapeDtypeStruct((tp, pack, part), BF16),
        compiler_params=pltpu.CompilerParams(vmem_limit_bytes=48 << 20),
    )(*inners, *weights)


def place_kernel(at_ref, near_ref, far_ref, *refs):
    gate_ref, up_ref, down_ref = refs[-3:]
    fine, wide = down_ref.shape

    def write(source):
        gate_ref[...] = source[0].astype(F32)
        up_ref[...] = source[1].astype(F32)
        for j in range(wide // fine):
            down_ref[:, pl.ds(j * fine, fine)] = source[2, pl.ds(j * fine, fine), :].astype(F32)

    pl.when(pl.program_id(0) == 0)(lambda: write(near_ref))
    pl.when(pl.program_id(0) == 1)(lambda: write(far_ref))


def place_grads(at, near, far, experts, held):
    _, wide, fine = near.shape
    source = pl.BlockSpec(near.shape, lambda i, at_ref: (0, 0, 0))
    gate = pl.BlockSpec((None, wide, fine), lambda i, at_ref: (at_ref[i], 0, 0))
    down = pl.BlockSpec((None, fine, wide), lambda i, at_ref: (at_ref[i], 0, 0))
    return pl.pallas_call(
        place_kernel,
        cost_estimate=pl.CostEstimate(flops=4 * MICRO, bytes_accessed=0, transcendentals=0),
        grid_spec=pltpu.PrefetchScalarGridSpec(
            num_scalar_prefetch=1,
            grid=(2,),
            in_specs=[source, source] + [pl.BlockSpec(memory_space=pl.ANY)] * len(held),
            out_specs=[gate, gate, down],
        ),
        out_shape=[jax.ShapeDtypeStruct((experts, wide, fine), F32)] * 2
        + [jax.ShapeDtypeStruct((experts, fine, wide), F32)],
        input_output_aliases={3 + i: i for i in range(len(held))},
        compiler_params=pltpu.CompilerParams(vmem_limit_bytes=32 << 20),
    )(at, near, far, *held)


def share_kernel(over_tp, x_ref, out_ref, slots, ss, sr):
    c, t = lax.axis_index("ctx"), lax.axis_index("tp")
    n, tp = lax.axis_size("ctx"), lax.axis_size("tp")
    me = c * tp + t
    everyone = [(far_c, far_t) for far_c in range(n) for far_t in range(tp)]
    signal_all(
        [({"ctx": far_c, "tp": far_t}, (c != far_c) | (t != far_t)) for far_c, far_t in everyone]
    )

    def copy(far_c, far_t):
        return pltpu.make_async_remote_copy(
            src_ref=x_ref,
            dst_ref=slots.at[me],
            send_sem=ss.at[far_c * tp + far_t],
            recv_sem=sr.at[me],
            device_id={"ctx": far_c, "tp": far_t},
            device_id_type=MESH,
        )

    for far_c, far_t in everyone:

        @pl.when((c != far_c) | (t != far_t))
        def _():
            copy(far_c, far_t).start()

    slots[me] = x_ref[...]
    for at in range(n * tp):

        @pl.when(me != at)
        def _():
            pltpu.make_async_remote_copy(
                src_ref=slots.at[at],
                dst_ref=slots.at[at],
                send_sem=ss.at[at],
                recv_sem=sr.at[at],
                device_id={"tp": lax.rem(t + 1, tp)},
                device_id_type=MESH,
            ).wait_recv()

    sums = [sum(slots[far_c * tp + far_t] for far_c in range(n)) for far_t in range(tp)]
    if over_tp:
        out_ref[...] = sum(sums)
    else:
        for far_t in range(tp):
            out_ref[far_t] = sums[far_t]
    for far_c, far_t in everyone:

        @pl.when((c != far_c) | (t != far_t))
        def _():
            copy(far_c, far_t).wait_send()


def share(v, over_tp, ident):
    n, tp = lax.axis_size("ctx"), lax.axis_size("tp")
    dma = pltpu.SemaphoreType.DMA
    near = pl.BlockSpec(memory_space=pltpu.VMEM)
    return pl.pallas_call(
        functools.partial(share_kernel, over_tp),
        cost_estimate=pl.CostEstimate(flops=8 * MICRO, bytes_accessed=0, transcendentals=0),
        out_shape=jax.ShapeDtypeStruct(v.shape if over_tp else (tp,) + v.shape, v.dtype),
        in_specs=[near],
        out_specs=near,
        scratch_shapes=[pltpu.VMEM((n * tp,) + v.shape, v.dtype)] + [dma((n * tp,))] * 2,
        compiler_params=pltpu.CompilerParams(
            collective_id=ident, has_side_effects=True, vmem_limit_bytes=32 << 20
        ),
    )(v)


def body(
    tokens,
    cotangent,
    lengths,
    routes,
    attn_gain,
    w_query,
    w_key,
    w_value,
    q_gain,
    k_gain,
    w_out,
    mlp_gain,
    w_router,
    w_gate,
    w_up,
    w_down,
):
    dp_at, ctx_at, tp_at = (lax.axis_index(a) for a in ("dp", "ctx", "tp"))
    dp_count, ctx_count, tp_count = (lax.axis_size(a) for a in ("dp", "ctx", "tp"))
    rows, width = tokens.shape
    wide = w_query.shape[0]
    local = w_query.shape[1]
    heads = local // HEAD
    experts = w_router.shape[1]
    mine = experts // ctx_count
    part = width // tp_count
    column_at = lax.rem(tp_at, 2) * 2 + tp_at // 2

    def fetch(v):
        others = [
            lax.ppermute(v, "dp", [((i + s) % dp_count, i) for i in range(dp_count)])
            for s in range(1, dp_count)
        ]
        return [v] + others

    def hand_over(blocks):
        total = blocks[0].astype(F32)
        for s in range(1, dp_count):
            pairs = [(i, (i + s) % dp_count) for i in range(dp_count)]
            total = total + lax.ppermute(blocks[s].astype(BF16), "dp", pairs).astype(F32)
        return total

    def swap(blocks):
        return [
            lax.ppermute(blocks[s], "dp", [(i, (i + s) % dp_count) for i in range(dp_count)])
            for s in range(1, dp_count)
        ]

    def add(blocks, arrived):
        return sum(v.astype(F32) for v in [blocks[0]] + arrived).astype(BF16)

    def columns(v):
        return lax.dynamic_slice_in_dim(v, column_at * part, part, v.ndim - 1)

    def block(v, s):
        return v[:, s * wide : (s + 1) * wide]

    def own_experts(w):
        return lax.dynamic_slice_in_dim(w, ctx_at * mine, mine, 0)

    small = jnp.concatenate(
        [attn_gain[None], q_gain[None], k_gain[None], mlp_gain[None], w_router.T], axis=0
    )
    small = jnp.concatenate(fetch(small), axis=1)
    gains = small[:4].astype(F32)
    router_w = small[4:]
    gain_one, gain_two = gains[0], columns(gains[3])

    def heads_gain(v):
        back = jnp.roll(v, dp_at * wide)
        return lax.dynamic_slice_in_dim(back, tp_at * local, local)

    gain_q, gain_k = heads_gain(gains[1]), heads_gain(gains[2])
    own_cols = local // ctx_count
    head_at = tp_at * local + ctx_at * own_cols

    def own_heads(w):
        return lax.dynamic_slice_in_dim(w, ctx_at * own_cols, own_cols, 1)

    def natural(v):
        return jnp.roll(v, dp_at * wide, axis=-1)

    gain_q, gain_k = lax.dynamic_slice_in_dim(natural(gains[1:3]), head_at, own_cols, 1)
    heads_w = jnp.concatenate([own_heads(w) for w in (w_query, w_key, w_value)], axis=1)
    weights = (w_gate, w_up, w_down)
    beside_at = jnp.bitwise_xor(ctx_at, 2)

    def experts_of(w, plane):
        return lax.dynamic_slice_in_dim(w, plane * mine, mine, 0)


    own_slices = [experts_of(w, ctx_at) for w in weights]
    tokens = jnp.roll(tokens, -dp_at * wide, axis=1)

    inputs = tokens.astype(F32)
    scale_one = lax.rsqrt(jnp.mean(inputs * inputs, axis=1, keepdims=True) + EPS)
    hidden_one = columns((inputs * scale_one * gain_one).astype(BF16))
    hidden_one, own_slices = lax.optimization_barrier((hidden_one, own_slices))
    hidden_one, *got = spread(
        hidden_one, 1, [("w", heads_w), ("w", w_out), ("w", own_slices[0])]
    )

    def listed(w, received):
        return [w] + [received[s] for s in range(dp_count - 1)]

    heads_w, out_w = listed(heads_w, got[0]), listed(w_out, got[1])
    own_w = [listed(own_slices[0], got[2]), fetch(own_slices[1]), None]
    if wide % part == 0:

        def upstream_columns(at):
            return lax.dynamic_slice_in_dim(
                cotangent, lax.rem(at * part + dp_at * wide, width), part, 1
            )

    else:
        turned_cotangent = jnp.roll(cotangent, -dp_at * wide, axis=1)

        def upstream_columns(at):
            return lax.dynamic_slice_in_dim(turned_cotangent, at * part, part, 1)

    chosen = jnp.any(
        routes[:, :, None] == jnp.arange(experts, dtype=jnp.int32)[None, None, :], axis=1
    )
    upstream_all = jnp.concatenate([upstream_columns(tp_at), chosen.astype(BF16).T])
    upstream_all = lax.all_gather(upstream_all, "ctx", axis=0, tiled=False)
    chosen_all = upstream_all[:, rows:].transpose(0, 2, 1).reshape(-1, experts).astype(F32)
    hidden_one, upstream_all = lax.optimization_barrier((hidden_one, upstream_all))
    upstream_all = lax.all_gather(upstream_all[:, :rows].reshape(-1, part), "tp", axis=1, tiled=True)
    raw = sum(dot(block(hidden_one, s), w) for s, w in enumerate(heads_w))
    q_raw, k_raw = raw[:, :own_cols], raw[:, own_cols : 2 * own_cols]
    values = raw[:, 2 * own_cols :].astype(BF16)
    pack = raw.shape[0]
    squares = share(
        jnp.stack([jnp.sum(q_raw * q_raw, axis=1), jnp.sum(k_raw * k_raw, axis=1)]), True, 5
    )
    q_scale, k_scale = lax.rsqrt(squares / width + EPS)[:, :, None]
    q_hat, k_hat = q_raw * q_scale, k_raw * k_scale
    cosine, sine = rotation(lengths[0], 0, pack)
    mine_heads = own_cols // HEAD

    def turn(v, sine):
        return rotate(v.reshape(pack, mine_heads, HEAD), cosine, sine)

    def by_head(v):
        return v.astype(BF16).reshape(pack, mine_heads, HEAD).transpose(1, 0, 2)

    q_all, k_all = by_head(turn(q_hat * gain_q, sine)), by_head(turn(k_hat * gain_k, sine))
    v_all = by_head(values)
    attended_all, log = attend(lengths, q_all, k_all, v_all)
    attended = to_rows((attended_all,))[0].reshape(rows, local)
    branch = jnp.concatenate([dot(attended, w).astype(BF16) for w in out_w], axis=1)
    branch, own_w[1] = lax.optimization_barrier((branch, own_w[1]))
    branch = collect(branch, 1, 2)
    inputs_c = columns(inputs)
    mixed = inputs_c + branch
    square = lax.psum(jnp.sum(mixed * mixed, axis=1), "tp")
    scale_two = lax.rsqrt(square / width + EPS)[:, None]
    normed_two = mixed * scale_two
    hidden_mine = (normed_two * gain_two).astype(BF16)
    hidden_two, got = spread(hidden_mine, 3, [("w", own_slices[2])])
    own_w[2] = listed(own_slices[2], got)
    hidden_two, late = lax.optimization_barrier((hidden_two, weights))
    far_slices = [experts_of(w, beside_at) for w in late]
    far_slices = [jnp.concatenate(far_slices[:2]), far_slices[2]]

    tie = lax.optimization_barrier
    grads, sums, there = {}, {}, {}

    def run(e):
        far = e >= mine
        w = far_w if far else own_w
        number = e % mine
        out = expert(
            number, hidden_two, upstream_all, chosen_all, router_w, w, far, not far, [], 20 + e
        )
        grads[e] = [out[-2], out[-1]]
        return list(out[:-2])

    def start_x(e):
        grads[e][1] = swap([None] + [grads[e][1][s] for s in range(dp_count - 1)])

    def end_x(e, after):
        grads[e][1], after = tie((grads[e][1], after))
        sums[e] = add([grads[e][0]], grads[e][1])
        return after

    def start_z(e):
        there[e] = lax.ppermute(sums[e], "ctx", [(i, i ^ 1) for i in range(ctx_count)])

    def end_z(e, after):
        there[e], after = tie((there[e], after))
        return after

    parts = []
    for e in range(mine):
        parts.append(run(e))
        if e > 0:
            hidden_two = end_x(e - 1, (hidden_two, grads[e][1]))[0]
            start_z(e - 1)
        if e > 2:
            hidden_two = end_z(e - 3, hidden_two)
        start_x(e)
    mixture = mixture_parts([p[0] for p in parts], own_w[2], tp_count)
    mixture, hidden_two = tie((mixture, hidden_two))
    mixture = lax.psum_scatter(mixture, "tp", scatter_dimension=0, tiled=False)
    dots = jnp.concatenate([p[3] for p in parts], axis=1).T
    dots, hidden_two = tie((dots, hidden_two))
    far_both = fetch(far_slices[0])
    expert_in, dots = returns(
        [[p[1] for p in parts], [p[2] for p in parts]],
        own_w[:2],
        dots,
        False,
        4,
    )
    far_both, expert_in, late_down = tie((far_both, expert_in, far_slices[1]))
    far_down = fetch(late_down)
    for e in range(1, mine - 1):
        expert_in = end_z(e, expert_in)
    expert_in, mixture = tie((expert_in, mixture))
    mixture = lax.psum_scatter(mixture, "ctx", scatter_dimension=0, tiled=True)

    dots = dots.reshape(experts, rows).T
    hidden_rows = lax.dynamic_slice_in_dim(hidden_two, ctx_at * rows, rows, 0)
    route_mine = jax.nn.softmax(dot_t(hidden_rows, router_w), axis=1)
    d_logits = (
        route_mine * (dots - jnp.sum(route_mine * dots, axis=1, keepdims=True))
    ).astype(BF16)
    router_grad = t_dot(d_logits, hidden_mine)
    d_hidden_two = expert_in + dot(d_logits, columns(router_w))
    gain_two_grad = jnp.sum(d_hidden_two * normed_two, axis=0)
    pull_two = d_hidden_two * gain_two
    mean_two = lax.psum(jnp.sum(pull_two * mixed, axis=1), "tp")[:, None] / width
    mean_two = end_x(mine - 1, mean_two)
    sums[mine - 1], mean_two = tie((sums[mine - 1], mean_two))
    start_z(mine - 1)
    d_mixed = (
        upstream_columns(column_at).astype(F32) + scale_two * pull_two - mixed * scale_two**3 * mean_two
    )

    d_branch = join(d_mixed.astype(BF16), 7)
    d_branch = end_z(mine - 1, d_branch)
    hidden_two, d_branch, far_down, mixture = tie((hidden_two, d_branch, far_down, mixture))
    output = lax.all_gather(mixed + mixture.astype(F32), "tp", axis=0, tiled=False)
    far_w = [far_both, far_both, far_down]
    d_attended = sum(dot_t(block(d_branch, s), w) for s, w in enumerate(out_w)).astype(BF16)
    out_grad = swap([t_dot(block(d_branch, s), attended).astype(BF16) for s in range(dp_count)])
    out_mine = t_dot(block(d_branch, 0), attended)
    d_all = to_heads((d_attended,), heads)[0]
    run(mine)
    start_x(mine)
    d_all, grads[mine][0], out_grad, output = tie((d_all, grads[mine][0], out_grad, output))
    out_grad = add([out_mine], out_grad)
    out_grad = lax.psum_scatter(out_grad, "ctx", scatter_dimension=0, tiled=True)
    dq_all, dk_all, dv_all = attend_back(lengths, q_all, k_all, v_all, d_all, log)
    def by_token(v):
        return v.transpose(1, 0, 2).reshape(pack, own_cols)

    d_q_normed = turn(by_token(dq_all), -sine).reshape(pack, own_cols)
    d_k_normed = turn(by_token(dk_all), -sine).reshape(pack, own_cols)
    q_pull, k_pull = d_q_normed * gain_q, d_k_normed * gain_k
    totals = share(
        jnp.stack([jnp.sum(q_pull * q_raw, axis=1), jnp.sum(k_pull * k_raw, axis=1)]), True, 6
    )
    q_mean, k_mean = totals[:, :, None] / width
    d_q_raw = (q_scale * q_pull - q_raw * q_scale**3 * q_mean).astype(BF16)
    d_k_raw = (k_scale * k_pull - k_raw * k_scale**3 * k_mean).astype(BF16)
    d_raw = jnp.concatenate([d_q_raw, d_k_raw, by_token(dv_all)], axis=1)
    heads_mine = t_dot(block(hidden_one, 0), d_raw)
    heads_grads = [t_dot(block(hidden_one, s), d_raw).astype(BF16) for s in range(dp_count)]
    heads_mine, heads_grads, d_raw, hidden_two, out_grad = tie(
        (heads_mine, heads_grads, d_raw, hidden_two, out_grad)
    )
    out_grad = lax.all_gather(out_grad, "ctx", axis=0, tiled=True)
    held = []

    def put(e):
        nonlocal held
        plane = ctx_at if e < mine else beside_at
        at = plane * mine + e % mine
        other = jnp.bitwise_xor(plane, 1) * mine + e % mine
        held = place_grads(
            jnp.stack([at, other]).astype(jnp.int32), sums[e], there[e], experts, held
        )

    for e in range(mine + 1, 2 * mine):
        run(e)
        if e > mine + 1:
            for i in range(2 * (e - mine - 2), 2 * (e - mine - 1)):
                there[i], grads[e] = tie((there[i], grads[e]))
                put(i)
        step = (hidden_two, d_raw, grads[e], held)
        if e > mine + 1:
            step = end_z(e - 2, step)
        step = end_x(e - 1, step)
        if e == mine + 1:
            out_grad, step = tie((out_grad, step))
        sums[e - 1], step = tie((sums[e - 1], step))
        hidden_two, d_raw, grads[e], held = step
        start_z(e - 1)
        if e < 2 * mine - 1:
            start_x(e)
    heads_grads, grads[2 * mine - 1] = tie((heads_grads, grads[2 * mine - 1]))
    start_x(2 * mine - 1)
    heads_grads = swap(heads_grads)
    (d_hidden,) = returns(
        [[d_raw]],
        [[w[None] for w in heads_w]],
        None,
        False,
        8,
    )
    d_hidden = end_z(2 * mine - 2, end_x(2 * mine - 1, d_hidden))
    heads_grads, out_grad, d_hidden = tie((heads_grads, out_grad, d_hidden))
    gain_one_grad = jnp.sum(d_hidden * inputs_c * scale_one, axis=0)
    heads_gains = lax.dynamic_update_slice_in_dim(
        jnp.zeros((2, local), F32),
        jnp.stack([jnp.sum(d_q_normed * q_hat, axis=0), jnp.sum(d_k_normed * k_hat, axis=0)]),
        ctx_at * own_cols,
        1,
    )
    small_grads = jnp.concatenate(
        [gain_one_grad[None], gain_two_grad[None], router_grad, heads_gains]
    )
    small_grads = jnp.pad(small_grads, ((0, -small_grads.shape[0] % 8), (0, 0)))
    small_grads = share(small_grads, False, 9)

    d_hidden, small_grads, heads_grads, sums[2 * mine - 1] = tie(
        (d_hidden, small_grads, heads_grads, sums[2 * mine - 1])
    )
    start_z(2 * mine - 1)
    heads_grads = add([heads_mine], heads_grads)
    heads_grads = lax.all_gather(heads_grads, "ctx", axis=0, tiled=False)
    pull_one = d_hidden * columns(gain_one)
    mean_one = lax.psum(jnp.sum(pull_one * inputs_c, axis=1), "tp")[:, None] / width
    d_inputs = d_mixed + scale_one * pull_one - inputs_c * scale_one**3 * mean_one

    def whole(every):
        every = [every[(p % 2) * 2 + p // 2] for p in range(tp_count)]
        return natural(jnp.concatenate(every, axis=1))

    output = whole(output)
    d_inputs = join(d_inputs, 10)
    d_inputs = natural(d_inputs)
    turned = [small_grads[(p % 2) * 2 + p // 2, : 2 + experts] for p in range(tp_count)]
    heads_gains = small_grads[:, 2 + experts : 4 + experts].transpose(1, 0, 2).reshape(2, width)
    small_grads = jnp.concatenate([natural(jnp.concatenate(turned, axis=1)), heads_gains])
    small_grads = hand_over(
        [small_grads if s == 0 else small_grads for s in range(dp_count)]
    )
    small_grads = lax.dynamic_slice_in_dim(small_grads, dp_at * wide, wide, 1)

    def heads_grad(i):
        v = heads_grads[:, :, i * own_cols : (i + 1) * own_cols].astype(F32)
        return v.transpose(1, 0, 2).reshape(wide, local)

    for e in range(mine, 2 * mine - 1):
        there[e], d_hidden = tie((there[e], d_hidden))
    for e in range(mine, 2 * mine):
        put(e)
    return (
        output,
        d_inputs,
        small_grads[0],
        heads_grad(0),
        heads_grad(1),
        heads_grad(2),
        small_grads[2 + experts],
        small_grads[3 + experts],
        out_grad.astype(F32).T,
        small_grads[1],
        small_grads[2 : 2 + experts].T,
        held[0],
        held[1],
        held[2],
    )


def solution(mesh):
    in_specs = (
        P(("dp", "ctx"), None),
        P(("dp", "ctx"), None),
        P("dp", None),
        P(("dp", "ctx"), None),
        P("dp"),
        P("dp", "tp"),
        P("dp", "tp"),
        P("dp", "tp"),
        P("dp"),
        P("dp"),
        P("tp", "dp"),
        P("dp"),
        P("dp", None),
        P(None, "dp", "tp"),
        P(None, "dp", "tp"),
        P(None, "tp", "dp"),
    )
    out_specs = (
        P(("dp", "ctx"), None),
        P(("dp", "ctx"), None),
        P("dp"),
        P("dp", "tp"),
        P("dp", "tp"),
        P("dp", "tp"),
        P("dp"),
        P("dp"),
        P("tp", "dp"),
        P("dp"),
        P("dp", None),
        P(None, "dp", "tp"),
        P(None, "dp", "tp"),
        P(None, "tp", "dp"),
    )
    return jax.shard_map(body, mesh=mesh, in_specs=in_specs, out_specs=out_specs, check_vma=False)
```

```python
import functools

import jax
import jax.numpy as jnp
from jax import lax
from jax.experimental import pallas as pl
from jax.experimental.pallas import tpu as pltpu
from jax.sharding import PartitionSpec as P

HEAD = 128
EPS = 1e-05
THETA = 10000.0
BLOCK = 256
BF16 = jnp.bfloat16
F32 = jnp.float32
MESH = pl.DeviceIdType.MESH
MICRO = 1 << 26


def dot(a, b):
    return jnp.dot(a, b, preferred_element_type=F32)


def dot_t(a, b):
    return lax.dot_general(a, b, (((1,), (1,)), ((), ())), preferred_element_type=F32)


def t_dot(a, b):
    return lax.dot_general(a, b, (((0,), (0,)), ((), ())), preferred_element_type=F32)


def rotation(row, first, rows):
    ends = jnp.cumsum(row)
    index = first + jnp.arange(rows, dtype=jnp.int32)
    before = jnp.where(index[:, None] >= ends[None, :], ends[None, :], 0)
    position = index - jnp.max(before, axis=1)
    inverse = THETA ** (-jnp.arange(0, HEAD, 2).astype(F32) / HEAD)
    angle = position.astype(F32)[:, None] * inverse[None, :]
    cosine, sine = jnp.cos(angle), jnp.sin(angle)
    return (
        jnp.concatenate([cosine, cosine], axis=1)[:, None, :],
        jnp.concatenate([-sine, sine], axis=1)[:, None, :],
    )


def rotate(v, cosine, sine):
    return v * cosine + jnp.roll(v, HEAD // 2, axis=2) * sine


def allowed_block(lengths_ref, base, rows, columns):
    index = base + lax.broadcasted_iota(jnp.int32, (rows, 1), 0)
    start = jnp.zeros((rows, 1), jnp.int32)
    end = 0
    for at in range(lengths_ref.shape[1]):
        end = end + lengths_ref[0, at]
        start = jnp.where(index >= end, end, start)
    key = lax.broadcasted_iota(jnp.int32, (rows, columns), 1)
    return (key >= start) & (key <= index)


def attend_kernel(lengths_ref, q_ref, k_ref, v_ref, out_ref, log_ref):
    scale = HEAD ** (-0.5)
    rows = q_ref.shape[0]
    for base in range(0, rows, BLOCK):
        upto = base + BLOCK
        own = pl.ds(base, BLOCK)
        keys, values = k_ref[pl.ds(0, upto), :], v_ref[pl.ds(0, upto), :]
        scores = dot_t(q_ref[own, :], keys) * scale
        scores = jnp.where(allowed_block(lengths_ref, base, BLOCK, upto), scores, -1e30)
        top = jnp.max(scores, axis=1, keepdims=True)
        weights = jnp.exp(scores - top)
        total = jnp.sum(weights, axis=1, keepdims=True)
        probs = (weights * (1.0 / total)).astype(BF16)
        out_ref[own, :] = dot(probs, values).astype(BF16)
        log_ref[own, :] = top + jnp.log(total)


def attend(lengths, q, k, v):
    heads, rows, _ = q.shape
    spec = pl.BlockSpec((None, rows, HEAD), lambda h: (h, 0, 0))
    column = pl.BlockSpec((None, rows, 1), lambda h: (h, 0, 0))
    return pl.pallas_call(
        attend_kernel,
        cost_estimate=pl.CostEstimate(flops=7 * MICRO, bytes_accessed=0, transcendentals=0),
        grid=(heads,),
        out_shape=(
            jax.ShapeDtypeStruct((heads, rows, HEAD), BF16),
            jax.ShapeDtypeStruct((heads, rows, 1), F32),
        ),
        in_specs=[pl.BlockSpec(memory_space=pltpu.SMEM), spec, spec, spec],
        out_specs=(spec, column),
        compiler_params=pltpu.CompilerParams(vmem_limit_bytes=48 << 20),
    )(lengths, q, k, v)


def attend_back_kernel(
    lengths_ref, q_ref, k_ref, v_ref, d_ref, log_ref, dq_ref, dk_ref, dv_ref, dk_sum, dv_sum
):
    scale = HEAD ** (-0.5)
    rows = q_ref.shape[0]
    dk_sum[...] = jnp.zeros_like(dk_sum)
    dv_sum[...] = jnp.zeros_like(dv_sum)
    for base in range(0, rows, BLOCK):
        upto = base + BLOCK
        own, seen = pl.ds(base, BLOCK), pl.ds(0, upto)
        q, d = q_ref[own, :], d_ref[own, :]
        keys, values = k_ref[seen, :], v_ref[seen, :]
        scores = dot_t(q, keys) * scale - log_ref[own, :]
        probs = jnp.where(
            allowed_block(lengths_ref, base, BLOCK, upto), jnp.exp(scores), 0.0
        )
        d_probs = dot_t(d, values)
        delta = jnp.sum(probs * d_probs, axis=1, keepdims=True)
        d_raw = (probs * (d_probs - delta) * scale).astype(BF16)
        dq_ref[own, :] = dot(d_raw, keys).astype(dq_ref.dtype)
        dk_sum[seen, :] += t_dot(d_raw, q)
        dv_sum[seen, :] += t_dot(probs.astype(BF16), d)
    dk_ref[...] = dk_sum[...].astype(dk_ref.dtype)
    dv_ref[...] = dv_sum[...].astype(dv_ref.dtype)


def attend_back(lengths, q, k, v, d, log):
    heads, rows, _ = q.shape
    spec = pl.BlockSpec((None, rows, HEAD), lambda h: (h, 0, 0))
    column = pl.BlockSpec((None, rows, 1), lambda h: (h, 0, 0))
    return pl.pallas_call(
        attend_back_kernel,
        cost_estimate=pl.CostEstimate(flops=10 * MICRO, bytes_accessed=0, transcendentals=0),
        grid=(heads,),
        out_shape=(jax.ShapeDtypeStruct((heads, rows, HEAD), F32),) * 2
        + (jax.ShapeDtypeStruct((heads, rows, HEAD), BF16),),
        in_specs=[pl.BlockSpec(memory_space=pltpu.SMEM), spec, spec, spec, spec, column],
        out_specs=(spec,) * 3,
        scratch_shapes=[pltpu.VMEM((rows, HEAD), F32)] * 2,
        compiler_params=pltpu.CompilerParams(vmem_limit_bytes=48 << 20),
    )(lengths, q, k, v, d, log)


def to_heads(parts, heads):
    count = lax.axis_size("ctx")
    rows = parts[0].shape[0]
    stacked = jnp.stack([p.reshape(rows, count, heads // count, HEAD) for p in parts])
    sent = stacked.transpose(2, 0, 3, 1, 4)
    got = lax.all_to_all(sent, "ctx", 0, 0, tiled=True)
    return got.transpose(1, 2, 0, 3, 4).reshape(len(parts), heads // count, count * rows, HEAD)


def to_rows(parts):
    count = lax.axis_size("ctx")
    mine, pack, _ = parts[0].shape
    stacked = jnp.stack([p.reshape(mine, count, pack // count, HEAD) for p in parts])
    sent = stacked.transpose(2, 0, 1, 3, 4)
    got = lax.all_to_all(sent, "ctx", 0, 0, tiled=True)
    turned = got.transpose(1, 3, 0, 2, 4)
    return turned.reshape(len(parts), pack // count, count * mine, HEAD)


def carried(axes, sources, targets, sems):
    d, count = lax.axis_index("dp"), lax.axis_size("dp")
    copies = []
    for i, axis in enumerate(axes):
        pair = (sems[2 * i], sems[2 * i + 1])
        if axis == "z":
            partner = {"ctx": jnp.bitwise_xor(lax.axis_index("ctx"), 1)}
            copies.append(remote(sources[i], targets[i], pair, 0, partner))
            continue
        for s in range(1, count):
            source = sources[i].at[s - 1] if axis == "x" else sources[i]
            partner = {"dp": lax.rem(d + (s if axis == "x" else count - s), count)}
            copies.append(remote(source, targets[i].at[s - 1], pair, s - 1, partner))
    partners = []
    if any(axis != "z" for axis in axes):
        partners = [({"dp": lax.rem(d + s, count)}, d >= 0) for s in range(1, count)]
    return copies, partners


def beside():
    return [({"ctx": jnp.bitwise_xor(lax.axis_index("ctx"), 1)}, lax.axis_index("ctx") >= 0)]


def carry_operands(carry):
    dma, count = pltpu.SemaphoreType.DMA, lax.axis_size("dp")
    shapes, sems = [], []
    for axis, v in carry:
        shape = (count - 1,) + v.shape if axis == "w" else v.shape
        shapes.append(jax.ShapeDtypeStruct(shape, v.dtype))
        sems += [dma((1 if axis == "z" else count - 1,))] * 2
    return [v for _, v in carry], shapes, sems


def expert_kernel(blocks, number, far, mine, full, axes, *refs):
    refs = list(refs)

    def take(count):
        return [refs.pop(0) for _ in range(count)]

    hidden_ref, up_ref, chosen_ref, router_ref = take(4)
    gate_w, up_w, down_w = take(blocks), take(blocks), take(blocks)
    sources = take(len(axes))
    if full:
        inner_ref, dgate_ref, dup_ref, dots_ref = take(4)
    near_ref, others_ref = take(2)
    targets = take(len(axes))
    gate_sum, up_sum, down_sum = take(3)
    sems = take(2 * len(axes))
    turn, last = pl.program_id(0), pl.num_programs(0) - 1
    wide = gate_w[0].shape[0]

    def transfers():
        return carried(axes, sources, targets, sems)

    if axes:

        @pl.when(turn == 0)
        def _():
            copies, partners = transfers()
            signal_all(partners + (beside() if "z" in axes else []))
            for copy in copies:
                copy.start()

    hidden, upstream = hidden_ref[...], up_ref[...]

    def over(v, ws, f):
        return sum(f(v[:, s * wide : (s + 1) * wide], w[...]) for s, w in enumerate(ws))

    gate, up = over(hidden, gate_w, dot), over(hidden, up_w, dot)
    pulled = over(upstream, down_w, dot_t)
    logits = dot_t(hidden, router_ref[...])
    odds = jnp.exp(logits - jnp.max(logits, axis=1, keepdims=True))
    probs = odds / jnp.sum(odds, axis=1, keepdims=True) * chosen_ref[...]
    plane = lax.axis_index("ctx")
    if far:
        plane = jnp.bitwise_xor(plane, 2)
    named = lax.broadcasted_iota(jnp.int32, probs.shape, 1) == plane * mine + number
    weight = jnp.sum(jnp.where(named, probs, 0.0), axis=1, keepdims=True)
    sigma = jax.nn.sigmoid(gate)
    active = gate * sigma
    inner = (active * up).astype(BF16).astype(F32)
    if full:
        dots = jnp.sum(inner * pulled, axis=1, keepdims=True)
        dots_ref[...] = jnp.where(weight > 0.0, dots, 0.0)
    inner = (weight * inner).astype(BF16)
    pulled = weight * pulled
    d_gate = (pulled * up * sigma * (1.0 + gate * (1.0 - sigma))).astype(BF16)
    d_up = (pulled * active).astype(BF16)
    if full:
        inner_ref[...], dgate_ref[...], dup_ref[...] = inner, d_gate, d_up

    @pl.when(turn == 0)
    def _():
        gate_sum[...] = t_dot(d_gate, hidden)
        up_sum[...] = t_dot(d_up, hidden)
        down_sum[...] = t_dot(inner, upstream)

    @pl.when(turn > 0)
    def _():
        gate_sum[...] += t_dot(d_gate, hidden)
        up_sum[...] += t_dot(d_up, hidden)
        down_sum[...] += t_dot(inner, upstream)

    @pl.when(turn == last)
    def _():
        fine = down_sum.shape[0]
        for s in range(blocks):
            target = near_ref if s == 0 else others_ref.at[s - 1]
            own = pl.ds(s * wide, wide)
            target[0] = gate_sum[:, own].T.astype(BF16)
            target[1] = up_sum[:, own].T.astype(BF16)
            for j in range(wide // fine):
                target[2, pl.ds(j * fine, fine), :] = down_sum[
                    :, pl.ds(s * wide + j * fine, fine)
                ].astype(BF16)
        if axes:
            for copy in transfers()[0]:
                copy.wait()


def expert(e, hidden, upstream, chosen, router, weights, far, full, carry, ident, tile=512):
    gate_w, up_w, down_w = weights
    blocks = len(gate_w)
    pack, width = hidden.shape
    mine, fine, wide = down_w[0].shape
    first = up_w[0].shape[0] - mine
    operands, shapes, sems = carry_operands(carry)
    hbm = pl.BlockSpec(memory_space=pl.ANY)

    def token(n):
        return pl.BlockSpec((tile, n), lambda i: (i, 0))

    def weight(first, *shape):
        return pl.BlockSpec((None,) + shape, lambda i: (first + e, 0, 0))

    near = pl.BlockSpec((3, wide, fine), lambda i: (0, 0, 0))
    others = pl.BlockSpec((blocks - 1, 3, wide, fine), lambda i: (0, 0, 0, 0))
    out_specs, out_shape = [near, others], [
        jax.ShapeDtypeStruct((3, wide, fine), BF16),
        jax.ShapeDtypeStruct((blocks - 1, 3, wide, fine), BF16),
    ]
    if full:
        out_specs = [token(fine)] * 3 + [token(1)] + out_specs
        out_shape = (
            [jax.ShapeDtypeStruct((pack, fine), BF16)] * 3
            + [jax.ShapeDtypeStruct((pack, 1), F32)]
            + out_shape
        )
    remote_params = dict(collective_id=ident, has_side_effects=True) if carry else {}
    return pl.pallas_call(
        functools.partial(expert_kernel, blocks, e, far, mine, full, [axis for axis, _ in carry]),
        cost_estimate=pl.CostEstimate(flops=27 * MICRO, bytes_accessed=0, transcendentals=0),
        grid=(pack // tile,),
        in_specs=[token(width), token(width), token(chosen.shape[1])]
        + [pl.BlockSpec(router.shape, lambda i: (0, 0))]
        + [weight(0, wide, fine)] * blocks
        + [weight(first, wide, fine)] * blocks
        + [weight(0, fine, wide)] * blocks
        + [hbm] * len(operands),
        out_specs=out_specs + [hbm] * len(shapes),
        out_shape=out_shape + shapes,
        scratch_shapes=[pltpu.VMEM((fine, width), F32)] * 3 + sems,
        compiler_params=pltpu.CompilerParams(vmem_limit_bytes=56 << 20, **remote_params),
    )(hidden, upstream, chosen, router, *gate_w, *up_w, *down_w, *operands)


def signal_all(partners):
    barrier = pltpu.get_barrier_semaphore()
    count = 0
    for device, there in partners:

        @pl.when(there)
        def _():
            pl.semaphore_signal(barrier, inc=1, device_id=device, device_id_type=MESH)

        count = count + jnp.where(there, 1, 0)
    pl.semaphore_wait(barrier, count)


def place():
    c, t = lax.axis_index("ctx"), lax.axis_index("tp")
    core, side = lax.rem(t, 2), t // 2
    over_core = {"tp": t + 1 - 2 * core}
    over_side = {"tp": t + 2 - 4 * side}
    return c, lax.axis_size("ctx"), core, side, over_core, over_side


def remote(source, target, sems, at, device):
    send, recv = sems
    return pltpu.make_async_remote_copy(
        src_ref=source,
        dst_ref=target,
        send_sem=send.at[at],
        recv_sem=recv.at[at],
        device_id=device,
        device_id_type=MESH,
    )


def spread_kernel(axes, x_ref, *refs):
    count = len(axes)
    sources, out_ref, targets = refs[:count], refs[count], refs[count + 1 : 2 * count + 1]
    local, zs, zr, ys, yr, cs, cr = refs[2 * count + 1 : 2 * count + 8]
    moving, more = carried(axes, sources, targets, refs[2 * count + 8 :])
    c, n, core, side, over_core, over_side = place()
    rows, part = x_ref.shape
    left, right = {"ctx": c - 1}, {"ctx": c + 1}
    signal_all(
        [(left, c > 0), (right, c < n - 1), (over_core, c >= 0), (over_side, c >= 0)] + more
    )
    for copy in moving:
        copy.start()
    mine = core * 2 + side
    other = core * 2 + 1 - side

    def tile(owner, column):
        return out_ref.at[
            pl.ds(pl.multiple_of(owner * rows, rows), rows),
            pl.ds(pl.multiple_of(column * part, part), part),
        ]

    def along(owner, source, target, at):
        return remote(source, tile(owner, mine), (zs, zr), at, target)

    keep = pltpu.make_async_copy(x_ref, tile(c, mine), local)
    keep.start()

    @pl.when(c > 0)
    def _():
        along(c, x_ref, left, n + c).start()

    @pl.when(c < n - 1)
    def _():
        along(c, x_ref, right, c).start()

    def to_side(owner, source):
        return remote(source, tile(owner, mine), (ys, yr), owner, over_side)

    def to_core(owner, column, source, which):
        return remote(source, tile(owner, column), (cs, cr), which * n + owner, over_core)

    to_side(c, x_ref).start()
    to_core(c, mine, x_ref, 0).start()

    def from_side(owner):
        here = tile(owner, other)
        remote(here, here, (ys, yr), owner, over_side).wait_recv()
        to_core(owner, other, here, 1).start()

    from_side(c)
    for far in range(1, n):
        for sign, there, onward, more in (
            (-1, c - far >= 0, right, c < n - 1),
            (1, c + far < n, left, c > 0),
        ):
            owner = c + sign * far
            slot = owner if sign < 0 else n + owner

            @pl.when(there)
            def _():
                here = tile(owner, mine)
                along(owner, here, onward, slot).wait_recv()

                @pl.when(more)
                def _():
                    along(owner, here, onward, slot).start()

                to_side(owner, here).start()
                to_core(owner, mine, here, 0).start()

        for sign, there in ((-1, c - far >= 0), (1, c + far < n)):

            @pl.when(there)
            def _():
                from_side(c + sign * far)

    keep.wait()

    @pl.when(c > 0)
    def _():
        along(c, x_ref, left, n + c).wait_send()

    @pl.when(c < n - 1)
    def _():
        along(c, x_ref, right, c).wait_send()

    for far in range(1, n):
        for sign, there, onward, more in (
            (-1, c - far >= 0, right, c < n - 1),
            (1, c + far < n, left, c > 0),
        ):
            owner = c + sign * far

            @pl.when(there & more)
            def _():
                here = tile(owner, mine)
                along(owner, here, onward, owner if sign < 0 else n + owner).wait_send()

    for owner in range(n):
        to_side(owner, tile(owner, mine)).wait_send()
        to_core(owner, mine, tile(owner, mine), 0).wait_send()
        to_core(owner, other, tile(owner, other), 1).wait_send()
        for which, column in ((0, (1 - core) * 2 + side), (1, (1 - core) * 2 + 1 - side)):
            here = tile(owner, column)
            remote(here, here, (cs, cr), which * n + owner, over_core).wait_recv()
    for copy in moving:
        copy.wait()


def spread(v, ident, carry=()):
    operands, shapes, sems = carry_operands(carry)
    hbm = pl.BlockSpec(memory_space=pl.ANY)
    n, tp = lax.axis_size("ctx"), lax.axis_size("tp")
    rows, part = v.shape
    dma = pltpu.SemaphoreType.DMA
    return pl.pallas_call(
        functools.partial(spread_kernel, [axis for axis, _ in carry]),
        cost_estimate=pl.CostEstimate(flops=60 * MICRO, bytes_accessed=0, transcendentals=0),
        out_shape=[jax.ShapeDtypeStruct((n * rows, tp * part), v.dtype)] + shapes,
        in_specs=[hbm] * (1 + len(shapes)),
        out_specs=[hbm] * (1 + len(shapes)),
        scratch_shapes=[dma]
        + [dma((2 * n,))] * 2
        + [dma((n,))] * 2
        + [dma((2 * n,))] * 2
        + sems,
        compiler_params=pltpu.CompilerParams(collective_id=ident, has_side_effects=True),
    )(v, *operands)


def join_kernel(x_ref, out_ref, local, ss, sr):
    c, n, core, side, over_core, over_side = place()
    rows, part = x_ref.shape
    signal_all([(over_core, c >= 0), (over_side, c >= 0)])
    mine, other = core * 2 + side, core * 2 + 1 - side

    def tile(column):
        return out_ref.at[:, pl.ds(pl.multiple_of(column * part, part), part)]

    keep = pltpu.make_async_copy(x_ref, tile(mine), local)
    keep.start()
    first = remote(x_ref, tile(mine), (ss, sr), 0, over_side)
    first.start()
    second = remote(x_ref, tile(mine), (ss, sr), 1, over_core)
    second.start()
    first.wait_recv()
    third = remote(tile(other), tile(other), (ss, sr), 2, over_core)
    third.start()
    keep.wait()
    first.wait_send()
    second.wait()
    third.wait()


def join(v, ident):
    tp = lax.axis_size("tp")
    rows, part = v.shape
    dma = pltpu.SemaphoreType.DMA
    return pl.pallas_call(
        join_kernel,
        cost_estimate=pl.CostEstimate(flops=25 * MICRO, bytes_accessed=0, transcendentals=0),
        out_shape=jax.ShapeDtypeStruct((rows, tp * part), v.dtype),
        in_specs=[pl.BlockSpec(memory_space=pl.ANY)],
        out_specs=pl.BlockSpec(memory_space=pl.ANY),
        scratch_shapes=[dma] + [dma((3,))] * 2,
        compiler_params=pltpu.CompilerParams(collective_id=ident, has_side_effects=True),
    )(v)


def collect_kernel(
    owners, x_ref, out_ref, core_in, side_out, side_in, z_out, z_in, cs, cr, ys, yr, zs, zr
):
    c, n, core, side, over_core, over_side = place()
    rows, part = out_ref.shape
    left, right = {"ctx": c - 1}, {"ctx": c + 1}
    partners = [(over_core, c >= 0), (over_side, c >= 0)]
    if owners > 1:
        partners += [(left, c > 0), (right, c < n - 1)]
    signal_all(partners)

    def owner_of(i):
        if owners == 1:
            return 0
        owner = 0
        for at in range(n):
            for turn, far in enumerate(sorted(range(n), key=lambda o: -abs(o - at))):
                owner = jnp.where((c == at) & (i == turn), far, owner)
        return owner

    def own_rows(owner):
        return pl.ds(pl.multiple_of(owner * rows, rows), rows)

    def half(which):
        return pl.ds(pl.multiple_of(which * 2 * part, 2 * part), 2 * part)

    def quarter(which):
        return pl.ds(pl.multiple_of((core * 2 + which) * part, part), part)

    def to_core(i):
        source = x_ref.at[own_rows(owner_of(i)), half(1 - core)]
        return remote(source, core_in.at[i], (cs, cr), i, over_core)

    def to_side(i):
        return remote(side_out.at[i], side_in.at[i], (ys, yr), i, over_side)

    def to_left(owner):
        return remote(z_out.at[owner], z_in.at[1, owner], (zs, zr), n + owner, left)

    def to_right(owner):
        return remote(z_out.at[owner], z_in.at[0, owner], (zs, zr), owner, right)

    def from_core(i, which):
        local = x_ref[own_rows(owner_of(i)), quarter(which)].astype(F32)
        near = core_in[i, :, pl.ds(pl.multiple_of(which * part, part), part)]
        return local + near.astype(F32)

    for i in range(owners):
        to_core(i).start()

    def finish(i):
        to_side(i).wait_recv()
        owner = owner_of(i)
        total = from_core(i, side) + side_in[i].astype(F32)
        if owners == 1:
            out_ref[...] = total
            return

        @pl.when(owner > c)
        def _():
            @pl.when(c > 0)
            def _():
                to_right(owner).wait_recv()
                z_out[owner] = (total + z_in[0, owner].astype(F32)).astype(z_out.dtype)

            @pl.when(c == 0)
            def _():
                z_out[owner] = total.astype(z_out.dtype)

            to_right(owner).start()

        @pl.when(owner < c)
        def _():
            @pl.when(c < n - 1)
            def _():
                to_left(owner).wait_recv()
                z_out[owner] = (total + z_in[1, owner].astype(F32)).astype(z_out.dtype)

            @pl.when(c == n - 1)
            def _():
                z_out[owner] = total.astype(z_out.dtype)

            to_left(owner).start()

        @pl.when(owner == c)
        def _():
            out_ref[...] = total

    def step(i, carry):
        @pl.when(i < owners)
        def _():
            to_core(i).wait_recv()
            side_out[i] = from_core(i, 1 - side).astype(side_out.dtype)
            to_side(i).start()

        @pl.when(i > 0)
        def _():
            finish(i - 1)

        return carry

    lax.fori_loop(0, owners + 1, step, 0)

    if owners > 1:

        @pl.when(c > 0)
        def _():
            to_right(c).wait_recv()
            out_ref[...] += z_in[0, c].astype(F32)

        @pl.when(c < n - 1)
        def _():
            to_left(c).wait_recv()
            out_ref[...] += z_in[1, c].astype(F32)

    def close(i, carry):
        to_core(i).wait_send()
        to_side(i).wait_send()
        if owners > 1:
            owner = owner_of(i)

            @pl.when(owner > c)
            def _():
                to_right(owner).wait_send()

            @pl.when(owner < c)
            def _():
                to_left(owner).wait_send()

        return carry

    lax.fori_loop(0, owners, close, 0)


def collect(v, owners, ident):
    n, tp = lax.axis_size("ctx"), lax.axis_size("tp")
    rows, part = v.shape[0] // owners, v.shape[1] // tp
    dma = pltpu.SemaphoreType.DMA
    z = n if owners > 1 else 1
    return pl.pallas_call(
        functools.partial(collect_kernel, owners),
        cost_estimate=pl.CostEstimate(flops=17 * MICRO, bytes_accessed=0, transcendentals=0),
        out_shape=jax.ShapeDtypeStruct((rows, part), F32),
        in_specs=[pl.BlockSpec(memory_space=pltpu.VMEM)],
        out_specs=pl.BlockSpec(memory_space=pltpu.VMEM),
        scratch_shapes=[
            pltpu.VMEM((owners, rows, 2 * part), BF16),
            pltpu.VMEM((owners, rows, part), BF16),
            pltpu.VMEM((owners, rows, part), BF16),
            pltpu.VMEM((z, rows, part), BF16),
            pltpu.VMEM((2, z, rows, part), BF16),
        ]
        + [dma((owners,))] * 4
        + [dma((2 * z,))] * 2,
        compiler_params=pltpu.CompilerParams(
            collective_id=ident, has_side_effects=True, vmem_limit_bytes=48 << 20
        ),
    )(v)


def returns_kernel(kinds, mine, blocks, flipped, with_dots, axes, *refs):
    refs = list(refs)

    def take(count):
        return [refs.pop(0) for _ in range(count)]

    lhs_refs, weight_refs = take(kinds * mine), take(kinds * blocks)
    dots_ref = take(1)[0] if with_dots else None
    sources = take(len(axes))
    out_ref = take(1)[0]
    dots_out = take(1)[0] if with_dots else None
    targets = take(len(axes))
    lhs, weights, core_out, core_in, keep, near, side_out, side_in, z_out, z_in = take(10)
    ls, ws, cs, cr, ys, yr, zs, zr = take(8)
    dots_in, ds, dr = take(3) if with_dots else (None, None, None)
    moving, more = carried(axes, sources, targets, take(2 * len(axes)))
    c, n, core, side, over_core, over_side = place()
    t, tp = lax.axis_index("tp"), lax.axis_size("tp")
    rows, part = out_ref.shape
    fine = lhs_refs[0].shape[1]
    wide = out_ref.shape[1] * tp // blocks
    half_blocks = blocks // 2
    left, right = {"ctx": c - 1}, {"ctx": c + 1}

    loads = []
    for k in range(kinds):
        for e in range(mine):
            at = k * mine + e
            columns = pl.ds(at * fine, fine)
            loads.append(pltpu.make_async_copy(lhs_refs[at], lhs.at[:, columns], ls.at[at]))
            for s in range(blocks):
                source = weight_refs[k * blocks + s].at[e]
                target = weights.at[s, columns, :] if flipped else weights.at[s, :, columns]
                loads.append(pltpu.make_async_copy(source, target, ws.at[at * blocks + s]))
    for load in loads:
        load.start()
    if with_dots:
        others = []
        for far_c in range(n):
            for far_t in range(tp):
                others.append(({"ctx": far_c, "tp": far_t}, (c != far_c) | (t != far_t)))
    else:
        others = [(over_core, c >= 0), (over_side, c >= 0), (left, c > 0), (right, c < n - 1)]
    others += more
    signal_all(others)
    for copy in moving:
        copy.start()

    def own_rows(owner):
        return pl.ds(pl.multiple_of(owner * rows, rows), rows)

    def dots_copy(owner, far_t):
        source = dots_ref.at[:, own_rows(owner)]
        return pltpu.make_async_remote_copy(
            src_ref=source,
            dst_ref=dots_in.at[c * tp + t],
            send_sem=ds.at[owner * tp + far_t],
            recv_sem=dr.at[c * tp + t],
            device_id={"ctx": owner, "tp": far_t},
            device_id_type=MESH,
        )

    def dots_from(at):
        here = dots_in.at[at]
        return pltpu.make_async_remote_copy(
            src_ref=here,
            dst_ref=here,
            send_sem=ds.at[at],
            recv_sem=dr.at[at],
            device_id=over_core,
            device_id_type=MESH,
        )

    if with_dots:
        for owner in range(n):
            for far_t in range(tp):

                @pl.when((c != owner) | (t != far_t))
                def _():
                    dots_copy(owner, far_t).start()

        dots_in[c * tp + t] = dots_ref[:, own_rows(c)]

    for load in loads:
        load.wait()

    def owner_of(i):
        owner = 0
        for at in range(n):
            for turn, far in enumerate(sorted(range(n), key=lambda o: -abs(o - at))):
                owner = jnp.where((c == at) & (i == turn), far, owner)
        return owner

    def to_core(i):
        return remote(core_out.at[i], core_in.at[i], (cs, cr), i, over_core)

    def to_side(i):
        return remote(side_out.at[i], side_in.at[i], (ys, yr), i, over_side)

    def to_left(owner):
        return remote(z_out.at[owner], z_in.at[1, owner], (zs, zr), n + owner, left)

    def to_right(owner):
        return remote(z_out.at[owner], z_in.at[0, owner], (zs, zr), owner, right)

    def product(i, which, into):
        taken = lhs[own_rows(owner_of(i)), :]
        for j in range(half_blocks):
            w = weights[which * half_blocks + j]
            into(j, dot(taken, w) if flipped else dot_t(taken, w))

    def columns_of(j):
        return pl.ds(j * wide, wide)

    def quarter(which):
        return pl.ds(pl.multiple_of(which * part, part), part)

    def begin(i):
        def send_part(j, v):
            core_out[i, :, columns_of(j)] = v.astype(core_out.dtype)

        def keep_part(j, v):
            keep[lax.rem(i, 2), :, columns_of(j)] = v

        product(i, 1 - core, send_part)
        to_core(i).start()
        product(i, core, keep_part)

    def cross(i):
        to_core(i).wait_recv()
        slot = lax.rem(i, 2)

        def summed(which):
            return keep[slot, :, quarter(which)] + core_in[i, :, quarter(which)].astype(F32)

        side_out[i] = summed(1 - side).astype(side_out.dtype)
        to_side(i).start()
        near[slot] = summed(side)

    def finish(i):
        to_side(i).wait_recv()
        owner = owner_of(i)
        total = near[lax.rem(i, 2)] + side_in[i].astype(F32)

        @pl.when(owner > c)
        def _():
            @pl.when(c > 0)
            def _():
                to_right(owner).wait_recv()
                z_out[owner] = (total + z_in[0, owner].astype(F32)).astype(z_out.dtype)

            @pl.when(c == 0)
            def _():
                z_out[owner] = total.astype(z_out.dtype)

            to_right(owner).start()

        @pl.when(owner < c)
        def _():
            @pl.when(c < n - 1)
            def _():
                to_left(owner).wait_recv()
                z_out[owner] = (total + z_in[1, owner].astype(F32)).astype(z_out.dtype)

            @pl.when(c == n - 1)
            def _():
                z_out[owner] = total.astype(z_out.dtype)

            to_left(owner).start()

        @pl.when(owner == c)
        def _():
            out_ref[...] = total

    def step(i, carry):
        @pl.when(i < n)
        def _():
            begin(i)

        @pl.when(i > 1)
        def _():
            finish(i - 2)

        @pl.when((i > 0) & (i <= n))
        def _():
            cross(i - 1)

        return carry

    lax.fori_loop(0, n + 2, step, 0)

    @pl.when(c > 0)
    def _():
        to_right(c).wait_recv()
        out_ref[...] += z_in[0, c].astype(F32)

    @pl.when(c < n - 1)
    def _():
        to_left(c).wait_recv()
        out_ref[...] += z_in[1, c].astype(F32)

    if with_dots:
        for at in range(n * tp):

            @pl.when(c * tp + t != at)
            def _():
                dots_from(at).wait_recv()

        for at in range(n):
            dots_out[at] = sum(dots_in[at * tp + far_t] for far_t in range(tp))
        for owner in range(n):
            for far_t in range(tp):

                @pl.when((c != owner) | (t != far_t))
                def _():
                    dots_copy(owner, far_t).wait_send()

    def close(i, carry):
        to_core(i).wait_send()
        to_side(i).wait_send()
        owner = owner_of(i)

        @pl.when(owner > c)
        def _():
            to_right(owner).wait_send()

        @pl.when(owner < c)
        def _():
            to_left(owner).wait_send()

        return carry

    lax.fori_loop(0, n, close, 0)
    for copy in moving:
        copy.wait()


def returns(lhs, weights, dots, flipped, ident, carry=()):
    n, tp = lax.axis_size("ctx"), lax.axis_size("tp")
    kinds, mine = len(lhs), len(lhs[0])
    blocks = len(weights[0])
    pack, fine = lhs[0][0].shape
    wide = weights[0][0].shape[2 if flipped else 1]
    rows, part = pack // n, wide * blocks // tp
    deep = kinds * mine * fine
    dma, vmem = pltpu.SemaphoreType.DMA, pltpu.VMEM
    hbm = pl.BlockSpec(memory_space=pl.ANY)
    near = pl.BlockSpec(memory_space=pltpu.VMEM)
    operands = [v for kind in lhs for v in kind] + [w for kind in weights for w in kind]
    in_specs = [hbm] * len(operands)
    out_shape = [jax.ShapeDtypeStruct((rows, part), F32)]
    extra = []
    if dots is not None:
        operands.append(dots)
        in_specs.append(near)
        out_shape.append(jax.ShapeDtypeStruct((n, mine, rows), F32))
        extra = [vmem((n * tp, mine, rows), F32), dma((n * tp,)), dma((n * tp,))]
    carried_in, shapes, sems = carry_operands(carry)
    axes = [axis for axis, _ in carry]
    return pl.pallas_call(
        functools.partial(
            returns_kernel, kinds, mine, blocks, flipped, dots is not None, axes
        ),
        cost_estimate=pl.CostEstimate(flops=65 * MICRO, bytes_accessed=0, transcendentals=0),
        out_shape=out_shape + shapes,
        in_specs=in_specs + [hbm] * len(shapes),
        out_specs=[near] * len(out_shape) + [hbm] * len(shapes),
        scratch_shapes=[
            vmem((pack, deep), BF16),
            vmem((blocks, deep, wide) if flipped else (blocks, wide, deep), BF16),
            vmem((n, rows, 2 * part), BF16),
            vmem((n, rows, 2 * part), BF16),
            vmem((2, rows, 2 * part), F32),
            vmem((2, rows, part), F32),
            vmem((n, rows, part), BF16),
            vmem((n, rows, part), BF16),
            vmem((n, rows, part), BF16),
            vmem((2, n, rows, part), BF16),
            dma((kinds * mine,)),
            dma((kinds * mine * blocks,)),
        ]
        + [dma((n,))] * 4
        + [dma((2 * n,))] * 2
        + extra
        + sems,
        compiler_params=pltpu.CompilerParams(
            collective_id=ident, has_side_effects=True, vmem_limit_bytes=56 << 20
        ),
    )(*operands, *carried_in)


def mixture_kernel(blocks, tp, *refs):
    inner_refs, out_ref = refs[: -1 - blocks], refs[-1]
    weights = refs[-1 - blocks : -1]
    wide, part = weights[0].shape[2], out_ref.shape[2]
    step = min(wide, part)
    inners = [r[...] for r in inner_refs]
    for start in range(0, wide * blocks, step):
        s, here = start // wide, pl.ds(start % wide, step)
        total = sum(dot(v, weights[s][e, :, here]) for e, v in enumerate(inners))
        column = start // part
        out_ref[(column % 2) * 2 + column // 2, :, pl.ds(start % part, step)] = total.astype(BF16)


def mixture_parts(inners, weights, tp, tile=512):
    pack, fine = inners[0].shape
    mine, blocks = len(inners), len(weights)
    wide = weights[0].shape[2]
    part = wide * blocks // tp
    return pl.pallas_call(
        functools.partial(mixture_kernel, blocks, tp),
        cost_estimate=pl.CostEstimate(flops=15 * MICRO, bytes_accessed=0, transcendentals=0),
        grid=(pack // tile,),
        in_specs=[pl.BlockSpec((tile, fine), lambda i: (i, 0))] * mine
        + [pl.BlockSpec((mine, fine, wide), lambda i: (0, 0, 0))] * blocks,
        out_specs=pl.BlockSpec((tp, tile, part), lambda i: (0, i, 0)),
        out_shape=jax.ShapeDtypeStruct((tp, pack, part), BF16),
        compiler_params=pltpu.CompilerParams(vmem_limit_bytes=48 << 20),
    )(*inners, *weights)


def place_kernel(at_ref, near_ref, far_ref, *refs):
    gate_ref, up_ref, down_ref = refs[-3:]
    fine, wide = down_ref.shape

    def write(source):
        gate_ref[...] = source[0].astype(F32)
        up_ref[...] = source[1].astype(F32)
        for j in range(wide // fine):
            down_ref[:, pl.ds(j * fine, fine)] = source[2, pl.ds(j * fine, fine), :].astype(F32)

    pl.when(pl.program_id(0) == 0)(lambda: write(near_ref))
    pl.when(pl.program_id(0) == 1)(lambda: write(far_ref))


def place_grads(at, near, far, experts, held):
    _, wide, fine = near.shape
    source = pl.BlockSpec(near.shape, lambda i, at_ref: (0, 0, 0))
    gate = pl.BlockSpec((None, wide, fine), lambda i, at_ref: (at_ref[i], 0, 0))
    down = pl.BlockSpec((None, fine, wide), lambda i, at_ref: (at_ref[i], 0, 0))
    return pl.pallas_call(
        place_kernel,
        cost_estimate=pl.CostEstimate(flops=4 * MICRO, bytes_accessed=0, transcendentals=0),
        grid_spec=pltpu.PrefetchScalarGridSpec(
            num_scalar_prefetch=1,
            grid=(2,),
            in_specs=[source, source] + [pl.BlockSpec(memory_space=pl.ANY)] * len(held),
            out_specs=[gate, gate, down],
        ),
        out_shape=[jax.ShapeDtypeStruct((experts, wide, fine), F32)] * 2
        + [jax.ShapeDtypeStruct((experts, fine, wide), F32)],
        input_output_aliases={3 + i: i for i in range(len(held))},
        compiler_params=pltpu.CompilerParams(vmem_limit_bytes=32 << 20),
    )(at, near, far, *held)


def share_kernel(over_tp, x_ref, out_ref, slots, ss, sr):
    c, t = lax.axis_index("ctx"), lax.axis_index("tp")
    n, tp = lax.axis_size("ctx"), lax.axis_size("tp")
    me = c * tp + t
    everyone = [(far_c, far_t) for far_c in range(n) for far_t in range(tp)]
    signal_all(
        [({"ctx": far_c, "tp": far_t}, (c != far_c) | (t != far_t)) for far_c, far_t in everyone]
    )

    def copy(far_c, far_t):
        return pltpu.make_async_remote_copy(
            src_ref=x_ref,
            dst_ref=slots.at[me],
            send_sem=ss.at[far_c * tp + far_t],
            recv_sem=sr.at[me],
            device_id={"ctx": far_c, "tp": far_t},
            device_id_type=MESH,
        )

    for far_c, far_t in everyone:

        @pl.when((c != far_c) | (t != far_t))
        def _():
            copy(far_c, far_t).start()

    slots[me] = x_ref[...]
    for at in range(n * tp):

        @pl.when(me != at)
        def _():
            pltpu.make_async_remote_copy(
                src_ref=slots.at[at],
                dst_ref=slots.at[at],
                send_sem=ss.at[at],
                recv_sem=sr.at[at],
                device_id={"tp": lax.rem(t + 1, tp)},
                device_id_type=MESH,
            ).wait_recv()

    sums = [sum(slots[far_c * tp + far_t] for far_c in range(n)) for far_t in range(tp)]
    if over_tp:
        out_ref[...] = sum(sums)
    else:
        for far_t in range(tp):
            out_ref[far_t] = sums[far_t]
    for far_c, far_t in everyone:

        @pl.when((c != far_c) | (t != far_t))
        def _():
            copy(far_c, far_t).wait_send()


def share(v, over_tp, ident):
    n, tp = lax.axis_size("ctx"), lax.axis_size("tp")
    dma = pltpu.SemaphoreType.DMA
    near = pl.BlockSpec(memory_space=pltpu.VMEM)
    return pl.pallas_call(
        functools.partial(share_kernel, over_tp),
        cost_estimate=pl.CostEstimate(flops=8 * MICRO, bytes_accessed=0, transcendentals=0),
        out_shape=jax.ShapeDtypeStruct(v.shape if over_tp else (tp,) + v.shape, v.dtype),
        in_specs=[near],
        out_specs=near,
        scratch_shapes=[pltpu.VMEM((n * tp,) + v.shape, v.dtype)] + [dma((n * tp,))] * 2,
        compiler_params=pltpu.CompilerParams(
            collective_id=ident, has_side_effects=True, vmem_limit_bytes=32 << 20
        ),
    )(v)


def body(
    tokens,
    cotangent,
    lengths,
    routes,
    attn_gain,
    w_query,
    w_key,
    w_value,
    q_gain,
    k_gain,
    w_out,
    mlp_gain,
    w_router,
    w_gate,
    w_up,
    w_down,
):
    dp_at, ctx_at, tp_at = (lax.axis_index(a) for a in ("dp", "ctx", "tp"))
    dp_count, ctx_count, tp_count = (lax.axis_size(a) for a in ("dp", "ctx", "tp"))
    rows, width = tokens.shape
    wide = w_query.shape[0]
    local = w_query.shape[1]
    heads = local // HEAD
    experts = w_router.shape[1]
    mine = experts // ctx_count
    part = width // tp_count
    column_at = lax.rem(tp_at, 2) * 2 + tp_at // 2

    def fetch(v):
        others = [
            lax.ppermute(v, "dp", [((i + s) % dp_count, i) for i in range(dp_count)])
            for s in range(1, dp_count)
        ]
        return [v] + others

    def hand_over(blocks):
        total = blocks[0].astype(F32)
        for s in range(1, dp_count):
            pairs = [(i, (i + s) % dp_count) for i in range(dp_count)]
            total = total + lax.ppermute(blocks[s].astype(BF16), "dp", pairs).astype(F32)
        return total

    def swap(blocks):
        return [
            lax.ppermute(blocks[s], "dp", [(i, (i + s) % dp_count) for i in range(dp_count)])
            for s in range(1, dp_count)
        ]

    def add(blocks, arrived):
        return sum(v.astype(F32) for v in [blocks[0]] + arrived).astype(BF16)

    def columns(v):
        return lax.dynamic_slice_in_dim(v, column_at * part, part, v.ndim - 1)

    def block(v, s):
        return v[:, s * wide : (s + 1) * wide]

    def own_experts(w):
        return lax.dynamic_slice_in_dim(w, ctx_at * mine, mine, 0)

    small = jnp.concatenate(
        [attn_gain[None], q_gain[None], k_gain[None], mlp_gain[None], w_router.T], axis=0
    )
    small = jnp.concatenate(fetch(small), axis=1)
    gains = small[:4].astype(F32)
    router_w = small[4:]
    gain_one, gain_two = gains[0], columns(gains[3])

    def heads_gain(v):
        back = jnp.roll(v, dp_at * wide)
        return lax.dynamic_slice_in_dim(back, tp_at * local, local)

    gain_q, gain_k = heads_gain(gains[1]), heads_gain(gains[2])
    own_cols = local // ctx_count
    head_at = tp_at * local + ctx_at * own_cols

    def own_heads(w):
        return lax.dynamic_slice_in_dim(w, ctx_at * own_cols, own_cols, 1)

    def natural(v):
        return jnp.roll(v, dp_at * wide, axis=-1)

    gain_q, gain_k = lax.dynamic_slice_in_dim(natural(gains[1:3]), head_at, own_cols, 1)
    heads_w = jnp.concatenate([own_heads(w) for w in (w_query, w_key, w_value)], axis=1)
    weights = (w_gate, w_up, w_down)
    beside_at = jnp.bitwise_xor(ctx_at, 2)

    def experts_of(w, plane):
        return lax.dynamic_slice_in_dim(w, plane * mine, mine, 0)


    own_slices = [experts_of(w, ctx_at) for w in weights]
    tokens = jnp.roll(tokens, -dp_at * wide, axis=1)

    inputs = tokens.astype(F32)
    scale_one = lax.rsqrt(jnp.mean(inputs * inputs, axis=1, keepdims=True) + EPS)
    hidden_one = columns((inputs * scale_one * gain_one).astype(BF16))
    hidden_one, own_slices = lax.optimization_barrier((hidden_one, own_slices))
    hidden_one, *got = spread(
        hidden_one, 1, [("w", heads_w), ("w", w_out), ("w", own_slices[0])]
    )

    def listed(w, received):
        return [w] + [received[s] for s in range(dp_count - 1)]

    heads_w, out_w = listed(heads_w, got[0]), listed(w_out, got[1])
    own_w = [listed(own_slices[0], got[2]), fetch(own_slices[1]), None]
    if wide % part == 0:

        def upstream_columns(at):
            return lax.dynamic_slice_in_dim(
                cotangent, lax.rem(at * part + dp_at * wide, width), part, 1
            )

    else:
        turned_cotangent = jnp.roll(cotangent, -dp_at * wide, axis=1)

        def upstream_columns(at):
            return lax.dynamic_slice_in_dim(turned_cotangent, at * part, part, 1)

    chosen = jnp.any(
        routes[:, :, None] == jnp.arange(experts, dtype=jnp.int32)[None, None, :], axis=1
    )
    upstream_all = jnp.concatenate([upstream_columns(tp_at), chosen.astype(BF16).T])
    upstream_all = lax.all_gather(upstream_all, "ctx", axis=0, tiled=False)
    chosen_all = upstream_all[:, rows:].transpose(0, 2, 1).reshape(-1, experts).astype(F32)
    hidden_one, upstream_all = lax.optimization_barrier((hidden_one, upstream_all))
    upstream_all = lax.all_gather(upstream_all[:, :rows].reshape(-1, part), "tp", axis=1, tiled=True)
    raw = sum(dot(block(hidden_one, s), w) for s, w in enumerate(heads_w))
    q_raw, k_raw = raw[:, :own_cols], raw[:, own_cols : 2 * own_cols]
    values = raw[:, 2 * own_cols :].astype(BF16)
    pack = raw.shape[0]
    squares = share(
        jnp.stack([jnp.sum(q_raw * q_raw, axis=1), jnp.sum(k_raw * k_raw, axis=1)]), True, 5
    )
    q_scale, k_scale = lax.rsqrt(squares / width + EPS)[:, :, None]
    q_hat, k_hat = q_raw * q_scale, k_raw * k_scale
    cosine, sine = rotation(lengths[0], 0, pack)
    mine_heads = own_cols // HEAD

    def turn(v, sine):
        return rotate(v.reshape(pack, mine_heads, HEAD), cosine, sine)

    def by_head(v):
        return v.astype(BF16).reshape(pack, mine_heads, HEAD).transpose(1, 0, 2)

    q_all, k_all = by_head(turn(q_hat * gain_q, sine)), by_head(turn(k_hat * gain_k, sine))
    v_all = by_head(values)
    attended_all, log = attend(lengths, q_all, k_all, v_all)
    attended = to_rows((attended_all,))[0].reshape(rows, local)
    branch = jnp.concatenate([dot(attended, w).astype(BF16) for w in out_w], axis=1)
    branch, own_w[1] = lax.optimization_barrier((branch, own_w[1]))
    branch = collect(branch, 1, 2)
    inputs_c = columns(inputs)
    mixed = inputs_c + branch
    square = lax.psum(jnp.sum(mixed * mixed, axis=1), "tp")
    scale_two = lax.rsqrt(square / width + EPS)[:, None]
    normed_two = mixed * scale_two
    hidden_mine = (normed_two * gain_two).astype(BF16)
    hidden_two, got = spread(hidden_mine, 3, [("w", own_slices[2])])
    own_w[2] = listed(own_slices[2], got)
    hidden_two, late = lax.optimization_barrier((hidden_two, weights))
    far_slices = [experts_of(w, beside_at) for w in late]
    far_slices = [jnp.concatenate(far_slices[:2]), far_slices[2]]

    tie = lax.optimization_barrier
    grads, sums, there = {}, {}, {}

    def run(e):
        far = e >= mine
        w = far_w if far else own_w
        number = e % mine
        out = expert(
            number, hidden_two, upstream_all, chosen_all, router_w, w, far, not far, [], 20 + e
        )
        grads[e] = [out[-2], out[-1]]
        return list(out[:-2])

    def start_x(e):
        grads[e][1] = swap([None] + [grads[e][1][s] for s in range(dp_count - 1)])

    def end_x(e, after):
        grads[e][1], after = tie((grads[e][1], after))
        sums[e] = add([grads[e][0]], grads[e][1])
        return after

    def start_z(e):
        there[e] = lax.ppermute(sums[e], "ctx", [(i, i ^ 1) for i in range(ctx_count)])

    def end_z(e, after):
        there[e], after = tie((there[e], after))
        return after

    parts = []
    for e in range(mine):
        parts.append(run(e))
        if e > 0:
            hidden_two = end_x(e - 1, (hidden_two, grads[e][1]))[0]
            if e == 1:
                hidden_two, far_slices = tie((hidden_two, far_slices))
            start_z(e - 1)
        if e > 2:
            hidden_two = end_z(e - 3, hidden_two)
        start_x(e)
    mixture = mixture_parts([p[0] for p in parts], own_w[2], tp_count)
    mixture, hidden_two = tie((mixture, hidden_two))
    mixture = lax.psum_scatter(mixture, "tp", scatter_dimension=0, tiled=False)
    dots = jnp.concatenate([p[3] for p in parts], axis=1).T
    dots, hidden_two = tie((dots, hidden_two))
    far_both = fetch(far_slices[0])
    expert_in, dots = returns(
        [[p[1] for p in parts], [p[2] for p in parts]],
        own_w[:2],
        dots,
        False,
        4,
    )
    far_both, expert_in, late_down = tie((far_both, expert_in, far_slices[1]))
    far_down = fetch(late_down)
    for e in range(1, mine - 1):
        expert_in = end_z(e, expert_in)
    expert_in, mixture = tie((expert_in, mixture))
    mixture = lax.psum_scatter(mixture, "ctx", scatter_dimension=0, tiled=True)

    dots = dots.reshape(experts, rows).T
    hidden_rows = lax.dynamic_slice_in_dim(hidden_two, ctx_at * rows, rows, 0)
    route_mine = jax.nn.softmax(dot_t(hidden_rows, router_w), axis=1)
    d_logits = (
        route_mine * (dots - jnp.sum(route_mine * dots, axis=1, keepdims=True))
    ).astype(BF16)
    router_grad = t_dot(d_logits, hidden_mine)
    d_hidden_two = expert_in + dot(d_logits, columns(router_w))
    gain_two_grad = jnp.sum(d_hidden_two * normed_two, axis=0)
    pull_two = d_hidden_two * gain_two
    mean_two = lax.psum(jnp.sum(pull_two * mixed, axis=1), "tp")[:, None] / width
    mean_two = end_x(mine - 1, mean_two)
    sums[mine - 1], mean_two = tie((sums[mine - 1], mean_two))
    start_z(mine - 1)
    d_mixed = (
        upstream_columns(column_at).astype(F32) + scale_two * pull_two - mixed * scale_two**3 * mean_two
    )

    d_branch = join(d_mixed.astype(BF16), 7)
    d_branch = end_z(mine - 1, d_branch)
    hidden_two, d_branch, far_down, mixture = tie((hidden_two, d_branch, far_down, mixture))
    output = lax.all_gather(mixed + mixture.astype(F32), "tp", axis=0, tiled=False)
    far_w = [far_both, far_both, far_down]
    d_attended = sum(dot_t(block(d_branch, s), w) for s, w in enumerate(out_w)).astype(BF16)
    out_grad = swap([t_dot(block(d_branch, s), attended).astype(BF16) for s in range(dp_count)])
    out_mine = t_dot(block(d_branch, 0), attended)
    d_all = to_heads((d_attended,), heads)[0]
    run(mine)
    start_x(mine)
    d_all, grads[mine][0], out_grad, output = tie((d_all, grads[mine][0], out_grad, output))
    out_grad = add([out_mine], out_grad)
    out_grad = lax.psum_scatter(out_grad, "ctx", scatter_dimension=0, tiled=True)
    dq_all, dk_all, dv_all = attend_back(lengths, q_all, k_all, v_all, d_all, log)
    def by_token(v):
        return v.transpose(1, 0, 2).reshape(pack, own_cols)

    d_q_normed = turn(by_token(dq_all), -sine).reshape(pack, own_cols)
    d_k_normed = turn(by_token(dk_all), -sine).reshape(pack, own_cols)
    q_pull, k_pull = d_q_normed * gain_q, d_k_normed * gain_k
    totals = share(
        jnp.stack([jnp.sum(q_pull * q_raw, axis=1), jnp.sum(k_pull * k_raw, axis=1)]), True, 6
    )
    q_mean, k_mean = totals[:, :, None] / width
    d_q_raw = (q_scale * q_pull - q_raw * q_scale**3 * q_mean).astype(BF16)
    d_k_raw = (k_scale * k_pull - k_raw * k_scale**3 * k_mean).astype(BF16)
    d_raw = jnp.concatenate([d_q_raw, d_k_raw, by_token(dv_all)], axis=1)
    heads_mine = t_dot(block(hidden_one, 0), d_raw)
    heads_grads = [t_dot(block(hidden_one, s), d_raw).astype(BF16) for s in range(dp_count)]
    heads_mine, heads_grads, d_raw, hidden_two, out_grad = tie(
        (heads_mine, heads_grads, d_raw, hidden_two, out_grad)
    )
    out_grad = lax.all_gather(out_grad, "ctx", axis=0, tiled=True)
    held = []

    def put(e):
        nonlocal held
        plane = ctx_at if e < mine else beside_at
        at = plane * mine + e % mine
        other = jnp.bitwise_xor(plane, 1) * mine + e % mine
        held = place_grads(
            jnp.stack([at, other]).astype(jnp.int32), sums[e], there[e], experts, held
        )

    for e in range(mine + 1, 2 * mine):
        run(e)
        if e > mine + 1:
            for i in range(2 * (e - mine - 2), 2 * (e - mine - 1)):
                there[i], grads[e] = tie((there[i], grads[e]))
                put(i)
        step = (hidden_two, d_raw, grads[e], held)
        if e > mine + 1:
            step = end_z(e - 2, step)
        step = end_x(e - 1, step)
        if e == mine + 1:
            out_grad, step = tie((out_grad, step))
        sums[e - 1], step = tie((sums[e - 1], step))
        hidden_two, d_raw, grads[e], held = step
        start_z(e - 1)
        if e < 2 * mine - 1:
            start_x(e)
    heads_grads, grads[2 * mine - 1] = tie((heads_grads, grads[2 * mine - 1]))
    start_x(2 * mine - 1)
    heads_grads = swap(heads_grads)
    (d_hidden,) = returns(
        [[d_raw]],
        [[w[None] for w in heads_w]],
        None,
        False,
        8,
    )
    d_hidden = end_z(2 * mine - 2, end_x(2 * mine - 1, d_hidden))
    heads_grads, out_grad, d_hidden = tie((heads_grads, out_grad, d_hidden))
    gain_one_grad = jnp.sum(d_hidden * inputs_c * scale_one, axis=0)
    heads_gains = lax.dynamic_update_slice_in_dim(
        jnp.zeros((2, local), F32),
        jnp.stack([jnp.sum(d_q_normed * q_hat, axis=0), jnp.sum(d_k_normed * k_hat, axis=0)]),
        ctx_at * own_cols,
        1,
    )
    small_grads = jnp.concatenate(
        [gain_one_grad[None], gain_two_grad[None], router_grad, heads_gains]
    )
    small_shape, across = small_grads.shape, 3 * own_cols
    small_count = small_grads.size
    small_rows = -(-small_count // (16 * across)) * 16
    small_grads = jnp.pad(
        small_grads.astype(BF16).reshape(-1), (0, small_rows * across - small_count)
    )
    heads_grads = add([heads_mine], heads_grads)
    heads_grads = jnp.concatenate([heads_grads, small_grads.reshape(small_rows, across)])
    heads_grads = lax.all_gather(heads_grads, "ctx", axis=0, tiled=False)
    start_z(2 * mine - 1)
    small_grads = heads_grads[:, wide:].astype(F32).sum(axis=0).reshape(-1)[:small_count]
    small_grads = lax.all_gather(small_grads.reshape(small_shape), "tp", axis=0, tiled=False)
    pull_one = d_hidden * columns(gain_one)
    mean_one = lax.psum(jnp.sum(pull_one * inputs_c, axis=1), "tp")[:, None] / width
    d_inputs = d_mixed + scale_one * pull_one - inputs_c * scale_one**3 * mean_one

    def whole(every):
        every = [every[(p % 2) * 2 + p // 2] for p in range(tp_count)]
        return natural(jnp.concatenate(every, axis=1))

    output = whole(output)
    d_inputs = join(d_inputs, 10)
    d_inputs = natural(d_inputs)
    turned = [small_grads[(p % 2) * 2 + p // 2, : 2 + experts] for p in range(tp_count)]
    heads_gains = small_grads[:, 2 + experts : 4 + experts].transpose(1, 0, 2).reshape(2, width)
    small_grads = jnp.concatenate([natural(jnp.concatenate(turned, axis=1)), heads_gains])
    small_grads = hand_over(
        [small_grads if s == 0 else small_grads for s in range(dp_count)]
    )
    small_grads = lax.dynamic_slice_in_dim(small_grads, dp_at * wide, wide, 1)

    def heads_grad(i):
        v = heads_grads[:, :wide, i * own_cols : (i + 1) * own_cols].astype(F32)
        return v.transpose(1, 0, 2).reshape(wide, local)

    for e in range(mine, 2 * mine - 1):
        there[e], d_hidden = tie((there[e], d_hidden))
    for e in range(mine, 2 * mine):
        put(e)
    return (
        output,
        d_inputs,
        small_grads[0],
        heads_grad(0),
        heads_grad(1),
        heads_grad(2),
        small_grads[2 + experts],
        small_grads[3 + experts],
        out_grad.astype(F32).T,
        small_grads[1],
        small_grads[2 : 2 + experts].T,
        held[0],
        held[1],
        held[2],
    )


def solution(mesh):
    in_specs = (
        P(("dp", "ctx"), None),
        P(("dp", "ctx"), None),
        P("dp", None),
        P(("dp", "ctx"), None),
        P("dp"),
        P("dp", "tp"),
        P("dp", "tp"),
        P("dp", "tp"),
        P("dp"),
        P("dp"),
        P("tp", "dp"),
        P("dp"),
        P("dp", None),
        P(None, "dp", "tp"),
        P(None, "dp", "tp"),
        P(None, "tp", "dp"),
    )
    out_specs = (
        P(("dp", "ctx"), None),
        P(("dp", "ctx"), None),
        P("dp"),
        P("dp", "tp"),
        P("dp", "tp"),
        P("dp", "tp"),
        P("dp"),
        P("dp"),
        P("tp", "dp"),
        P("dp"),
        P("dp", None),
        P(None, "dp", "tp"),
        P(None, "dp", "tp"),
        P(None, "tp", "dp"),
    )
    return jax.shard_map(body, mesh=mesh, in_specs=in_specs, out_specs=out_specs, check_vma=False)
```

```python
import functools

import jax
import jax.numpy as jnp
from jax import lax
from jax.experimental import pallas as pl
from jax.experimental.pallas import tpu as pltpu
from jax.sharding import PartitionSpec as P

HEAD = 128
EPS = 1e-05
THETA = 10000.0
BLOCK = 256
BF16 = jnp.bfloat16
F32 = jnp.float32
MESH = pl.DeviceIdType.MESH
MICRO = 1 << 26


def dot(a, b):
    return jnp.dot(a, b, preferred_element_type=F32)


def dot_t(a, b):
    return lax.dot_general(a, b, (((1,), (1,)), ((), ())), preferred_element_type=F32)


def t_dot(a, b):
    return lax.dot_general(a, b, (((0,), (0,)), ((), ())), preferred_element_type=F32)


def rotation(row, first, rows):
    ends = jnp.cumsum(row)
    index = first + jnp.arange(rows, dtype=jnp.int32)
    before = jnp.where(index[:, None] >= ends[None, :], ends[None, :], 0)
    position = index - jnp.max(before, axis=1)
    inverse = THETA ** (-jnp.arange(0, HEAD, 2).astype(F32) / HEAD)
    angle = position.astype(F32)[:, None] * inverse[None, :]
    cosine, sine = jnp.cos(angle), jnp.sin(angle)
    return (
        jnp.concatenate([cosine, cosine], axis=1)[:, None, :],
        jnp.concatenate([-sine, sine], axis=1)[:, None, :],
    )


def rotate(v, cosine, sine):
    return v * cosine + jnp.roll(v, HEAD // 2, axis=2) * sine


def allowed_block(lengths_ref, base, rows, columns):
    index = base + lax.broadcasted_iota(jnp.int32, (rows, 1), 0)
    start = jnp.zeros((rows, 1), jnp.int32)
    end = 0
    for at in range(lengths_ref.shape[1]):
        end = end + lengths_ref[0, at]
        start = jnp.where(index >= end, end, start)
    key = lax.broadcasted_iota(jnp.int32, (rows, columns), 1)
    return (key >= start) & (key <= index)


def attend_kernel(lengths_ref, q_ref, k_ref, v_ref, out_ref, log_ref):
    scale = HEAD ** (-0.5)
    rows = q_ref.shape[0]
    for base in range(0, rows, BLOCK):
        upto = base + BLOCK
        own = pl.ds(base, BLOCK)
        keys, values = k_ref[pl.ds(0, upto), :], v_ref[pl.ds(0, upto), :]
        scores = dot_t(q_ref[own, :], keys) * scale
        scores = jnp.where(allowed_block(lengths_ref, base, BLOCK, upto), scores, -1e30)
        top = jnp.max(scores, axis=1, keepdims=True)
        weights = jnp.exp(scores - top)
        total = jnp.sum(weights, axis=1, keepdims=True)
        probs = (weights * (1.0 / total)).astype(BF16)
        out_ref[own, :] = dot(probs, values).astype(BF16)
        log_ref[own, :] = top + jnp.log(total)


def attend(lengths, q, k, v):
    heads, rows, _ = q.shape
    spec = pl.BlockSpec((None, rows, HEAD), lambda h: (h, 0, 0))
    column = pl.BlockSpec((None, rows, 1), lambda h: (h, 0, 0))
    return pl.pallas_call(
        attend_kernel,
        cost_estimate=pl.CostEstimate(flops=7 * MICRO, bytes_accessed=0, transcendentals=0),
        grid=(heads,),
        out_shape=(
            jax.ShapeDtypeStruct((heads, rows, HEAD), BF16),
            jax.ShapeDtypeStruct((heads, rows, 1), F32),
        ),
        in_specs=[pl.BlockSpec(memory_space=pltpu.SMEM), spec, spec, spec],
        out_specs=(spec, column),
        compiler_params=pltpu.CompilerParams(vmem_limit_bytes=48 << 20),
    )(lengths, q, k, v)


def attend_back_kernel(
    lengths_ref, q_ref, k_ref, v_ref, d_ref, log_ref, dq_ref, dk_ref, dv_ref, dk_sum, dv_sum
):
    scale = HEAD ** (-0.5)
    rows = q_ref.shape[0]
    dk_sum[...] = jnp.zeros_like(dk_sum)
    dv_sum[...] = jnp.zeros_like(dv_sum)
    for base in range(0, rows, BLOCK):
        upto = base + BLOCK
        own, seen = pl.ds(base, BLOCK), pl.ds(0, upto)
        q, d = q_ref[own, :], d_ref[own, :]
        keys, values = k_ref[seen, :], v_ref[seen, :]
        scores = dot_t(q, keys) * scale - log_ref[own, :]
        probs = jnp.where(
            allowed_block(lengths_ref, base, BLOCK, upto), jnp.exp(scores), 0.0
        )
        d_probs = dot_t(d, values)
        delta = jnp.sum(probs * d_probs, axis=1, keepdims=True)
        d_raw = (probs * (d_probs - delta) * scale).astype(BF16)
        dq_ref[own, :] = dot(d_raw, keys).astype(dq_ref.dtype)
        dk_sum[seen, :] += t_dot(d_raw, q)
        dv_sum[seen, :] += t_dot(probs.astype(BF16), d)
    dk_ref[...] = dk_sum[...].astype(dk_ref.dtype)
    dv_ref[...] = dv_sum[...].astype(dv_ref.dtype)


def attend_back(lengths, q, k, v, d, log):
    heads, rows, _ = q.shape
    spec = pl.BlockSpec((None, rows, HEAD), lambda h: (h, 0, 0))
    column = pl.BlockSpec((None, rows, 1), lambda h: (h, 0, 0))
    return pl.pallas_call(
        attend_back_kernel,
        cost_estimate=pl.CostEstimate(flops=10 * MICRO, bytes_accessed=0, transcendentals=0),
        grid=(heads,),
        out_shape=(jax.ShapeDtypeStruct((heads, rows, HEAD), F32),) * 2
        + (jax.ShapeDtypeStruct((heads, rows, HEAD), BF16),),
        in_specs=[pl.BlockSpec(memory_space=pltpu.SMEM), spec, spec, spec, spec, column],
        out_specs=(spec,) * 3,
        scratch_shapes=[pltpu.VMEM((rows, HEAD), F32)] * 2,
        compiler_params=pltpu.CompilerParams(vmem_limit_bytes=48 << 20),
    )(lengths, q, k, v, d, log)


def to_heads(parts, heads):
    count = lax.axis_size("ctx")
    rows = parts[0].shape[0]
    stacked = jnp.stack([p.reshape(rows, count, heads // count, HEAD) for p in parts])
    sent = stacked.transpose(2, 0, 3, 1, 4)
    got = lax.all_to_all(sent, "ctx", 0, 0, tiled=True)
    return got.transpose(1, 2, 0, 3, 4).reshape(len(parts), heads // count, count * rows, HEAD)


def to_rows(parts):
    count = lax.axis_size("ctx")
    mine, pack, _ = parts[0].shape
    stacked = jnp.stack([p.reshape(mine, count, pack // count, HEAD) for p in parts])
    sent = stacked.transpose(2, 0, 1, 3, 4)
    got = lax.all_to_all(sent, "ctx", 0, 0, tiled=True)
    turned = got.transpose(1, 3, 0, 2, 4)
    return turned.reshape(len(parts), pack // count, count * mine, HEAD)


def carried(axes, sources, targets, sems):
    d, count = lax.axis_index("dp"), lax.axis_size("dp")
    copies = []
    for i, axis in enumerate(axes):
        pair = (sems[2 * i], sems[2 * i + 1])
        if axis == "z":
            partner = {"ctx": jnp.bitwise_xor(lax.axis_index("ctx"), 1)}
            copies.append(remote(sources[i], targets[i], pair, 0, partner))
            continue
        for s in range(1, count):
            source = sources[i].at[s - 1] if axis == "x" else sources[i]
            partner = {"dp": lax.rem(d + (s if axis == "x" else count - s), count)}
            copies.append(remote(source, targets[i].at[s - 1], pair, s - 1, partner))
    partners = []
    if any(axis != "z" for axis in axes):
        partners = [({"dp": lax.rem(d + s, count)}, d >= 0) for s in range(1, count)]
    return copies, partners


def beside():
    return [({"ctx": jnp.bitwise_xor(lax.axis_index("ctx"), 1)}, lax.axis_index("ctx") >= 0)]


def carry_operands(carry):
    dma, count = pltpu.SemaphoreType.DMA, lax.axis_size("dp")
    shapes, sems = [], []
    for axis, v in carry:
        shape = (count - 1,) + v.shape if axis == "w" else v.shape
        shapes.append(jax.ShapeDtypeStruct(shape, v.dtype))
        sems += [dma((1 if axis == "z" else count - 1,))] * 2
    return [v for _, v in carry], shapes, sems


def expert_kernel(blocks, number, far, mine, full, axes, *refs):
    refs = list(refs)

    def take(count):
        return [refs.pop(0) for _ in range(count)]

    hidden_ref, up_ref, chosen_ref, router_ref = take(4)
    gate_w, up_w, down_w = take(blocks), take(blocks), take(blocks)
    sources = take(len(axes))
    if full:
        inner_ref, dgate_ref, dup_ref, dots_ref = take(4)
    near_ref, others_ref = take(2)
    targets = take(len(axes))
    gate_sum, up_sum, down_sum = take(3)
    sems = take(2 * len(axes))
    turn, last = pl.program_id(0), pl.num_programs(0) - 1
    wide = gate_w[0].shape[0]

    def transfers():
        return carried(axes, sources, targets, sems)

    if axes:

        @pl.when(turn == 0)
        def _():
            copies, partners = transfers()
            signal_all(partners + (beside() if "z" in axes else []))
            for copy in copies:
                copy.start()

    hidden, upstream = hidden_ref[...], up_ref[...]

    def over(v, ws, f):
        return sum(f(v[:, s * wide : (s + 1) * wide], w[...]) for s, w in enumerate(ws))

    gate, up = over(hidden, gate_w, dot), over(hidden, up_w, dot)
    pulled = over(upstream, down_w, dot_t)
    logits = dot_t(hidden, router_ref[...])
    odds = jnp.exp(logits - jnp.max(logits, axis=1, keepdims=True))
    probs = odds / jnp.sum(odds, axis=1, keepdims=True) * chosen_ref[...]
    plane = lax.axis_index("ctx")
    if far:
        plane = jnp.bitwise_xor(plane, 2)
    named = lax.broadcasted_iota(jnp.int32, probs.shape, 1) == plane * mine + number
    weight = jnp.sum(jnp.where(named, probs, 0.0), axis=1, keepdims=True)
    sigma = jax.nn.sigmoid(gate)
    active = gate * sigma
    inner = (active * up).astype(BF16).astype(F32)
    if full:
        dots = jnp.sum(inner * pulled, axis=1, keepdims=True)
        dots_ref[...] = jnp.where(weight > 0.0, dots, 0.0)
    inner = (weight * inner).astype(BF16)
    pulled = weight * pulled
    d_gate = (pulled * up * sigma * (1.0 + gate * (1.0 - sigma))).astype(BF16)
    d_up = (pulled * active).astype(BF16)
    if full:
        inner_ref[...], dgate_ref[...], dup_ref[...] = inner, d_gate, d_up

    @pl.when(turn == 0)
    def _():
        gate_sum[...] = t_dot(d_gate, hidden)
        up_sum[...] = t_dot(d_up, hidden)
        down_sum[...] = t_dot(inner, upstream)

    @pl.when(turn > 0)
    def _():
        gate_sum[...] += t_dot(d_gate, hidden)
        up_sum[...] += t_dot(d_up, hidden)
        down_sum[...] += t_dot(inner, upstream)

    @pl.when(turn == last)
    def _():
        fine = down_sum.shape[0]
        for s in range(blocks):
            target = near_ref if s == 0 else others_ref.at[s - 1]
            own = pl.ds(s * wide, wide)
            target[0] = gate_sum[:, own].T.astype(BF16)
            target[1] = up_sum[:, own].T.astype(BF16)
            for j in range(wide // fine):
                target[2, pl.ds(j * fine, fine), :] = down_sum[
                    :, pl.ds(s * wide + j * fine, fine)
                ].astype(BF16)
        if axes:
            for copy in transfers()[0]:
                copy.wait()


def expert(e, hidden, upstream, chosen, router, weights, far, full, carry, ident, tile=512):
    gate_w, up_w, down_w = weights
    blocks = len(gate_w)
    pack, width = hidden.shape
    mine, fine, wide = down_w[0].shape
    first = up_w[0].shape[0] - mine
    operands, shapes, sems = carry_operands(carry)
    hbm = pl.BlockSpec(memory_space=pl.ANY)

    def token(n):
        return pl.BlockSpec((tile, n), lambda i: (i, 0))

    def weight(first, *shape):
        return pl.BlockSpec((None,) + shape, lambda i: (first + e, 0, 0))

    near = pl.BlockSpec((3, wide, fine), lambda i: (0, 0, 0))
    others = pl.BlockSpec((blocks - 1, 3, wide, fine), lambda i: (0, 0, 0, 0))
    out_specs, out_shape = [near, others], [
        jax.ShapeDtypeStruct((3, wide, fine), BF16),
        jax.ShapeDtypeStruct((blocks - 1, 3, wide, fine), BF16),
    ]
    if full:
        out_specs = [token(fine)] * 3 + [token(1)] + out_specs
        out_shape = (
            [jax.ShapeDtypeStruct((pack, fine), BF16)] * 3
            + [jax.ShapeDtypeStruct((pack, 1), F32)]
            + out_shape
        )
    remote_params = dict(collective_id=ident, has_side_effects=True) if carry else {}
    return pl.pallas_call(
        functools.partial(expert_kernel, blocks, e, far, mine, full, [axis for axis, _ in carry]),
        cost_estimate=pl.CostEstimate(flops=27 * MICRO, bytes_accessed=0, transcendentals=0),
        grid=(pack // tile,),
        in_specs=[token(width), token(width), token(chosen.shape[1])]
        + [pl.BlockSpec(router.shape, lambda i: (0, 0))]
        + [weight(0, wide, fine)] * blocks
        + [weight(first, wide, fine)] * blocks
        + [weight(0, fine, wide)] * blocks
        + [hbm] * len(operands),
        out_specs=out_specs + [hbm] * len(shapes),
        out_shape=out_shape + shapes,
        scratch_shapes=[pltpu.VMEM((fine, width), F32)] * 3 + sems,
        compiler_params=pltpu.CompilerParams(vmem_limit_bytes=56 << 20, **remote_params),
    )(hidden, upstream, chosen, router, *gate_w, *up_w, *down_w, *operands)


def signal_all(partners):
    barrier = pltpu.get_barrier_semaphore()
    count = 0
    for device, there in partners:

        @pl.when(there)
        def _():
            pl.semaphore_signal(barrier, inc=1, device_id=device, device_id_type=MESH)

        count = count + jnp.where(there, 1, 0)
    pl.semaphore_wait(barrier, count)


def place():
    c, t = lax.axis_index("ctx"), lax.axis_index("tp")
    core, side = lax.rem(t, 2), t // 2
    over_core = {"tp": t + 1 - 2 * core}
    over_side = {"tp": t + 2 - 4 * side}
    return c, lax.axis_size("ctx"), core, side, over_core, over_side


def remote(source, target, sems, at, device):
    send, recv = sems
    return pltpu.make_async_remote_copy(
        src_ref=source,
        dst_ref=target,
        send_sem=send.at[at],
        recv_sem=recv.at[at],
        device_id=device,
        device_id_type=MESH,
    )


def spread_kernel(axes, x_ref, *refs):
    count = len(axes)
    sources, out_ref, targets = refs[:count], refs[count], refs[count + 1 : 2 * count + 1]
    local, zs, zr, ys, yr, cs, cr = refs[2 * count + 1 : 2 * count + 8]
    moving, more = carried(axes, sources, targets, refs[2 * count + 8 :])
    c, n, core, side, over_core, over_side = place()
    rows, part = x_ref.shape
    left, right = {"ctx": c - 1}, {"ctx": c + 1}
    signal_all(
        [(left, c > 0), (right, c < n - 1), (over_core, c >= 0), (over_side, c >= 0)] + more
    )
    for copy in moving:
        copy.start()
    mine = core * 2 + side
    other = core * 2 + 1 - side

    def tile(owner, column):
        return out_ref.at[
            pl.ds(pl.multiple_of(owner * rows, rows), rows),
            pl.ds(pl.multiple_of(column * part, part), part),
        ]

    def along(owner, source, target, at):
        return remote(source, tile(owner, mine), (zs, zr), at, target)

    keep = pltpu.make_async_copy(x_ref, tile(c, mine), local)
    keep.start()

    @pl.when(c > 0)
    def _():
        along(c, x_ref, left, n + c).start()

    @pl.when(c < n - 1)
    def _():
        along(c, x_ref, right, c).start()

    def to_side(owner, source):
        return remote(source, tile(owner, mine), (ys, yr), owner, over_side)

    def to_core(owner, column, source, which):
        return remote(source, tile(owner, column), (cs, cr), which * n + owner, over_core)

    to_side(c, x_ref).start()
    to_core(c, mine, x_ref, 0).start()

    def from_side(owner):
        here = tile(owner, other)
        remote(here, here, (ys, yr), owner, over_side).wait_recv()
        to_core(owner, other, here, 1).start()

    from_side(c)
    for far in range(1, n):
        for sign, there, onward, more in (
            (-1, c - far >= 0, right, c < n - 1),
            (1, c + far < n, left, c > 0),
        ):
            owner = c + sign * far
            slot = owner if sign < 0 else n + owner

            @pl.when(there)
            def _():
                here = tile(owner, mine)
                along(owner, here, onward, slot).wait_recv()

                @pl.when(more)
                def _():
                    along(owner, here, onward, slot).start()

                to_side(owner, here).start()
                to_core(owner, mine, here, 0).start()

        for sign, there in ((-1, c - far >= 0), (1, c + far < n)):

            @pl.when(there)
            def _():
                from_side(c + sign * far)

    keep.wait()

    @pl.when(c > 0)
    def _():
        along(c, x_ref, left, n + c).wait_send()

    @pl.when(c < n - 1)
    def _():
        along(c, x_ref, right, c).wait_send()

    for far in range(1, n):
        for sign, there, onward, more in (
            (-1, c - far >= 0, right, c < n - 1),
            (1, c + far < n, left, c > 0),
        ):
            owner = c + sign * far

            @pl.when(there & more)
            def _():
                here = tile(owner, mine)
                along(owner, here, onward, owner if sign < 0 else n + owner).wait_send()

    for owner in range(n):
        to_side(owner, tile(owner, mine)).wait_send()
        to_core(owner, mine, tile(owner, mine), 0).wait_send()
        to_core(owner, other, tile(owner, other), 1).wait_send()
        for which, column in ((0, (1 - core) * 2 + side), (1, (1 - core) * 2 + 1 - side)):
            here = tile(owner, column)
            remote(here, here, (cs, cr), which * n + owner, over_core).wait_recv()
    for copy in moving:
        copy.wait()


def spread(v, ident, carry=()):
    operands, shapes, sems = carry_operands(carry)
    hbm = pl.BlockSpec(memory_space=pl.ANY)
    n, tp = lax.axis_size("ctx"), lax.axis_size("tp")
    rows, part = v.shape
    dma = pltpu.SemaphoreType.DMA
    return pl.pallas_call(
        functools.partial(spread_kernel, [axis for axis, _ in carry]),
        cost_estimate=pl.CostEstimate(flops=60 * MICRO, bytes_accessed=0, transcendentals=0),
        out_shape=[jax.ShapeDtypeStruct((n * rows, tp * part), v.dtype)] + shapes,
        in_specs=[hbm] * (1 + len(shapes)),
        out_specs=[hbm] * (1 + len(shapes)),
        scratch_shapes=[dma]
        + [dma((2 * n,))] * 2
        + [dma((n,))] * 2
        + [dma((2 * n,))] * 2
        + sems,
        compiler_params=pltpu.CompilerParams(collective_id=ident, has_side_effects=True),
    )(v, *operands)


def join_kernel(x_ref, out_ref, local, ss, sr):
    c, n, core, side, over_core, over_side = place()
    rows, part = x_ref.shape
    signal_all([(over_core, c >= 0), (over_side, c >= 0)])
    mine, other = core * 2 + side, core * 2 + 1 - side

    def tile(column):
        return out_ref.at[:, pl.ds(pl.multiple_of(column * part, part), part)]

    keep = pltpu.make_async_copy(x_ref, tile(mine), local)
    keep.start()
    first = remote(x_ref, tile(mine), (ss, sr), 0, over_side)
    first.start()
    second = remote(x_ref, tile(mine), (ss, sr), 1, over_core)
    second.start()
    first.wait_recv()
    third = remote(tile(other), tile(other), (ss, sr), 2, over_core)
    third.start()
    keep.wait()
    first.wait_send()
    second.wait()
    third.wait()


def join(v, ident):
    tp = lax.axis_size("tp")
    rows, part = v.shape
    dma = pltpu.SemaphoreType.DMA
    return pl.pallas_call(
        join_kernel,
        cost_estimate=pl.CostEstimate(flops=25 * MICRO, bytes_accessed=0, transcendentals=0),
        out_shape=jax.ShapeDtypeStruct((rows, tp * part), v.dtype),
        in_specs=[pl.BlockSpec(memory_space=pl.ANY)],
        out_specs=pl.BlockSpec(memory_space=pl.ANY),
        scratch_shapes=[dma] + [dma((3,))] * 2,
        compiler_params=pltpu.CompilerParams(collective_id=ident, has_side_effects=True),
    )(v)


def collect_kernel(
    owners, x_ref, out_ref, core_in, side_out, side_in, z_out, z_in, cs, cr, ys, yr, zs, zr
):
    c, n, core, side, over_core, over_side = place()
    rows, part = out_ref.shape
    left, right = {"ctx": c - 1}, {"ctx": c + 1}
    partners = [(over_core, c >= 0), (over_side, c >= 0)]
    if owners > 1:
        partners += [(left, c > 0), (right, c < n - 1)]
    signal_all(partners)

    def owner_of(i):
        if owners == 1:
            return 0
        owner = 0
        for at in range(n):
            for turn, far in enumerate(sorted(range(n), key=lambda o: -abs(o - at))):
                owner = jnp.where((c == at) & (i == turn), far, owner)
        return owner

    def own_rows(owner):
        return pl.ds(pl.multiple_of(owner * rows, rows), rows)

    def half(which):
        return pl.ds(pl.multiple_of(which * 2 * part, 2 * part), 2 * part)

    def quarter(which):
        return pl.ds(pl.multiple_of((core * 2 + which) * part, part), part)

    def to_core(i):
        source = x_ref.at[own_rows(owner_of(i)), half(1 - core)]
        return remote(source, core_in.at[i], (cs, cr), i, over_core)

    def to_side(i):
        return remote(side_out.at[i], side_in.at[i], (ys, yr), i, over_side)

    def to_left(owner):
        return remote(z_out.at[owner], z_in.at[1, owner], (zs, zr), n + owner, left)

    def to_right(owner):
        return remote(z_out.at[owner], z_in.at[0, owner], (zs, zr), owner, right)

    def from_core(i, which):
        local = x_ref[own_rows(owner_of(i)), quarter(which)].astype(F32)
        near = core_in[i, :, pl.ds(pl.multiple_of(which * part, part), part)]
        return local + near.astype(F32)

    for i in range(owners):
        to_core(i).start()

    def finish(i):
        to_side(i).wait_recv()
        owner = owner_of(i)
        total = from_core(i, side) + side_in[i].astype(F32)
        if owners == 1:
            out_ref[...] = total
            return

        @pl.when(owner > c)
        def _():
            @pl.when(c > 0)
            def _():
                to_right(owner).wait_recv()
                z_out[owner] = (total + z_in[0, owner].astype(F32)).astype(z_out.dtype)

            @pl.when(c == 0)
            def _():
                z_out[owner] = total.astype(z_out.dtype)

            to_right(owner).start()

        @pl.when(owner < c)
        def _():
            @pl.when(c < n - 1)
            def _():
                to_left(owner).wait_recv()
                z_out[owner] = (total + z_in[1, owner].astype(F32)).astype(z_out.dtype)

            @pl.when(c == n - 1)
            def _():
                z_out[owner] = total.astype(z_out.dtype)

            to_left(owner).start()

        @pl.when(owner == c)
        def _():
            out_ref[...] = total

    def step(i, carry):
        @pl.when(i < owners)
        def _():
            to_core(i).wait_recv()
            side_out[i] = from_core(i, 1 - side).astype(side_out.dtype)
            to_side(i).start()

        @pl.when(i > 0)
        def _():
            finish(i - 1)

        return carry

    lax.fori_loop(0, owners + 1, step, 0)

    if owners > 1:

        @pl.when(c > 0)
        def _():
            to_right(c).wait_recv()
            out_ref[...] += z_in[0, c].astype(F32)

        @pl.when(c < n - 1)
        def _():
            to_left(c).wait_recv()
            out_ref[...] += z_in[1, c].astype(F32)

    def close(i, carry):
        to_core(i).wait_send()
        to_side(i).wait_send()
        if owners > 1:
            owner = owner_of(i)

            @pl.when(owner > c)
            def _():
                to_right(owner).wait_send()

            @pl.when(owner < c)
            def _():
                to_left(owner).wait_send()

        return carry

    lax.fori_loop(0, owners, close, 0)


def collect(v, owners, ident):
    n, tp = lax.axis_size("ctx"), lax.axis_size("tp")
    rows, part = v.shape[0] // owners, v.shape[1] // tp
    dma = pltpu.SemaphoreType.DMA
    z = n if owners > 1 else 1
    return pl.pallas_call(
        functools.partial(collect_kernel, owners),
        cost_estimate=pl.CostEstimate(flops=17 * MICRO, bytes_accessed=0, transcendentals=0),
        out_shape=jax.ShapeDtypeStruct((rows, part), F32),
        in_specs=[pl.BlockSpec(memory_space=pltpu.VMEM)],
        out_specs=pl.BlockSpec(memory_space=pltpu.VMEM),
        scratch_shapes=[
            pltpu.VMEM((owners, rows, 2 * part), BF16),
            pltpu.VMEM((owners, rows, part), BF16),
            pltpu.VMEM((owners, rows, part), BF16),
            pltpu.VMEM((z, rows, part), BF16),
            pltpu.VMEM((2, z, rows, part), BF16),
        ]
        + [dma((owners,))] * 4
        + [dma((2 * z,))] * 2,
        compiler_params=pltpu.CompilerParams(
            collective_id=ident, has_side_effects=True, vmem_limit_bytes=48 << 20
        ),
    )(v)


def returns_kernel(kinds, mine, blocks, flipped, with_dots, axes, *refs):
    refs = list(refs)

    def take(count):
        return [refs.pop(0) for _ in range(count)]

    lhs_refs, weight_refs = take(kinds * mine), take(kinds * blocks)
    dots_ref = take(1)[0] if with_dots else None
    sources = take(len(axes))
    out_ref = take(1)[0]
    dots_out = take(1)[0] if with_dots else None
    targets = take(len(axes))
    lhs, weights, core_out, core_in, keep, near, side_out, side_in, z_out, z_in = take(10)
    ls, ws, cs, cr, ys, yr, zs, zr = take(8)
    dots_in, ds, dr = take(3) if with_dots else (None, None, None)
    moving, more = carried(axes, sources, targets, take(2 * len(axes)))
    c, n, core, side, over_core, over_side = place()
    t, tp = lax.axis_index("tp"), lax.axis_size("tp")
    rows, part = out_ref.shape
    fine = lhs_refs[0].shape[1]
    wide = out_ref.shape[1] * tp // blocks
    half_blocks = blocks // 2
    left, right = {"ctx": c - 1}, {"ctx": c + 1}

    loads = []
    for k in range(kinds):
        for e in range(mine):
            at = k * mine + e
            columns = pl.ds(at * fine, fine)
            loads.append(pltpu.make_async_copy(lhs_refs[at], lhs.at[:, columns], ls.at[at]))
            for s in range(blocks):
                source = weight_refs[k * blocks + s].at[e]
                target = weights.at[s, columns, :] if flipped else weights.at[s, :, columns]
                loads.append(pltpu.make_async_copy(source, target, ws.at[at * blocks + s]))
    for load in loads:
        load.start()
    if with_dots:
        others = []
        for far_c in range(n):
            for far_t in range(tp):
                others.append(({"ctx": far_c, "tp": far_t}, (c != far_c) | (t != far_t)))
    else:
        others = [(over_core, c >= 0), (over_side, c >= 0), (left, c > 0), (right, c < n - 1)]
    others += more
    signal_all(others)
    for copy in moving:
        copy.start()

    def own_rows(owner):
        return pl.ds(pl.multiple_of(owner * rows, rows), rows)

    def dots_copy(owner, far_t):
        source = dots_ref.at[:, own_rows(owner)]
        return pltpu.make_async_remote_copy(
            src_ref=source,
            dst_ref=dots_in.at[c * tp + t],
            send_sem=ds.at[owner * tp + far_t],
            recv_sem=dr.at[c * tp + t],
            device_id={"ctx": owner, "tp": far_t},
            device_id_type=MESH,
        )

    def dots_from(at):
        here = dots_in.at[at]
        return pltpu.make_async_remote_copy(
            src_ref=here,
            dst_ref=here,
            send_sem=ds.at[at],
            recv_sem=dr.at[at],
            device_id=over_core,
            device_id_type=MESH,
        )

    if with_dots:
        for owner in range(n):
            for far_t in range(tp):

                @pl.when((c != owner) | (t != far_t))
                def _():
                    dots_copy(owner, far_t).start()

        dots_in[c * tp + t] = dots_ref[:, own_rows(c)]

    for load in loads:
        load.wait()

    def owner_of(i):
        owner = 0
        for at in range(n):
            for turn, far in enumerate(sorted(range(n), key=lambda o: -abs(o - at))):
                owner = jnp.where((c == at) & (i == turn), far, owner)
        return owner

    def to_core(i):
        return remote(core_out.at[i], core_in.at[i], (cs, cr), i, over_core)

    def to_side(i):
        return remote(side_out.at[i], side_in.at[i], (ys, yr), i, over_side)

    def to_left(owner):
        return remote(z_out.at[owner], z_in.at[1, owner], (zs, zr), n + owner, left)

    def to_right(owner):
        return remote(z_out.at[owner], z_in.at[0, owner], (zs, zr), owner, right)

    def product(i, which, into):
        taken = lhs[own_rows(owner_of(i)), :]
        for j in range(half_blocks):
            w = weights[which * half_blocks + j]
            into(j, dot(taken, w) if flipped else dot_t(taken, w))

    def columns_of(j):
        return pl.ds(j * wide, wide)

    def quarter(which):
        return pl.ds(pl.multiple_of(which * part, part), part)

    def begin(i):
        def send_part(j, v):
            core_out[i, :, columns_of(j)] = v.astype(core_out.dtype)

        def keep_part(j, v):
            keep[lax.rem(i, 2), :, columns_of(j)] = v

        product(i, 1 - core, send_part)
        to_core(i).start()
        product(i, core, keep_part)

    def cross(i):
        to_core(i).wait_recv()
        slot = lax.rem(i, 2)

        def summed(which):
            return keep[slot, :, quarter(which)] + core_in[i, :, quarter(which)].astype(F32)

        side_out[i] = summed(1 - side).astype(side_out.dtype)
        to_side(i).start()
        near[slot] = summed(side)

    def finish(i):
        to_side(i).wait_recv()
        owner = owner_of(i)
        total = near[lax.rem(i, 2)] + side_in[i].astype(F32)

        @pl.when(owner > c)
        def _():
            @pl.when(c > 0)
            def _():
                to_right(owner).wait_recv()
                z_out[owner] = (total + z_in[0, owner].astype(F32)).astype(z_out.dtype)

            @pl.when(c == 0)
            def _():
                z_out[owner] = total.astype(z_out.dtype)

            to_right(owner).start()

        @pl.when(owner < c)
        def _():
            @pl.when(c < n - 1)
            def _():
                to_left(owner).wait_recv()
                z_out[owner] = (total + z_in[1, owner].astype(F32)).astype(z_out.dtype)

            @pl.when(c == n - 1)
            def _():
                z_out[owner] = total.astype(z_out.dtype)

            to_left(owner).start()

        @pl.when(owner == c)
        def _():
            out_ref[...] = total

    def step(i, carry):
        @pl.when(i < n)
        def _():
            begin(i)

        @pl.when(i > 1)
        def _():
            finish(i - 2)

        @pl.when((i > 0) & (i <= n))
        def _():
            cross(i - 1)

        return carry

    lax.fori_loop(0, n + 2, step, 0)

    @pl.when(c > 0)
    def _():
        to_right(c).wait_recv()
        out_ref[...] += z_in[0, c].astype(F32)

    @pl.when(c < n - 1)
    def _():
        to_left(c).wait_recv()
        out_ref[...] += z_in[1, c].astype(F32)

    if with_dots:
        for at in range(n * tp):

            @pl.when(c * tp + t != at)
            def _():
                dots_from(at).wait_recv()

        for at in range(n):
            dots_out[at] = sum(dots_in[at * tp + far_t] for far_t in range(tp))
        for owner in range(n):
            for far_t in range(tp):

                @pl.when((c != owner) | (t != far_t))
                def _():
                    dots_copy(owner, far_t).wait_send()

    def close(i, carry):
        to_core(i).wait_send()
        to_side(i).wait_send()
        owner = owner_of(i)

        @pl.when(owner > c)
        def _():
            to_right(owner).wait_send()

        @pl.when(owner < c)
        def _():
            to_left(owner).wait_send()

        return carry

    lax.fori_loop(0, n, close, 0)
    for copy in moving:
        copy.wait()


def returns(lhs, weights, dots, flipped, ident, carry=()):
    n, tp = lax.axis_size("ctx"), lax.axis_size("tp")
    kinds, mine = len(lhs), len(lhs[0])
    blocks = len(weights[0])
    pack, fine = lhs[0][0].shape
    wide = weights[0][0].shape[2 if flipped else 1]
    rows, part = pack // n, wide * blocks // tp
    deep = kinds * mine * fine
    dma, vmem = pltpu.SemaphoreType.DMA, pltpu.VMEM
    hbm = pl.BlockSpec(memory_space=pl.ANY)
    near = pl.BlockSpec(memory_space=pltpu.VMEM)
    operands = [v for kind in lhs for v in kind] + [w for kind in weights for w in kind]
    in_specs = [hbm] * len(operands)
    out_shape = [jax.ShapeDtypeStruct((rows, part), F32)]
    extra = []
    if dots is not None:
        operands.append(dots)
        in_specs.append(near)
        out_shape.append(jax.ShapeDtypeStruct((n, mine, rows), F32))
        extra = [vmem((n * tp, mine, rows), F32), dma((n * tp,)), dma((n * tp,))]
    carried_in, shapes, sems = carry_operands(carry)
    axes = [axis for axis, _ in carry]
    return pl.pallas_call(
        functools.partial(
            returns_kernel, kinds, mine, blocks, flipped, dots is not None, axes
        ),
        cost_estimate=pl.CostEstimate(flops=65 * MICRO, bytes_accessed=0, transcendentals=0),
        out_shape=out_shape + shapes,
        in_specs=in_specs + [hbm] * len(shapes),
        out_specs=[near] * len(out_shape) + [hbm] * len(shapes),
        scratch_shapes=[
            vmem((pack, deep), BF16),
            vmem((blocks, deep, wide) if flipped else (blocks, wide, deep), BF16),
            vmem((n, rows, 2 * part), BF16),
            vmem((n, rows, 2 * part), BF16),
            vmem((2, rows, 2 * part), F32),
            vmem((2, rows, part), F32),
            vmem((n, rows, part), BF16),
            vmem((n, rows, part), BF16),
            vmem((n, rows, part), BF16),
            vmem((2, n, rows, part), BF16),
            dma((kinds * mine,)),
            dma((kinds * mine * blocks,)),
        ]
        + [dma((n,))] * 4
        + [dma((2 * n,))] * 2
        + extra
        + sems,
        compiler_params=pltpu.CompilerParams(
            collective_id=ident, has_side_effects=True, vmem_limit_bytes=56 << 20
        ),
    )(*operands, *carried_in)


def mixture_kernel(blocks, tp, *refs):
    inner_refs, out_ref = refs[: -1 - blocks], refs[-1]
    weights = refs[-1 - blocks : -1]
    wide, part = weights[0].shape[2], out_ref.shape[2]
    step = min(wide, part)
    inners = [r[...] for r in inner_refs]
    for start in range(0, wide * blocks, step):
        s, here = start // wide, pl.ds(start % wide, step)
        total = sum(dot(v, weights[s][e, :, here]) for e, v in enumerate(inners))
        column = start // part
        out_ref[(column % 2) * 2 + column // 2, :, pl.ds(start % part, step)] = total.astype(BF16)


def mixture_parts(inners, weights, tp, tile=512):
    pack, fine = inners[0].shape
    mine, blocks = len(inners), len(weights)
    wide = weights[0].shape[2]
    part = wide * blocks // tp
    return pl.pallas_call(
        functools.partial(mixture_kernel, blocks, tp),
        cost_estimate=pl.CostEstimate(flops=15 * MICRO, bytes_accessed=0, transcendentals=0),
        grid=(pack // tile,),
        in_specs=[pl.BlockSpec((tile, fine), lambda i: (i, 0))] * mine
        + [pl.BlockSpec((mine, fine, wide), lambda i: (0, 0, 0))] * blocks,
        out_specs=pl.BlockSpec((tp, tile, part), lambda i: (0, i, 0)),
        out_shape=jax.ShapeDtypeStruct((tp, pack, part), BF16),
        compiler_params=pltpu.CompilerParams(vmem_limit_bytes=48 << 20),
    )(*inners, *weights)


def place_kernel(at_ref, near_ref, far_ref, *refs):
    gate_ref, up_ref, down_ref = refs[-3:]
    fine, wide = down_ref.shape

    def write(source):
        gate_ref[...] = source[0].astype(F32)
        up_ref[...] = source[1].astype(F32)
        for j in range(wide // fine):
            down_ref[:, pl.ds(j * fine, fine)] = source[2, pl.ds(j * fine, fine), :].astype(F32)

    pl.when(pl.program_id(0) == 0)(lambda: write(near_ref))
    pl.when(pl.program_id(0) == 1)(lambda: write(far_ref))


def place_grads(at, near, far, experts, held):
    _, wide, fine = near.shape
    source = pl.BlockSpec(near.shape, lambda i, at_ref: (0, 0, 0))
    gate = pl.BlockSpec((None, wide, fine), lambda i, at_ref: (at_ref[i], 0, 0))
    down = pl.BlockSpec((None, fine, wide), lambda i, at_ref: (at_ref[i], 0, 0))
    return pl.pallas_call(
        place_kernel,
        cost_estimate=pl.CostEstimate(flops=4 * MICRO, bytes_accessed=0, transcendentals=0),
        grid_spec=pltpu.PrefetchScalarGridSpec(
            num_scalar_prefetch=1,
            grid=(2,),
            in_specs=[source, source] + [pl.BlockSpec(memory_space=pl.ANY)] * len(held),
            out_specs=[gate, gate, down],
        ),
        out_shape=[jax.ShapeDtypeStruct((experts, wide, fine), F32)] * 2
        + [jax.ShapeDtypeStruct((experts, fine, wide), F32)],
        input_output_aliases={3 + i: i for i in range(len(held))},
        compiler_params=pltpu.CompilerParams(vmem_limit_bytes=32 << 20),
    )(at, near, far, *held)


def share_kernel(over_tp, x_ref, out_ref, slots, ss, sr):
    c, t = lax.axis_index("ctx"), lax.axis_index("tp")
    n, tp = lax.axis_size("ctx"), lax.axis_size("tp")
    me = c * tp + t
    everyone = [(far_c, far_t) for far_c in range(n) for far_t in range(tp)]
    signal_all(
        [({"ctx": far_c, "tp": far_t}, (c != far_c) | (t != far_t)) for far_c, far_t in everyone]
    )

    def copy(far_c, far_t):
        return pltpu.make_async_remote_copy(
            src_ref=x_ref,
            dst_ref=slots.at[me],
            send_sem=ss.at[far_c * tp + far_t],
            recv_sem=sr.at[me],
            device_id={"ctx": far_c, "tp": far_t},
            device_id_type=MESH,
        )

    for far_c, far_t in everyone:

        @pl.when((c != far_c) | (t != far_t))
        def _():
            copy(far_c, far_t).start()

    slots[me] = x_ref[...]
    for at in range(n * tp):

        @pl.when(me != at)
        def _():
            pltpu.make_async_remote_copy(
                src_ref=slots.at[at],
                dst_ref=slots.at[at],
                send_sem=ss.at[at],
                recv_sem=sr.at[at],
                device_id={"tp": lax.rem(t + 1, tp)},
                device_id_type=MESH,
            ).wait_recv()

    sums = [sum(slots[far_c * tp + far_t] for far_c in range(n)) for far_t in range(tp)]
    if over_tp:
        out_ref[...] = sum(sums)
    else:
        for far_t in range(tp):
            out_ref[far_t] = sums[far_t]
    for far_c, far_t in everyone:

        @pl.when((c != far_c) | (t != far_t))
        def _():
            copy(far_c, far_t).wait_send()


def share(v, over_tp, ident):
    n, tp = lax.axis_size("ctx"), lax.axis_size("tp")
    dma = pltpu.SemaphoreType.DMA
    near = pl.BlockSpec(memory_space=pltpu.VMEM)
    return pl.pallas_call(
        functools.partial(share_kernel, over_tp),
        cost_estimate=pl.CostEstimate(flops=8 * MICRO, bytes_accessed=0, transcendentals=0),
        out_shape=jax.ShapeDtypeStruct(v.shape if over_tp else (tp,) + v.shape, v.dtype),
        in_specs=[near],
        out_specs=near,
        scratch_shapes=[pltpu.VMEM((n * tp,) + v.shape, v.dtype)] + [dma((n * tp,))] * 2,
        compiler_params=pltpu.CompilerParams(
            collective_id=ident, has_side_effects=True, vmem_limit_bytes=32 << 20
        ),
    )(v)


def body(
    tokens,
    cotangent,
    lengths,
    routes,
    attn_gain,
    w_query,
    w_key,
    w_value,
    q_gain,
    k_gain,
    w_out,
    mlp_gain,
    w_router,
    w_gate,
    w_up,
    w_down,
):
    dp_at, ctx_at, tp_at = (lax.axis_index(a) for a in ("dp", "ctx", "tp"))
    dp_count, ctx_count, tp_count = (lax.axis_size(a) for a in ("dp", "ctx", "tp"))
    rows, width = tokens.shape
    wide = w_query.shape[0]
    local = w_query.shape[1]
    heads = local // HEAD
    experts = w_router.shape[1]
    mine = experts // ctx_count
    part = width // tp_count
    column_at = lax.rem(tp_at, 2) * 2 + tp_at // 2

    def fetch(v):
        others = [
            lax.ppermute(v, "dp", [((i + s) % dp_count, i) for i in range(dp_count)])
            for s in range(1, dp_count)
        ]
        return [v] + others

    def hand_over(blocks):
        total = blocks[0].astype(F32)
        for s in range(1, dp_count):
            pairs = [(i, (i + s) % dp_count) for i in range(dp_count)]
            total = total + lax.ppermute(blocks[s].astype(BF16), "dp", pairs).astype(F32)
        return total

    def swap(blocks):
        return [
            lax.ppermute(blocks[s], "dp", [(i, (i + s) % dp_count) for i in range(dp_count)])
            for s in range(1, dp_count)
        ]

    def add(blocks, arrived):
        return sum(v.astype(F32) for v in [blocks[0]] + arrived).astype(BF16)

    def columns(v):
        return lax.dynamic_slice_in_dim(v, column_at * part, part, v.ndim - 1)

    def block(v, s):
        return v[:, s * wide : (s + 1) * wide]

    def own_experts(w):
        return lax.dynamic_slice_in_dim(w, ctx_at * mine, mine, 0)

    small = jnp.concatenate(
        [attn_gain[None], q_gain[None], k_gain[None], mlp_gain[None], w_router.T], axis=0
    )
    small = jnp.concatenate(fetch(small), axis=1)
    gains = small[:4].astype(F32)
    router_w = small[4:]
    gain_one, gain_two = gains[0], columns(gains[3])

    def heads_gain(v):
        back = jnp.roll(v, dp_at * wide)
        return lax.dynamic_slice_in_dim(back, tp_at * local, local)

    gain_q, gain_k = heads_gain(gains[1]), heads_gain(gains[2])
    own_cols = local // ctx_count
    head_at = tp_at * local + ctx_at * own_cols

    def own_heads(w):
        return lax.dynamic_slice_in_dim(w, ctx_at * own_cols, own_cols, 1)

    def natural(v):
        return jnp.roll(v, dp_at * wide, axis=-1)

    gain_q, gain_k = lax.dynamic_slice_in_dim(natural(gains[1:3]), head_at, own_cols, 1)
    heads_w = jnp.concatenate([own_heads(w) for w in (w_query, w_key, w_value)], axis=1)
    weights = (w_gate, w_up, w_down)
    beside_at = jnp.bitwise_xor(ctx_at, 2)

    def experts_of(w, plane):
        return lax.dynamic_slice_in_dim(w, plane * mine, mine, 0)


    own_slices = [experts_of(w, ctx_at) for w in weights]
    tokens = jnp.roll(tokens, -dp_at * wide, axis=1)

    inputs = tokens.astype(F32)
    scale_one = lax.rsqrt(jnp.mean(inputs * inputs, axis=1, keepdims=True) + EPS)
    hidden_one = columns((inputs * scale_one * gain_one).astype(BF16))
    hidden_one, own_slices = lax.optimization_barrier((hidden_one, own_slices))
    hidden_one, *got = spread(
        hidden_one, 1, [("w", heads_w), ("w", w_out), ("w", own_slices[0])]
    )

    def listed(w, received):
        return [w] + [received[s] for s in range(dp_count - 1)]

    heads_w, out_w = listed(heads_w, got[0]), listed(w_out, got[1])
    own_w = [listed(own_slices[0], got[2]), fetch(own_slices[1]), None]
    if wide % part == 0:

        def upstream_columns(at):
            return lax.dynamic_slice_in_dim(
                cotangent, lax.rem(at * part + dp_at * wide, width), part, 1
            )

    else:
        turned_cotangent = jnp.roll(cotangent, -dp_at * wide, axis=1)

        def upstream_columns(at):
            return lax.dynamic_slice_in_dim(turned_cotangent, at * part, part, 1)

    chosen = jnp.any(
        routes[:, :, None] == jnp.arange(experts, dtype=jnp.int32)[None, None, :], axis=1
    )
    upstream_all = jnp.concatenate([upstream_columns(tp_at), chosen.astype(BF16).T])
    upstream_all = lax.all_gather(upstream_all, "ctx", axis=0, tiled=False)
    chosen_all = upstream_all[:, rows:].transpose(0, 2, 1).reshape(-1, experts).astype(F32)
    hidden_one, upstream_all = lax.optimization_barrier((hidden_one, upstream_all))
    upstream_all = lax.all_gather(upstream_all[:, :rows].reshape(-1, part), "tp", axis=1, tiled=True)
    raw = sum(dot(block(hidden_one, s), w) for s, w in enumerate(heads_w))
    q_raw, k_raw = raw[:, :own_cols], raw[:, own_cols : 2 * own_cols]
    values = raw[:, 2 * own_cols :].astype(BF16)
    pack = raw.shape[0]
    squares = share(
        jnp.stack([jnp.sum(q_raw * q_raw, axis=1), jnp.sum(k_raw * k_raw, axis=1)]), True, 5
    )
    q_scale, k_scale = lax.rsqrt(squares / width + EPS)[:, :, None]
    q_hat, k_hat = q_raw * q_scale, k_raw * k_scale
    cosine, sine = rotation(lengths[0], 0, pack)
    mine_heads = own_cols // HEAD

    def turn(v, sine):
        return rotate(v.reshape(pack, mine_heads, HEAD), cosine, sine)

    def by_head(v):
        return v.astype(BF16).reshape(pack, mine_heads, HEAD).transpose(1, 0, 2)

    q_all, k_all = by_head(turn(q_hat * gain_q, sine)), by_head(turn(k_hat * gain_k, sine))
    v_all = by_head(values)
    attended_all, log = attend(lengths, q_all, k_all, v_all)
    attended = to_rows((attended_all,))[0].reshape(rows, local)
    branch = jnp.concatenate([dot(attended, w).astype(BF16) for w in out_w], axis=1)
    branch, own_w[1] = lax.optimization_barrier((branch, own_w[1]))
    branch = collect(branch, 1, 2)
    inputs_c = columns(inputs)
    mixed = inputs_c + branch
    square = lax.psum(jnp.sum(mixed * mixed, axis=1), "tp")
    scale_two = lax.rsqrt(square / width + EPS)[:, None]
    normed_two = mixed * scale_two
    hidden_mine = (normed_two * gain_two).astype(BF16)
    hidden_two, got = spread(hidden_mine, 3, [("w", own_slices[2])])
    own_w[2] = listed(own_slices[2], got)
    hidden_two, late = lax.optimization_barrier((hidden_two, weights))
    far_slices = [experts_of(w, beside_at) for w in late]
    far_slices = [jnp.concatenate(far_slices[:2]), far_slices[2]]

    tie = lax.optimization_barrier
    grads, sums, there = {}, {}, {}

    def run(e):
        far = e >= mine
        w = far_w if far else own_w
        number = e % mine
        out = expert(
            number, hidden_two, upstream_all, chosen_all, router_w, w, far, not far, [], 20 + e
        )
        grads[e] = [out[-2], out[-1]]
        return list(out[:-2])

    def start_x(e):
        grads[e][1] = swap([None] + [grads[e][1][s] for s in range(dp_count - 1)])

    def end_x(e, after):
        grads[e][1], after = tie((grads[e][1], after))
        sums[e] = add([grads[e][0]], grads[e][1])
        return after

    def start_z(e):
        there[e] = lax.ppermute(sums[e], "ctx", [(i, i ^ 1) for i in range(ctx_count)])

    def end_z(e, after):
        there[e], after = tie((there[e], after))
        return after

    parts = []
    for e in range(mine):
        parts.append(run(e))
        if e > 0:
            hidden_two = end_x(e - 1, (hidden_two, grads[e][1]))[0]
            if e == 1:
                hidden_two, far_slices = tie((hidden_two, far_slices))
            start_z(e - 1)
        if e > 2:
            hidden_two = end_z(e - 3, hidden_two)
        start_x(e)
    mixture = mixture_parts([p[0] for p in parts], own_w[2], tp_count)
    mixture, hidden_two = tie((mixture, hidden_two))
    mixture = lax.psum_scatter(mixture, "tp", scatter_dimension=0, tiled=False)
    dots = jnp.concatenate([p[3] for p in parts], axis=1).T
    dots, hidden_two = tie((dots, hidden_two))
    far_both = fetch(far_slices[0])
    expert_in, dots = returns(
        [[p[1] for p in parts], [p[2] for p in parts]],
        own_w[:2],
        dots,
        False,
        4,
    )
    far_both, expert_in, late_down = tie((far_both, expert_in, far_slices[1]))
    far_down = fetch(late_down)
    for e in range(1, mine - 1):
        expert_in = end_z(e, expert_in)
    expert_in, mixture = tie((expert_in, mixture))
    mixture = lax.psum_scatter(mixture, "ctx", scatter_dimension=0, tiled=True)

    dots = dots.reshape(experts, rows).T
    hidden_rows = lax.dynamic_slice_in_dim(hidden_two, ctx_at * rows, rows, 0)
    route_mine = jax.nn.softmax(dot_t(hidden_rows, router_w), axis=1)
    d_logits = (
        route_mine * (dots - jnp.sum(route_mine * dots, axis=1, keepdims=True))
    ).astype(BF16)
    router_grad = t_dot(d_logits, hidden_mine)
    d_hidden_two = expert_in + dot(d_logits, columns(router_w))
    gain_two_grad = jnp.sum(d_hidden_two * normed_two, axis=0)
    pull_two = d_hidden_two * gain_two
    mean_two = lax.psum(jnp.sum(pull_two * mixed, axis=1), "tp")[:, None] / width
    mean_two = end_x(mine - 1, mean_two)
    sums[mine - 1], mean_two = tie((sums[mine - 1], mean_two))
    start_z(mine - 1)
    d_mixed = (
        upstream_columns(column_at).astype(F32) + scale_two * pull_two - mixed * scale_two**3 * mean_two
    )

    d_branch = join(d_mixed.astype(BF16), 7)
    d_branch = end_z(mine - 1, d_branch)
    hidden_two, d_branch, far_down, mixture = tie((hidden_two, d_branch, far_down, mixture))
    output = lax.all_gather(mixed + mixture.astype(F32), "tp", axis=0, tiled=False)
    far_w = [far_both, far_both, far_down]
    d_attended = sum(dot_t(block(d_branch, s), w) for s, w in enumerate(out_w)).astype(BF16)
    out_grad = swap([t_dot(block(d_branch, s), attended).astype(BF16) for s in range(dp_count)])
    out_mine = t_dot(block(d_branch, 0), attended)
    d_all = to_heads((d_attended,), heads)[0]
    run(mine)
    start_x(mine)
    d_all, grads[mine][0], out_grad, output = tie((d_all, grads[mine][0], out_grad, output))
    out_grad = add([out_mine], out_grad)
    out_grad = lax.psum_scatter(out_grad, "ctx", scatter_dimension=0, tiled=True)
    dq_all, dk_all, dv_all = attend_back(lengths, q_all, k_all, v_all, d_all, log)
    def by_token(v):
        return v.transpose(1, 0, 2).reshape(pack, own_cols)

    d_q_normed = turn(by_token(dq_all), -sine).reshape(pack, own_cols)
    d_k_normed = turn(by_token(dk_all), -sine).reshape(pack, own_cols)
    q_pull, k_pull = d_q_normed * gain_q, d_k_normed * gain_k
    totals = share(
        jnp.stack([jnp.sum(q_pull * q_raw, axis=1), jnp.sum(k_pull * k_raw, axis=1)]), True, 6
    )
    q_mean, k_mean = totals[:, :, None] / width
    d_q_raw = (q_scale * q_pull - q_raw * q_scale**3 * q_mean).astype(BF16)
    d_k_raw = (k_scale * k_pull - k_raw * k_scale**3 * k_mean).astype(BF16)
    d_raw = jnp.concatenate([d_q_raw, d_k_raw, by_token(dv_all)], axis=1)
    heads_mine = t_dot(block(hidden_one, 0), d_raw)
    heads_grads = [t_dot(block(hidden_one, s), d_raw).astype(BF16) for s in range(dp_count)]
    heads_mine, heads_grads, d_raw, hidden_two, out_grad = tie(
        (heads_mine, heads_grads, d_raw, hidden_two, out_grad)
    )
    out_grad = lax.all_gather(out_grad, "ctx", axis=0, tiled=True)
    held = []

    def put(e):
        nonlocal held
        plane = ctx_at if e < mine else beside_at
        at = plane * mine + e % mine
        other = jnp.bitwise_xor(plane, 1) * mine + e % mine
        held = place_grads(
            jnp.stack([at, other]).astype(jnp.int32), sums[e], there[e], experts, held
        )

    for e in range(mine + 1, 2 * mine):
        run(e)
        if e > mine + 1:
            for i in range(2 * (e - mine - 2), 2 * (e - mine - 1)):
                there[i], grads[e] = tie((there[i], grads[e]))
                put(i)
        step = (hidden_two, d_raw, grads[e], held)
        if e > mine + 1:
            step = end_z(e - 2, step)
        step = end_x(e - 1, step)
        if e == mine + 1:
            out_grad, step = tie((out_grad, step))
        sums[e - 1], step = tie((sums[e - 1], step))
        hidden_two, d_raw, grads[e], held = step
        start_z(e - 1)
        if e < 2 * mine - 1:
            start_x(e)
    heads_grads, grads[2 * mine - 1] = tie((heads_grads, grads[2 * mine - 1]))
    start_x(2 * mine - 1)
    heads_grads = swap(heads_grads)
    (d_hidden,) = returns(
        [[d_raw]],
        [[w[None] for w in heads_w]],
        None,
        False,
        8,
    )
    d_hidden = end_z(2 * mine - 2, end_x(2 * mine - 1, d_hidden))
    heads_grads, out_grad, d_hidden = tie((heads_grads, out_grad, d_hidden))
    gain_one_grad = jnp.sum(d_hidden * inputs_c * scale_one, axis=0)
    heads_gains = lax.dynamic_update_slice_in_dim(
        jnp.zeros((2, local), F32),
        jnp.stack([jnp.sum(d_q_normed * q_hat, axis=0), jnp.sum(d_k_normed * k_hat, axis=0)]),
        ctx_at * own_cols,
        1,
    )
    small_grads = jnp.concatenate(
        [gain_one_grad[None], gain_two_grad[None], router_grad, heads_gains]
    )
    small_shape, across = small_grads.shape, 3 * own_cols
    small_count = small_grads.size
    small_rows = -(-small_count // (16 * across)) * 16
    small_grads = jnp.pad(
        small_grads.astype(BF16).reshape(-1), (0, small_rows * across - small_count)
    )
    heads_grads = add([heads_mine], heads_grads)
    heads_grads = jnp.concatenate([heads_grads, small_grads.reshape(small_rows, across)])
    heads_grads = lax.all_gather(heads_grads, "ctx", axis=0, tiled=False)
    start_z(2 * mine - 1)
    small_grads = heads_grads[:, wide:].astype(F32).sum(axis=0).reshape(-1)[:small_count]
    small_grads = lax.all_gather(small_grads.reshape(small_shape), "tp", axis=0, tiled=False)
    pull_one = d_hidden * columns(gain_one)
    mean_one = lax.psum(jnp.sum(pull_one * inputs_c, axis=1), "tp")[:, None] / width
    d_inputs = d_mixed + scale_one * pull_one - inputs_c * scale_one**3 * mean_one

    def whole(every):
        every = [every[(p % 2) * 2 + p // 2] for p in range(tp_count)]
        return natural(jnp.concatenate(every, axis=1))

    output = whole(output)
    d_inputs = join(d_inputs.astype(BF16), 10)
    d_inputs = natural(d_inputs).astype(F32)
    turned = [small_grads[(p % 2) * 2 + p // 2, : 2 + experts] for p in range(tp_count)]
    heads_gains = small_grads[:, 2 + experts : 4 + experts].transpose(1, 0, 2).reshape(2, width)
    small_grads = jnp.concatenate([natural(jnp.concatenate(turned, axis=1)), heads_gains])
    small_grads = hand_over(
        [small_grads if s == 0 else small_grads for s in range(dp_count)]
    )
    small_grads = lax.dynamic_slice_in_dim(small_grads, dp_at * wide, wide, 1)

    def heads_grad(i):
        v = heads_grads[:, :wide, i * own_cols : (i + 1) * own_cols].astype(F32)
        return v.transpose(1, 0, 2).reshape(wide, local)

    for e in range(mine, 2 * mine - 1):
        there[e], d_hidden = tie((there[e], d_hidden))
    for e in range(mine, 2 * mine):
        put(e)
    return (
        output,
        d_inputs,
        small_grads[0],
        heads_grad(0),
        heads_grad(1),
        heads_grad(2),
        small_grads[2 + experts],
        small_grads[3 + experts],
        out_grad.astype(F32).T,
        small_grads[1],
        small_grads[2 : 2 + experts].T,
        held[0],
        held[1],
        held[2],
    )


def solution(mesh):
    in_specs = (
        P(("dp", "ctx"), None),
        P(("dp", "ctx"), None),
        P("dp", None),
        P(("dp", "ctx"), None),
        P("dp"),
        P("dp", "tp"),
        P("dp", "tp"),
        P("dp", "tp"),
        P("dp"),
        P("dp"),
        P("tp", "dp"),
        P("dp"),
        P("dp", None),
        P(None, "dp", "tp"),
        P(None, "dp", "tp"),
        P(None, "tp", "dp"),
    )
    out_specs = (
        P(("dp", "ctx"), None),
        P(("dp", "ctx"), None),
        P("dp"),
        P("dp", "tp"),
        P("dp", "tp"),
        P("dp", "tp"),
        P("dp"),
        P("dp"),
        P("tp", "dp"),
        P("dp"),
        P("dp", None),
        P(None, "dp", "tp"),
        P(None, "dp", "tp"),
        P(None, "tp", "dp"),
    )
    return jax.shard_map(body, mesh=mesh, in_specs=in_specs, out_specs=out_specs, check_vma=False)
```
